256 devices in a mesh: lat: 32 (over x, z_lo, y), lon: 8 (over z_hi, core).
Axes of the slice: x: 4, y: 4, z: 8 (z_hi: 4, z_lo: 2; z = z_hi * 2 + z_lo), core: 2. Of those that a mesh axis runs over, the one named last changes fastest.
Arguments:
- grid_in: bfloat16 [128, 1440, 256], P('lat', 'lon'), may hold values from -6 to 6
- grid_cotangent: bfloat16 [128, 1440, 256], P('lat', 'lon'), may hold values from -6 to 6
- support_filter: float32 [128, 5, 1440], P('lat'), may hold values from -2.5 to 2.5
- band_half: int32 [128], P('lat'), may hold values from 1 to 2, as said below
- w_mix: bfloat16 [256, 256], replicated, may hold values from -0.375 to 0.375
- norm_gain: float32 [256], replicated, may hold values from 0.5 to 1.5
- w_up: bfloat16 [256, 1024], replicated, may hold values from -0.375 to 0.375
- w_down: bfloat16 [1024, 256], replicated, may hold values from -0.1875 to 0.1875
Outputs:
- grid_out: bfloat16 [128, 1440, 256], P('lat', 'lon')
- grid_grad: bfloat16 [128, 1440, 256], P('lat', 'lon')
- mix_grad: float32 [256, 256], replicated
- gain_grad: float32 [256], replicated
- up_grad: float32 [256, 1024], replicated
- down_grad: float32 [1024, 256], replicated
The draws below stay inside these ranges and needn't reach their ends.
Inputs may be any that keep to these rules, and one draw needn't show every extreme that they name: `band_half`: cycles within 4 of either pole have the full support 2.
All inputs are finite; a program needn't handle non-finite values.
Results may differ from the reference program's by a relative error of at most 0.023.
Values may be sent and summed in bfloat16 or wider, within the bound.
A program may use at most 64 MiB of HBM per device.

```python
import jax
import jax.numpy as jnp
from jax import lax

CHANNELS = 256
HIDDEN_SIZE = 1024
REACH = 2
NLAT = 128
NLON = 1440


def draw_band_half(key, part):
    key = jax.random.fold_in(key, 7)
    base_half = jax.random.randint(key, (NLAT,), 1, REACH + 1)
    cycle_ids = jnp.arange(NLAT)
    near_pole = jnp.minimum(cycle_ids, NLAT - 1 - cycle_ids) < 2 * REACH
    return jnp.where(near_pole, REACH, base_half).astype(jnp.int32)


def block_scale(stream_key, shape, split, least, high):
    loudness, own = 1.0, jax.random.fold_in(stream_key, 6)
    for position, shards_of in split:
        draws = jnp.exp(jax.random.uniform(jax.random.fold_in(own, position), (shards_of,), jnp.float32, least / len(split), high / len(split)))
        loudness = loudness * jnp.repeat(draws, shape[position] // shards_of).reshape([-1 if axis == position else 1 for axis in range(len(shape))])
    return loudness


def normal_values(stream_key, shape, scale, reach, pieces=(), kind=jnp.bfloat16):
    gain = block_scale(stream_key, shape, pieces, -0.22, 0.18) if pieces else 1.0
    drawn = jax.random.normal(stream_key, shape, jnp.float32) * scale * gain
    return jnp.minimum(jnp.maximum(drawn, -reach), reach).astype(kind)


def setup_inputs(seed: int = 0) -> dict:
    arg_keys = jax.random.split(jax.random.key(seed), 9)
    grid_in = normal_values(arg_keys[0], (NLAT, NLON, CHANNELS), 1.0, 6.0, ((0, 32), (1, 8)))
    grid_cotangent = normal_values(arg_keys[1], (NLAT, NLON, CHANNELS), 1.0, 6.0, ((0, 32), (1, 8)))
    support_filter = normal_values(arg_keys[2], (NLAT, 2 * REACH + 1, NLON), 0.4, 2.5, ((0, 32),), jnp.float32)
    band_half = draw_band_half(jax.random.fold_in(arg_keys[8], 71), 0)
    w_mix = normal_values(arg_keys[4], (CHANNELS, CHANNELS), CHANNELS ** -0.5, 0.375)
    norm_gain = jnp.clip(1.0 + 0.1 * jax.random.normal(arg_keys[5], (CHANNELS,), jnp.float32), 0.5, 1.5)
    w_up = normal_values(arg_keys[6], (CHANNELS, HIDDEN_SIZE), CHANNELS ** -0.5, 0.375)
    w_down = normal_values(arg_keys[7], (HIDDEN_SIZE, CHANNELS), HIDDEN_SIZE ** -0.5, 0.1875)
    return {"grid_in": grid_in, "grid_cotangent": grid_cotangent, "support_filter": support_filter, "band_half": band_half, "w_mix": w_mix, "norm_gain": norm_gain, "w_up": w_up, "w_down": w_down}


SQRT_TWO_PI = 0.7978845608028654
CUBIC = 0.044715

def gelu_tanh(values):
    tanh_arg = SQRT_TWO_PI * (values + CUBIC * values * values * values)
    return 0.5 * values * (1.0 + jnp.tanh(tanh_arg))

def gelu_slope(values):
    tanh_arg = SQRT_TWO_PI * (values + CUBIC * values * values * values)
    tangent = jnp.tanh(tanh_arg)
    return 0.5 * (1.0 + tangent) + 0.5 * values * (1.0 - tangent * tangent) * SQRT_TWO_PI * (1.0 + 3.0 * CUBIC * values * values)

def inner_rows(left_side, right_side):
    return lax.dot_general(left_side, right_side, (((0,), (0,)), ((), ())), preferred_element_type=jnp.float32)

def times_transpose(left_side, right_side):
    return lax.dot_general(left_side, right_side, (((1,), (1,)), ((), ())), preferred_element_type=jnp.float32)

def fourier_values(positions, mode_ids, length):
    half_len = length // 2
    frequency = jnp.where(mode_ids < half_len, mode_ids, mode_ids - half_len)
    phase_int = positions[:, None] * frequency[None, :] % length
    angle_rad = phase_int.astype(jnp.float32) * (2.0 * 3.141592653589793 / length)
    return jnp.where((mode_ids < half_len)[None, :], jnp.cos(angle_rad), jnp.sin(angle_rad))

def forward_table(positions, mode_ids, length):
    return fourier_values(positions, mode_ids, length).astype(jnp.bfloat16)

def inverse_table(mode_ids, positions, length):
    fourier = fourier_values(positions, mode_ids, length)
    weight = jnp.where(mode_ids == 0, 1.0, 2.0) / length
    return (jnp.transpose(fourier) * weight[:, None]).astype(jnp.bfloat16)

def masked_filter(support_filter, band_half):
    reach_rows = (support_filter.shape[1] - 1) // 2
    tap_offsets = jnp.arange(support_filter.shape[1], dtype=jnp.int32) - reach_rows
    inside = jnp.abs(tap_offsets)[None, :] <= band_half[:, None]
    return jnp.where(inside[:, :, None], support_filter, 0.0)

def band_forward(padded, filtered):
    lat_rows = filtered.shape[0]
    running = jnp.zeros((padded.shape[0], lat_rows, padded.shape[2]), jnp.float32)
    for tap_index in range(filtered.shape[1]):
        coeffs = jnp.transpose(filtered[:, tap_index, :])
        running = running + coeffs[:, :, None] * padded[:, tap_index:tap_index + lat_rows].astype(jnp.float32)
    return running.astype(jnp.bfloat16)

def band_adjoint(grad_padded, filter_padded, lat_rows):
    tap_count = filter_padded.shape[1]
    reach_rows = (tap_count - 1) // 2
    running = jnp.zeros((grad_padded.shape[0], lat_rows, grad_padded.shape[2]), jnp.float32)
    for tap_index in range(tap_count):
        begin_at = 2 * reach_rows - tap_index
        coeffs = jnp.transpose(filter_padded[begin_at:begin_at + lat_rows, tap_index, :])
        running = running + coeffs[:, :, None] * grad_padded[:, begin_at:begin_at + lat_rows].astype(jnp.float32)
    return running.astype(jnp.bfloat16)

def tail_pass(flat_in, flat_conv, cotangent, w_mix, norm_gain, w_up, w_down):
    mixed = jnp.dot(flat_conv, w_mix, preferred_element_type=jnp.float32)
    stream = (flat_in.astype(jnp.float32) + mixed).astype(jnp.bfloat16)
    stream_f = stream.astype(jnp.float32)
    inverse = lax.rsqrt(lax.optimization_barrier(jnp.mean(stream_f * stream_f, axis=-1, keepdims=True)) + 1e-06)
    normed = stream_f * inverse
    scaled = (normed * norm_gain).astype(jnp.bfloat16)
    before = jnp.dot(scaled, w_up, preferred_element_type=jnp.float32)
    hidden = gelu_tanh(before).astype(jnp.bfloat16)
    result = (stream_f + jnp.dot(hidden, w_down, preferred_element_type=jnp.float32)).astype(jnp.bfloat16)
    d_hidden = times_transpose(cotangent, w_down)
    down_term = inner_rows(hidden, cotangent)
    d_before = (d_hidden * gelu_slope(before)).astype(jnp.bfloat16)
    up_term = inner_rows(scaled, d_before)
    d_scaled = times_transpose(d_before, w_up)
    gain_term = lax.optimization_barrier(jnp.sum(d_scaled * normed, axis=0))
    gained = d_scaled * norm_gain
    d_stream = cotangent.astype(jnp.float32) + inverse * (gained - normed * lax.optimization_barrier(jnp.mean(gained * normed, axis=-1, keepdims=True)))
    d_stream16 = d_stream.astype(jnp.bfloat16)
    mix_term = inner_rows(flat_conv, d_stream16)
    d_conv = times_transpose(d_stream16, w_mix).astype(jnp.bfloat16)
    return (result, d_stream, d_conv, (mix_term, gain_term, up_term, down_term))

def reference(grid_in, grid_cotangent, support_filter, band_half, w_mix, norm_gain, w_up, w_down):
    lat_count, lon_count, channel_count = grid_in.shape
    hidden_count = w_up.shape[1]
    reach_rows = (support_filter.shape[1] - 1) // 2
    filtered = masked_filter(support_filter, band_half)
    positions = jnp.arange(lon_count, dtype=jnp.int32)
    forward = forward_table(positions, positions, lon_count).astype(jnp.float32)
    inverse = inverse_table(positions, positions, lon_count).astype(jnp.float32)
    spectra = jnp.einsum('jlc,lk->kjc', grid_in.astype(jnp.float32), forward).astype(jnp.bfloat16)
    padded = jnp.pad(spectra, ((0, 0), (reach_rows, reach_rows), (0, 0)))
    banded = band_forward(padded, filtered)
    conv_grid = jnp.einsum('kic,kl->ilc', banded.astype(jnp.float32), inverse).astype(jnp.bfloat16)

    def one_row(carried, row_items):
        row_in, row_conv, row_cot = row_items
        result, d_stream, d_conv, grad_terms = tail_pass(row_in, row_conv, row_cot, w_mix, norm_gain, w_up, w_down)
        carried = tuple((first_sum + second_sum for first_sum, second_sum in zip(carried, grad_terms)))
        return (carried, (result, d_stream, d_conv))
    initial = (jnp.zeros((channel_count, channel_count), jnp.float32), jnp.zeros((channel_count,), jnp.float32), jnp.zeros((channel_count, hidden_count), jnp.float32), jnp.zeros((hidden_count, channel_count), jnp.float32))
    summed, (grid_out, d_stream, d_conv) = lax.scan(one_row, initial, (grid_in, conv_grid, grid_cotangent))
    d_banded = jnp.einsum('ilc,kl->kic', d_conv.astype(jnp.float32), inverse).astype(jnp.bfloat16)
    grad_padded = jnp.pad(d_banded, ((0, 0), (reach_rows, reach_rows), (0, 0)))
    filter_padded = jnp.pad(filtered, ((reach_rows, reach_rows), (0, 0), (0, 0)))
    d_spectra = band_adjoint(grad_padded, filter_padded, lat_count)
    back_grid = jnp.einsum('kjc,lk->jlc', d_spectra.astype(jnp.float32), forward)
    grid_grad = (d_stream + back_grid).astype(jnp.bfloat16)
    norm_scale = float(lat_count * lon_count) ** (-0.5)
    return (grid_out, grid_grad, summed[0] * norm_scale, summed[1] * norm_scale, summed[2] * norm_scale, summed[3] * norm_scale)
```

```python
import jax
import jax.numpy as jnp
import ml_dtypes
import numpy as np
from jax import lax
from jax.experimental import pallas as pl
from jax.experimental.pallas import tpu as pltpu
from jax.sharding import PartitionSpec as P

SQRT_TWO_PI = 0.7978845608028654
CUBIC = 0.044715
MESH = pl.DeviceIdType.MESH
BF16 = jnp.bfloat16
F32 = jnp.float32

LAT = 32
LON = 8
PAIRS = LON // 2
ROWS = 4
COLS = 180
BLK = 192
NLON = LON * COLS
MODES = LON * BLK
CH = 256
HID = 1024
TAPS = 5
FLAT = ROWS * BLK


def fourier_tables():
    modes = np.arange(NLON)
    freq = np.where(modes < NLON // 2, modes, modes - NLON // 2)
    phase = (freq[:, None] * modes[None, :]) % NLON
    angle = phase * (2.0 * np.pi / NLON)
    values = np.where((modes < NLON // 2)[:, None], np.cos(angle), np.sin(angle))
    table = np.zeros((MODES, LON, BLK), np.float32)
    table[:NLON, :, :COLS] = values.reshape(NLON, LON, COLS)
    table = table.reshape(MODES, MODES).astype(ml_dtypes.bfloat16)
    return table, np.ascontiguousarray(table.T)


def expansion():
    fwd = np.zeros((32, TAPS, ROWS, 32), np.float32)
    bwd = np.zeros((64, TAPS, ROWS, 32), np.float32)
    for w in range(TAPS):
        for i in range(ROWS):
            fwd[8 * i + w, w, i] = 1.0
            bwd[8 * (i + w) + 4 - w, w, i] = 1.0
    fwd = fwd.reshape(32, TAPS * 128)
    bwd = bwd.reshape(64, TAPS * 128)
    return fwd.astype(ml_dtypes.bfloat16), bwd.astype(ml_dtypes.bfloat16)


def dot(a, b):
    return jnp.dot(a, b, preferred_element_type=F32)


def dot_rows(a, b):
    return lax.dot_general(a, b, (((0,), (0,)), ((), ())), preferred_element_type=F32)


def dot_transpose(a, b):
    return lax.dot_general(a, b, (((1,), (1,)), ((), ())), preferred_element_type=F32)


def lanes_of(shape):
    return lax.broadcasted_iota(jnp.int32, shape, 1)


def turn_groups(parts):
    lane = lanes_of(parts[0].shape)
    low = lane < 64
    a, b, c, d = parts
    a, c = jnp.where(low, a, pltpu.roll(c, 64, 1)), jnp.where(low, pltpu.roll(a, 64, 1), c)
    b, d = jnp.where(low, b, pltpu.roll(d, 64, 1)), jnp.where(low, pltpu.roll(b, 64, 1), d)
    even = (lane % 64) < 32
    a, b = jnp.where(even, a, pltpu.roll(b, 32, 1)), jnp.where(even, pltpu.roll(a, 96, 1), b)
    c, d = jnp.where(even, c, pltpu.roll(d, 32, 1)), jnp.where(even, pltpu.roll(c, 96, 1), d)
    return a, b, c, d


def kernel(
    gin, cot, filt, band, wmix, gain, wup, wdown, efwd, ebwd, fwd_hbm, inv_hbm,
    out, grad, mix_o, gain_o, up_o, down_o,
    fwd, inv, gpad, cpad, send, recv, hsend, hrecv, halo, fstage, fown, fhalo, coef, dcoef,
    spec, banded, conv, field, stream, scaled, before, dhid, hidden, dbef, dstream, dstream16,
    tsem, ssem, rsem, hssem, hrsem, fssem, frsem,
):
    lat = lax.axis_index("lat")
    me = lax.axis_index("lon")
    pair = me // 2
    after = lax.rem(lat + 1, LAT)
    ahead = lax.rem(lat + LAT - 1, LAT)

    get_fwd = pltpu.make_async_copy(fwd_hbm, fwd, tsem.at[0])
    get_inv = pltpu.make_async_copy(inv_hbm, inv, tsem.at[1])
    get_fwd.start()
    get_inv.start()

    barrier = pltpu.get_barrier_semaphore()
    for s in range(1, LON):
        pl.semaphore_signal(barrier, inc=1, device_id={"lon": lax.rem(me + s, LON)}, device_id_type=MESH)
    for there in (after, ahead):
        pl.semaphore_signal(barrier, inc=1, device_id={"lat": there}, device_id_type=MESH)

    def exchange(ph, q):
        return pltpu.make_async_remote_copy(
            src_ref=send.at[ph, q], dst_ref=recv.at[ph, me],
            send_sem=ssem.at[ph, q], recv_sem=rsem.at[ph, me],
            device_id={"lon": q}, device_id_type=MESH,
        )

    def arrived(ph, p):
        pltpu.make_async_remote_copy(
            src_ref=send.at[ph, p], dst_ref=recv.at[ph, p],
            send_sem=ssem.at[ph, p], recv_sem=rsem.at[ph, p],
            device_id={"lon": p}, device_id_type=MESH,
        ).wait_recv()

    def halo_copy(ph, side, g):
        return pltpu.make_async_remote_copy(
            src_ref=hsend.at[ph, side, g], dst_ref=hrecv.at[ph, side, g],
            send_sem=hssem.at[ph, side, g], recv_sem=hrsem.at[ph, side, g],
            device_id={"lat": after if side == 0 else ahead}, device_id_type=MESH,
        )

    def filter_copy(side):
        return pltpu.make_async_remote_copy(
            src_ref=fown.at[pl.ds(16 if side == 0 else 0, 16)], dst_ref=fhalo.at[side],
            send_sem=fssem.at[side], recv_sem=frsem.at[side],
            device_id={"lat": after if side == 0 else ahead}, device_id_type=MESH,
        )

    def pack(src, ph):
        @pl.loop(0, BLK // 64)
        def _(step):
            at = step * 64
            for half in range(2):
                parts = [
                    src[pl.ds(i * BLK + at, 64), half * 128 : half * 128 + 128].astype(F32)
                    for i in range(ROWS)
                ]
                for g, block in enumerate(turn_groups(parts)):
                    send[ph, half * 4 + g, pl.ds(at, 64), :] = block.astype(BF16)

    def unpack(ph, put):
        @pl.loop(0, BLK // 64)
        def _(step):
            at = step * 64
            for half in range(2):
                parts = [recv[ph, half * 4 + g, pl.ds(at, 64), :].astype(F32) for g in range(4)]
                for i, block in enumerate(turn_groups(parts)):
                    put(i, at, half, block)

    def start_exchange(ph):
        for s in range(1, LON):
            exchange(ph, lax.rem(me + s, LON)).start()

    def keep_own(ph):
        recv[ph, me] = send[ph, me]

    def gather_with_halo(ph, hp):
        for s in range(PAIRS):
            g = lax.rem(pair + s, PAIRS)
            if s == 0:
                arrived(ph, 2 * pair + 1 - (me - 2 * pair))
            else:
                arrived(ph, 2 * g)
                arrived(ph, 2 * g + 1)

            @pl.loop(0, BLK // 64)
            def _(step):
                at = pl.ds(step * 64, 64)
                one = recv[ph, 2 * g, at, :].astype(F32)
                two = recv[ph, 2 * g + 1, at, :].astype(F32)
                low = lanes_of(one.shape) < 64
                hsend[hp, 0, g, at, :] = jnp.where(low, pltpu.roll(one, 64, 1), two).astype(BF16)
                hsend[hp, 1, g, at, :] = jnp.where(low, one, pltpu.roll(two, 64, 1)).astype(BF16)

            halo_copy(hp, 0, g).start()
            halo_copy(hp, 1, g).start()
        for s in range(PAIRS):
            g = lax.rem(pair + s, PAIRS)
            halo_copy(hp, 0, g).wait_recv()
            halo_copy(hp, 1, g).wait_recv()

            @pl.loop(0, BLK // 64)
            def _(step):
                at = pl.ds(step * 64, 64)
                one = hrecv[hp, 0, g, at, :].astype(F32)
                two = hrecv[hp, 1, g, at, :].astype(F32)
                low = lanes_of(one.shape) < 64
                halo[2 * g, at, :] = jnp.where(low, one, pltpu.roll(two, 64, 1)).astype(BF16)
                halo[2 * g + 1, at, :] = jnp.where(low, pltpu.roll(one, 64, 1), two).astype(BF16)

    def to_modes(ph):
        @pl.loop(0, MODES // 512)
        def _(step):
            at = pl.ds(pl.multiple_of(step * 512, 512), 512)
            both = jnp.concatenate(
                [recv[ph].reshape(MODES, 128), halo[...].reshape(MODES, 128)], axis=1
            )
            spec[at, :] = dot(fwd[at, :], both)

    def band_sum(weights):
        @pl.loop(0, MODES // 64)
        def _(step):
            at = pl.ds(pl.multiple_of(step * 64, 64), 64)
            own = spec[at, 0:128]
            edge = spec[at, 128:256]
            lane = lanes_of(own.shape)
            half = pltpu.roll(own, 64, 1)
            windows = (
                jnp.where(lane < 64, edge, half),
                jnp.where(lane < 32, pltpu.roll(edge, 96, 1), pltpu.roll(own, 32, 1)),
                own,
                jnp.where(lane >= 96, pltpu.roll(edge, 32, 1), pltpu.roll(own, 96, 1)),
                jnp.where(lane >= 64, edge, half),
            )
            total = windows[0] * weights[at, 0:128]
            for w in range(1, TAPS):
                total = total + windows[w] * weights[at, w * 128 : w * 128 + 128]
            banded[at, :] = total.astype(BF16)

    def to_grid_and_send(ph):
        for s in range(PAIRS):
            g = lax.rem(pair + 1 + s, PAIRS)
            rows = pl.ds(pl.multiple_of(g * 2 * BLK, 2 * BLK), 2 * BLK)
            block = dot(inv[rows, :], banded[...]).astype(BF16)
            send[ph, 2 * g] = block[0:BLK]
            send[ph, 2 * g + 1] = block[BLK:]
            if s < PAIRS - 1:
                exchange(ph, 2 * g).start()
                exchange(ph, 2 * g + 1).start()
            else:
                exchange(ph, 2 * pair + 1 - (me - 2 * pair)).start()
        keep_own(ph)

    gpad[...] = jnp.zeros_like(gpad)
    cpad[...] = jnp.zeros_like(cpad)
    for i in range(ROWS):
        gpad[i * BLK : i * BLK + COLS, :] = gin[i]
        cpad[i * BLK : i * BLK + COLS, :] = cot[i]
    pack(gpad, 0)
    pl.semaphore_wait(barrier, LON - 1 + 2)
    start_exchange(0)
    keep_own(0)

    fstage[...] = jnp.zeros_like(fstage)
    tap = lax.broadcasted_iota(jnp.int32, (TAPS, NLON), 0)
    mode = lax.broadcasted_iota(jnp.int32, (TAPS, NLON), 1)
    scale = jnp.where(mode == 0, 1.0 / NLON, 2.0 / NLON)
    for i in range(ROWS):
        reaches = lat * ROWS + i + tap - 2
        keep = (jnp.abs(tap - 2) <= band[i]) & (reaches >= 0) & (reaches < LAT * ROWS)
        fstage[8 * i : 8 * i + TAPS, 0:NLON] = jnp.where(keep, filt[i] * scale, 0.0)
    fown[...] = fstage[...].astype(BF16)
    filter_copy(0).start()
    filter_copy(1).start()

    @pl.loop(0, MODES // 256)
    def _(step):
        at = pl.ds(pl.multiple_of(step * 256, 256), 256)
        coef[at, :] = dot_rows(fown[:, at], efwd[...])

    dhid[...] = dot_transpose(cpad[...], wdown[...])

    get_fwd.wait()
    gather_with_halo(0, 0)
    to_modes(0)
    band_sum(coef)
    get_inv.wait()
    to_grid_and_send(1)

    filter_copy(0).wait()
    filter_copy(1).wait()

    @pl.loop(0, MODES // 256)
    def _(step):
        at = pl.ds(pl.multiple_of(step * 256, 256), 256)
        rows = jnp.concatenate([fhalo[0, :, at], fown[:, at], fhalo[1, :, at]], axis=0)
        dcoef[at, :] = dot_rows(rows, ebwd[...])

    for s in range(1, LON):
        arrived(1, lax.rem(me + s, LON))

    def put_conv(i, at, half, block):
        conv[pl.ds(i * BLK + at, 64), half * 128 : half * 128 + 128] = block.astype(BF16)

    unpack(1, put_conv)

    field[...] = dot(conv[...], wmix[...])

    @pl.loop(0, FLAT // 64)
    def _(step):
        at = pl.ds(step * 64, 64)
        s16 = (gpad[at, :].astype(F32) + field[at, :]).astype(BF16)
        stream[at, :] = s16
        sf = s16.astype(F32)
        inverse = lax.rsqrt(jnp.mean(sf * sf, axis=-1, keepdims=True) + 1e-06)
        scaled[at, :] = (sf * inverse * gain[...]).astype(BF16)

    before[...] = dot(scaled[...], wup[...])

    @pl.loop(0, FLAT // 16)
    def _(step):
        at = pl.ds(step * 16, 16)
        u = before[at, :]
        u2 = u * u
        tangent = jnp.tanh(u * (SQRT_TWO_PI + (SQRT_TWO_PI * CUBIC) * u2))
        h = 0.5 * u
        hidden[at, :] = (h + h * tangent).astype(BF16)
        slope = (0.5 + 0.5 * tangent) + (h * (1.0 - tangent * tangent)) * (
            SQRT_TWO_PI + (3.0 * SQRT_TWO_PI * CUBIC) * u2
        )
        dbef[at, :] = (dhid[at, :] * slope).astype(BF16)

    field[...] = dot_transpose(dbef[...], wup[...])
    gain_o[...] = jnp.zeros_like(gain_o)

    @pl.loop(0, FLAT // 64)
    def _(step):
        at = pl.ds(step * 64, 64)
        sf = stream[at, :].astype(F32)
        inverse = lax.rsqrt(jnp.mean(sf * sf, axis=-1, keepdims=True) + 1e-06)
        normed = sf * inverse
        d_scaled = field[at, :]
        gain_o[...] += jnp.sum(d_scaled * normed, axis=0, keepdims=True)
        gained = d_scaled * gain[...]
        ds = cpad[at, :].astype(F32) + inverse * (
            gained - normed * jnp.mean(gained * normed, axis=-1, keepdims=True)
        )
        dstream[at, :] = ds
        dstream16[at, :] = ds.astype(BF16)

    field[...] = dot_transpose(dstream16[...], wmix[...])
    pack(field, 2)
    start_exchange(2)
    keep_own(2)

    field[...] = dot(hidden[...], wdown[...])
    for i in range(ROWS):
        at = slice(i * BLK, i * BLK + BLK)
        out[i] = (stream[at, :].astype(F32) + field[at, :])[0:COLS].astype(BF16)
    mix_o[...] = dot_rows(conv[...], dstream16[...])
    up_o[...] = dot_rows(scaled[...], dbef[...])
    down_o[...] = dot_rows(hidden[...], cpad[...])

    gather_with_halo(2, 1)
    to_modes(2)
    band_sum(dcoef)
    to_grid_and_send(3)
    for s in range(1, LON):
        arrived(3, lax.rem(me + s, LON))

    def put_field(i, at, half, block):
        rows = pl.ds(i * BLK + at, 64)
        lanes = slice(half * 128, half * 128 + 128)
        field[rows, lanes] = block + dstream[rows, lanes]

    unpack(3, put_field)
    for i in range(ROWS):
        grad[i] = field[i * BLK : i * BLK + BLK, :][0:COLS].astype(BF16)

    for ph in range(4):
        for s in range(1, LON):
            exchange(ph, lax.rem(me + s, LON)).wait_send()
    for hp in range(2):
        for g in range(PAIRS):
            halo_copy(hp, 0, g).wait_send()
            halo_copy(hp, 1, g).wait_send()


def local(grid_in, grid_cotangent, support_filter, band_half, w_mix, norm_gain, w_up, w_down):
    table, turned = fourier_tables()
    efwd, ebwd = expansion()
    vmem = pl.BlockSpec(memory_space=pltpu.VMEM)
    smem = pl.BlockSpec(memory_space=pltpu.SMEM)
    anywhere = pl.BlockSpec(memory_space=pl.ANY)
    outs = pl.pallas_call(
        kernel,
        out_shape=(
            jax.ShapeDtypeStruct((ROWS, COLS, CH), BF16),
            jax.ShapeDtypeStruct((ROWS, COLS, CH), BF16),
            jax.ShapeDtypeStruct((CH, CH), F32),
            jax.ShapeDtypeStruct((1, CH), F32),
            jax.ShapeDtypeStruct((CH, HID), F32),
            jax.ShapeDtypeStruct((HID, CH), F32),
        ),
        in_specs=[vmem, vmem, vmem, smem] + [vmem] * 6 + [anywhere] * 2,
        out_specs=[vmem] * 6,
        scratch_shapes=[
            pltpu.VMEM((MODES, MODES), BF16),
            pltpu.VMEM((MODES, MODES), BF16),
            pltpu.VMEM((FLAT, CH), BF16),
            pltpu.VMEM((FLAT, CH), BF16),
            pltpu.VMEM((4, LON, BLK, 128), BF16),
            pltpu.VMEM((4, LON, BLK, 128), BF16),
            pltpu.VMEM((2, 2, PAIRS, BLK, 128), BF16),
            pltpu.VMEM((2, 2, PAIRS, BLK, 128), BF16),
            pltpu.VMEM((LON, BLK, 128), BF16),
            pltpu.VMEM((32, MODES), F32),
            pltpu.VMEM((32, MODES), BF16),
            pltpu.VMEM((2, 16, MODES), BF16),
            pltpu.VMEM((MODES, TAPS * 128), F32),
            pltpu.VMEM((MODES, TAPS * 128), F32),
            pltpu.VMEM((MODES, 256), F32),
            pltpu.VMEM((MODES, 128), BF16),
            pltpu.VMEM((FLAT, CH), BF16),
            pltpu.VMEM((FLAT, CH), F32),
            pltpu.VMEM((FLAT, CH), BF16),
            pltpu.VMEM((FLAT, CH), BF16),
            pltpu.VMEM((FLAT, HID), F32),
            pltpu.VMEM((FLAT, HID), F32),
            pltpu.VMEM((FLAT, HID), BF16),
            pltpu.VMEM((FLAT, HID), BF16),
            pltpu.VMEM((FLAT, CH), F32),
            pltpu.VMEM((FLAT, CH), BF16),
            pltpu.SemaphoreType.DMA((2,)),
            pltpu.SemaphoreType.DMA((4, LON)),
            pltpu.SemaphoreType.DMA((4, LON)),
            pltpu.SemaphoreType.DMA((2, 2, PAIRS)),
            pltpu.SemaphoreType.DMA((2, 2, PAIRS)),
            pltpu.SemaphoreType.DMA((2,)),
            pltpu.SemaphoreType.DMA((2,)),
        ],
        compiler_params=pltpu.CompilerParams(
            collective_id=0, has_side_effects=True, vmem_limit_bytes=60 * 1024 * 1024
        ),
        cost_estimate=pl.CostEstimate(flops=4_700_000_000, bytes_accessed=14_000_000, transcendentals=800_000),
    )(
        grid_in, grid_cotangent, support_filter, band_half, w_mix, norm_gain.reshape(1, CH), w_up, w_down,
        jnp.asarray(efwd), jnp.asarray(ebwd), jnp.asarray(table), jnp.asarray(turned),
    )
    grid_out, grid_grad, mix_term, gain_term, up_term, down_term = outs
    summed = lax.psum((mix_term, gain_term.reshape(CH), up_term, down_term), ("lat", "lon"))
    norm_scale = float(LAT * ROWS * NLON) ** (-0.5)
    return (grid_out, grid_grad) + tuple(term * norm_scale for term in summed)


def solution(mesh):
    return jax.shard_map(
        local,
        mesh=mesh,
        in_specs=(
            P("lat", "lon", None),
            P("lat", "lon", None),
            P("lat", None, None),
            P("lat"),
            P(),
            P(),
            P(),
            P(),
        ),
        out_specs=(P("lat", "lon", None), P("lat", "lon", None), P(), P(), P(), P()),
        check_vma=False,
    )
```

```python
import jax
import jax.numpy as jnp
import ml_dtypes
import numpy as np
from jax import lax
from jax.experimental import pallas as pl
from jax.experimental.pallas import tpu as pltpu
from jax.sharding import PartitionSpec as P

SQRT_TWO_PI = 0.7978845608028654
CUBIC = 0.044715
MESH = pl.DeviceIdType.MESH
BF16 = jnp.bfloat16
F32 = jnp.float32

LAT = 32
LON = 8
PAIRS = LON // 2
ROWS = 4
COLS = 180
BLK = 192
NLON = LON * COLS
MODES = LON * BLK
CH = 256
HID = 1024
TAPS = 5
FLAT = ROWS * BLK

HALF = 2304
XA, YA = 320, 80
YB, XB = 256, 64
B_AT = 4 * XA
GAIN_AT = 2 * HALF
TILE = 16
Z_ROWS = 32
NORM_SCALE = float(LAT * ROWS * NLON) ** (-0.5)


def fourier_tables():
    modes = np.arange(NLON)
    freq = np.where(modes < NLON // 2, modes, modes - NLON // 2)
    phase = (freq[:, None] * modes[None, :]) % NLON
    angle = phase * (2.0 * np.pi / NLON)
    values = np.where((modes < NLON // 2)[:, None], np.cos(angle), np.sin(angle))
    table = np.zeros((MODES, LON, BLK), np.float32)
    table[:NLON, :, :COLS] = values.reshape(NLON, LON, COLS)
    table = table.reshape(MODES, MODES).astype(ml_dtypes.bfloat16)
    return table, np.ascontiguousarray(table.T)


def expansion():
    fwd = np.zeros((32, TAPS, ROWS, 32), np.float32)
    bwd = np.zeros((64, TAPS, ROWS, 32), np.float32)
    for w in range(TAPS):
        for i in range(ROWS):
            fwd[8 * i + w, w, i] = 1.0
            bwd[8 * (i + w) + 4 - w, w, i] = 1.0
    fwd = fwd.reshape(32, TAPS * 128)
    bwd = bwd.reshape(64, TAPS * 128)
    return fwd.astype(ml_dtypes.bfloat16), bwd.astype(ml_dtypes.bfloat16)


def dot(a, b):
    return jnp.dot(a, b, preferred_element_type=F32)


def dot_rows(a, b):
    return lax.dot_general(a, b, (((0,), (0,)), ((), ())), preferred_element_type=F32)


def dot_transpose(a, b):
    return lax.dot_general(a, b, (((1,), (1,)), ((), ())), preferred_element_type=F32)


def lanes_of(shape):
    return lax.broadcasted_iota(jnp.int32, shape, 1)


def turn_groups(parts):
    lane = lanes_of(parts[0].shape)
    low = lane < 64
    a, b, c, d = parts
    a, c = jnp.where(low, a, pltpu.roll(c, 64, 1)), jnp.where(low, pltpu.roll(a, 64, 1), c)
    b, d = jnp.where(low, b, pltpu.roll(d, 64, 1)), jnp.where(low, pltpu.roll(b, 64, 1), d)
    even = (lane % 64) < 32
    a, b = jnp.where(even, a, pltpu.roll(b, 32, 1)), jnp.where(even, pltpu.roll(a, 96, 1), b)
    c, d = jnp.where(even, c, pltpu.roll(d, 32, 1)), jnp.where(even, pltpu.roll(c, 96, 1), d)
    return a, b, c, d


def kernel(
    gin, cot, filt, band, wmix, gain, wup, wdown, efwd, ebwd, fwd_hbm, inv_hbm,
    out, grad, mix_o, gain_o, up_o, down_o,
    fwd, inv, gpad, cpad, send, recv, hsend, hrecv, halo, fstage, fown, fhalo, coef, dcoef,
    spec, banded, conv, field, stream, scaled, before, dhid, hidden, dbef, dstream, dstream16,
    gsum, part, csend, crecv, a1s, a1r, b1s, b1r, a1, b1, a2s, a2r, b2s, b2r, zf, zs, zr, zall, a3, b3, fin,
    tsem, ssem, rsem, hssem, hrsem, fssem, frsem, cssem, crsem, xssem, xrsem, yssem, yrsem, zssem, zrsem,
):
    lat = lax.axis_index("lat")
    me = lax.axis_index("lon")
    pair = me // 2
    after = lax.rem(lat + 1, LAT)
    ahead = lax.rem(lat + LAT - 1, LAT)
    core = me - 2 * pair
    x = lat // 8
    z_lo = lat // 4 - 2 * x
    y = lat - 8 * x - 4 * z_lo
    z = 2 * pair + z_lo
    mine = pl.multiple_of(core * HALF, HALF)

    def x_peer(to):
        return {"lat": to * 8 + z_lo * 4 + y}

    def y_peer(to):
        return {"lat": x * 8 + z_lo * 4 + to}

    def z_peer(to):
        return {"lat": x * 8 + (to - to // 2 * 2) * 4 + y, "lon": to // 2 * 2 + core}

    get_fwd = pltpu.make_async_copy(fwd_hbm, fwd, tsem.at[0])
    get_inv = pltpu.make_async_copy(inv_hbm, inv, tsem.at[1])
    get_fwd.start()
    get_inv.start()

    barrier = pltpu.get_barrier_semaphore()
    for s in range(1, LON):
        pl.semaphore_signal(barrier, inc=1, device_id={"lon": lax.rem(me + s, LON)}, device_id_type=MESH)
    for there in (after, ahead):
        pl.semaphore_signal(barrier, inc=1, device_id={"lat": there}, device_id_type=MESH)
    for s in range(1, 4):
        pl.semaphore_signal(barrier, inc=1, device_id=x_peer(lax.rem(x + s, 4)), device_id_type=MESH)
        pl.semaphore_signal(barrier, inc=1, device_id=y_peer(lax.rem(y + s, 4)), device_id_type=MESH)
    for s in range(1, 8):
        pl.semaphore_signal(barrier, inc=1, device_id=z_peer(lax.rem(z + s, 8)), device_id_type=MESH)

    def exchange(ph, q):
        return pltpu.make_async_remote_copy(
            src_ref=send.at[ph, q], dst_ref=recv.at[ph, me],
            send_sem=ssem.at[ph, q], recv_sem=rsem.at[ph, me],
            device_id={"lon": q}, device_id_type=MESH,
        )

    def arrived(ph, p):
        pltpu.make_async_remote_copy(
            src_ref=send.at[ph, p], dst_ref=recv.at[ph, p],
            send_sem=ssem.at[ph, p], recv_sem=rsem.at[ph, p],
            device_id={"lon": p}, device_id_type=MESH,
        ).wait_recv()

    def halo_copy(ph, side, g):
        return pltpu.make_async_remote_copy(
            src_ref=hsend.at[ph, side, g], dst_ref=hrecv.at[ph, side, g],
            send_sem=hssem.at[ph, side, g], recv_sem=hrsem.at[ph, side, g],
            device_id={"lat": after if side == 0 else ahead}, device_id_type=MESH,
        )

    def filter_copy(side):
        return pltpu.make_async_remote_copy(
            src_ref=fown.at[pl.ds(16 if side == 0 else 0, 16)], dst_ref=fhalo.at[side],
            send_sem=fssem.at[side], recv_sem=frsem.at[side],
            device_id={"lat": after if side == 0 else ahead}, device_id_type=MESH,
        )

    def pack(src, ph):
        @pl.loop(0, BLK // 64)
        def _(step):
            at = step * 64
            for half in range(2):
                parts = [
                    src[pl.ds(i * BLK + at, 64), half * 128 : half * 128 + 128].astype(F32)
                    for i in range(ROWS)
                ]
                for g, block in enumerate(turn_groups(parts)):
                    send[ph, half * 4 + g, pl.ds(at, 64), :] = block.astype(BF16)

    def unpack(ph, put):
        @pl.loop(0, BLK // 64)
        def _(step):
            at = step * 64
            for half in range(2):
                parts = [recv[ph, half * 4 + g, pl.ds(at, 64), :].astype(F32) for g in range(4)]
                for i, block in enumerate(turn_groups(parts)):
                    put(i, at, half, block)

    def start_exchange(ph):
        for s in range(1, LON):
            exchange(ph, lax.rem(me + s, LON)).start()

    def keep_own(ph):
        recv[ph, me] = send[ph, me]

    def gather_with_halo(ph, hp):
        for s in range(PAIRS):
            g = lax.rem(pair + s, PAIRS)
            if s == 0:
                arrived(ph, 2 * pair + 1 - (me - 2 * pair))
            else:
                arrived(ph, 2 * g)
                arrived(ph, 2 * g + 1)

            @pl.loop(0, BLK // 64)
            def _(step):
                at = pl.ds(step * 64, 64)
                one = recv[ph, 2 * g, at, :].astype(F32)
                two = recv[ph, 2 * g + 1, at, :].astype(F32)
                low = lanes_of(one.shape) < 64
                hsend[hp, 0, g, at, :] = jnp.where(low, pltpu.roll(one, 64, 1), two).astype(BF16)
                hsend[hp, 1, g, at, :] = jnp.where(low, one, pltpu.roll(two, 64, 1)).astype(BF16)

            halo_copy(hp, 0, g).start()
            halo_copy(hp, 1, g).start()
        for s in range(PAIRS):
            g = lax.rem(pair + s, PAIRS)
            halo_copy(hp, 0, g).wait_recv()
            halo_copy(hp, 1, g).wait_recv()

            @pl.loop(0, BLK // 64)
            def _(step):
                at = pl.ds(step * 64, 64)
                one = hrecv[hp, 0, g, at, :].astype(F32)
                two = hrecv[hp, 1, g, at, :].astype(F32)
                low = lanes_of(one.shape) < 64
                halo[2 * g, at, :] = jnp.where(low, one, pltpu.roll(two, 64, 1)).astype(BF16)
                halo[2 * g + 1, at, :] = jnp.where(low, pltpu.roll(one, 64, 1), two).astype(BF16)

    def to_modes(ph):
        @pl.loop(0, MODES // 512)
        def _(step):
            at = pl.ds(pl.multiple_of(step * 512, 512), 512)
            both = jnp.concatenate(
                [recv[ph].reshape(MODES, 128), halo[...].reshape(MODES, 128)], axis=1
            )
            spec[at, :] = dot(fwd[at, :], both)

    def band_sum(weights):
        @pl.loop(0, MODES // 64)
        def _(step):
            at = pl.ds(pl.multiple_of(step * 64, 64), 64)
            own = spec[at, 0:128]
            edge = spec[at, 128:256]
            lane = lanes_of(own.shape)
            half = pltpu.roll(own, 64, 1)
            windows = (
                jnp.where(lane < 64, edge, half),
                jnp.where(lane < 32, pltpu.roll(edge, 96, 1), pltpu.roll(own, 32, 1)),
                own,
                jnp.where(lane >= 96, pltpu.roll(edge, 32, 1), pltpu.roll(own, 96, 1)),
                jnp.where(lane >= 64, edge, half),
            )
            total = windows[0] * weights[at, 0:128]
            for w in range(1, TAPS):
                total = total + windows[w] * weights[at, w * 128 : w * 128 + 128]
            banded[at, :] = total.astype(BF16)

    def to_grid_and_send(ph):
        for s in range(PAIRS):
            g = lax.rem(pair + 1 + s, PAIRS)
            rows = pl.ds(pl.multiple_of(g * 2 * BLK, 2 * BLK), 2 * BLK)
            block = dot(inv[rows, :], banded[...]).astype(BF16)
            send[ph, 2 * g] = block[0:BLK]
            send[ph, 2 * g + 1] = block[BLK:]
            if s < PAIRS - 1:
                exchange(ph, 2 * g).start()
                exchange(ph, 2 * g + 1).start()
            else:
                exchange(ph, 2 * pair + 1 - (me - 2 * pair)).start()
        keep_own(ph)

    def core_copy(kind):
        src, dst = (csend, crecv) if kind == 0 else (fin.at[pl.ds(mine, HALF)], fin.at[pl.ds(mine, HALF)])
        return pltpu.make_async_remote_copy(
            src_ref=src, dst_ref=dst, send_sem=cssem.at[kind], recv_sem=crsem.at[kind],
            device_id={"lon": me + 1 - 2 * core}, device_id_type=MESH,
        )

    def core_arrived():
        at = pl.multiple_of((1 - core) * HALF, HALF)
        pltpu.make_async_remote_copy(
            src_ref=fin.at[pl.ds(at, HALF)], dst_ref=fin.at[pl.ds(at, HALF)],
            send_sem=cssem.at[1], recv_sem=crsem.at[1],
            device_id={"lon": me + 1 - 2 * core}, device_id_type=MESH,
        ).wait_recv()

    def x_copy(kind, to, own):
        src, dst = (
            (a1s.at[to], a1r.at[own]),
            (b2s.at[to], b2r.at[own]),
            (b3.at[pl.ds(own * XB, XB)], b3.at[pl.ds(own * XB, XB)]),
            (a3, fin.at[pl.ds(mine + own * XA, XA)]),
        )[kind]
        return src, dst

    def y_copy(kind, to, own):
        src, dst = (
            (b1s.at[to], b1r.at[own]),
            (a2s.at[to], a2r.at[own]),
            (a3.at[pl.ds(own * YA, YA)], a3.at[pl.ds(own * YA, YA)]),
            (b3, fin.at[pl.ds(mine + B_AT + own * YB, YB)]),
        )[kind]
        return src, dst

    def z_copy(kind, to, own):
        src, dst = (
            (zs.at[pl.ds(to * Z_ROWS, Z_ROWS)], zr.at[own]),
            (zall.at[pl.ds(own * Z_ROWS, Z_ROWS)], zall.at[pl.ds(own * Z_ROWS, Z_ROWS)]),
        )[kind]
        return src, dst

    rings = {
        "x": (x, 4, x_copy, x_peer, xssem, xrsem),
        "y": (y, 4, y_copy, y_peer, yssem, yrsem),
        "z": (z, 8, z_copy, z_peer, zssem, zrsem),
    }

    def ring_copy(axis, kind, to, own):
        _, _, copy, peer, send_sems, recv_sems = rings[axis]
        src, dst = copy(kind, to, own)
        return pltpu.make_async_remote_copy(
            src_ref=src, dst_ref=dst, send_sem=send_sems.at[kind, to], recv_sem=recv_sems.at[kind, own],
            device_id=peer(to), device_id_type=MESH,
        )

    def ring_start(axis, kind):
        here, count = rings[axis][:2]
        for s in range(1, count):
            ring_copy(axis, kind, lax.rem(here + s, count), here).start()

    def ring_arrived(axis, kind):
        here, count = rings[axis][:2]
        for s in range(1, count):
            there = lax.rem(here + s, count)
            ring_copy(axis, kind, there, there).wait_recv()

    def ring_sent(axis, kind):
        here, count = rings[axis][:2]
        for s in range(1, count):
            ring_copy(axis, kind, lax.rem(here + s, count), here).wait_send()

    def others(ref, here, count, rows):
        total = ref[lax.rem(here + 1, count), rows, :].astype(F32)
        for s in range(2, count):
            total = total + ref[lax.rem(here + s, count), rows, :].astype(F32)
        return total

    gain_rows = pl.ds(GAIN_AT, TILE)

    def sum_over_cores_start():
        theirs = pl.multiple_of((1 - core) * HALF, HALF)

        @pl.loop(0, HALF // 128)
        def _(step):
            csend[pl.ds(step * 128, 128), :] = part[pl.ds(theirs + step * 128, 128), :].astype(BF16)

        csend[HALF:, :] = part[gain_rows, :].astype(BF16)
        core_copy(0).start()

    def scatter_first():
        core_copy(0).wait_recv()

        def one(at, put, where):
            v = part[pl.ds(mine + at, 64), :] + crecv[pl.ds(at, 64), :].astype(F32)
            part[pl.ds(mine + at, 64), :] = v
            put[where[0], pl.ds(where[1], 64), :] = v.astype(BF16)

        for to in range(4):

            @pl.loop(0, XA // 64)
            def _(step):
                one(to * XA + step * 64, a1s, (to, step * 64))

            @pl.loop(0, YB // 64)
            def _(step):
                one(B_AT + to * YB + step * 64, b1s, (to, step * 64))

        g = part[gain_rows, :] + crecv[HALF:, :].astype(F32)
        part[gain_rows, :] = g
        for to in range(4):
            a1s[to, XA:, :] = g.astype(BF16)
        ring_start("x", 0)
        ring_start("y", 0)

    def scatter_second():
        ring_arrived("x", 0)
        ring_arrived("y", 0)

        @pl.loop(0, XA // 64)
        def _(step):
            rows = pl.ds(step * 64, 64)
            a1[rows, :] = part[pl.ds(mine + x * XA + step * 64, 64), :] + others(a1r, x, 4, rows)

        a1[XA:, :] = part[gain_rows, :] + others(a1r, x, 4, pl.ds(XA, TILE))

        @pl.loop(0, YB // 64)
        def _(step):
            rows = pl.ds(step * 64, 64)
            b1[rows, :] = part[pl.ds(mine + B_AT + y * YB + step * 64, 64), :] + others(b1r, y, 4, rows)

        for to in range(4):
            a2s[to, 0:YA, :] = a1[to * YA : to * YA + YA, :].astype(BF16)
            a2s[to, YA:, :] = a1[XA:, :].astype(BF16)
            b2s[to] = b1[to * XB : to * XB + XB, :].astype(BF16)
        ring_start("y", 1)
        ring_start("x", 1)

    def scatter_z():
        ring_arrived("y", 1)
        ring_arrived("x", 1)
        zf[YA + TILE + XB :, :] = jnp.zeros((8 * Z_ROWS - YA - TILE - XB, 128), F32)
        zf[0:YA, :] = a1[pl.ds(y * YA, YA), :] + others(a2r, y, 4, pl.ds(0, YA))
        zf[YA : YA + TILE, :] = a1[XA:, :] + others(a2r, y, 4, pl.ds(YA, TILE))
        zf[YA + TILE : YA + TILE + XB, :] = b1[pl.ds(x * XB, XB), :] + others(b2r, x, 4, pl.ds(0, XB))
        zs[...] = zf[...].astype(BF16)
        ring_start("z", 0)

    def gather_z():
        ring_arrived("z", 0)
        rows = pl.ds(pl.multiple_of(z * Z_ROWS, Z_ROWS), Z_ROWS)
        zall[rows, :] = (zf[rows, :] + others(zr, z, 8, pl.ds(0, Z_ROWS))).astype(BF16)
        ring_start("z", 1)

    def gather_first():
        ring_arrived("z", 1)
        a3[pl.ds(y * YA, YA), :] = zall[0:YA, :]
        b3[pl.ds(x * XB, XB), :] = zall[YA + TILE : YA + TILE + XB, :]
        ring_start("y", 2)
        ring_start("x", 2)

    def gather_second():
        ring_arrived("y", 2)
        ring_arrived("x", 2)
        ring_start("x", 3)
        ring_start("y", 3)
        fin[pl.ds(mine + x * XA, XA), :] = a3[...]
        fin[pl.ds(mine + B_AT + y * YB, YB), :] = b3[...]

    def gather_over_cores():
        ring_arrived("x", 3)
        ring_arrived("y", 3)
        core_copy(1).start()

    def write_sums():
        core_arrived()
        for h in range(2):
            lanes = slice(h * 128, h * 128 + 128)
            mix_o[:, lanes] = fin[h * 256 : h * 256 + 256, :].astype(F32) * NORM_SCALE
            down_o[:, lanes] = fin[2560 + h * 1024 : 2560 + h * 1024 + 1024, :].astype(F32) * NORM_SCALE
            gain_o[:, lanes] = zall[YA : YA + TILE, :].astype(F32)[h : h + 1, :] * NORM_SCALE
        for h in range(8):
            up_o[:, h * 128 : h * 128 + 128] = fin[512 + h * 256 : 768 + h * 256, :].astype(F32) * NORM_SCALE

    gpad[...] = jnp.zeros_like(gpad)
    cpad[...] = jnp.zeros_like(cpad)
    for i in range(ROWS):
        gpad[i * BLK : i * BLK + COLS, :] = gin[i]
        cpad[i * BLK : i * BLK + COLS, :] = cot[i]
    pack(gpad, 0)
    pl.semaphore_wait(barrier, LON - 1 + 2 + 3 + 3 + 7)
    start_exchange(0)
    keep_own(0)

    fstage[...] = jnp.zeros_like(fstage)
    tap = lax.broadcasted_iota(jnp.int32, (TAPS, NLON), 0)
    mode = lax.broadcasted_iota(jnp.int32, (TAPS, NLON), 1)
    scale = jnp.where(mode == 0, 1.0 / NLON, 2.0 / NLON)
    for i in range(ROWS):
        reaches = lat * ROWS + i + tap - 2
        keep = (jnp.abs(tap - 2) <= band[i]) & (reaches >= 0) & (reaches < LAT * ROWS)
        fstage[8 * i : 8 * i + TAPS, 0:NLON] = jnp.where(keep, filt[i] * scale, 0.0)
    fown[...] = fstage[...].astype(BF16)
    filter_copy(0).start()
    filter_copy(1).start()

    @pl.loop(0, MODES // 256)
    def _(step):
        at = pl.ds(pl.multiple_of(step * 256, 256), 256)
        coef[at, :] = dot_rows(fown[:, at], efwd[...])

    dhid[...] = dot_transpose(cpad[...], wdown[...])

    get_fwd.wait()
    gather_with_halo(0, 0)
    to_modes(0)
    band_sum(coef)
    get_inv.wait()
    to_grid_and_send(1)

    filter_copy(0).wait()
    filter_copy(1).wait()

    @pl.loop(0, MODES // 256)
    def _(step):
        at = pl.ds(pl.multiple_of(step * 256, 256), 256)
        rows = jnp.concatenate([fhalo[0, :, at], fown[:, at], fhalo[1, :, at]], axis=0)
        dcoef[at, :] = dot_rows(rows, ebwd[...])

    for s in range(1, LON):
        arrived(1, lax.rem(me + s, LON))

    def put_conv(i, at, half, block):
        conv[pl.ds(i * BLK + at, 64), half * 128 : half * 128 + 128] = block.astype(BF16)

    unpack(1, put_conv)

    field[...] = dot(conv[...], wmix[...])

    @pl.loop(0, FLAT // 64)
    def _(step):
        at = pl.ds(step * 64, 64)
        s16 = (gpad[at, :].astype(F32) + field[at, :]).astype(BF16)
        stream[at, :] = s16
        sf = s16.astype(F32)
        inverse = lax.rsqrt(jnp.mean(sf * sf, axis=-1, keepdims=True) + 1e-06)
        scaled[at, :] = (sf * inverse * gain[...]).astype(BF16)

    before[...] = dot(scaled[...], wup[...])

    @pl.loop(0, FLAT // 16)
    def _(step):
        at = pl.ds(step * 16, 16)
        u = before[at, :]
        u2 = u * u
        tangent = jnp.tanh(u * (SQRT_TWO_PI + (SQRT_TWO_PI * CUBIC) * u2))
        h = 0.5 * u
        hidden[at, :] = (h + h * tangent).astype(BF16)
        slope = (0.5 + 0.5 * tangent) + (h * (1.0 - tangent * tangent)) * (
            SQRT_TWO_PI + (3.0 * SQRT_TWO_PI * CUBIC) * u2
        )
        dbef[at, :] = (dhid[at, :] * slope).astype(BF16)

    field[...] = dot_transpose(dbef[...], wup[...])
    gsum[...] = jnp.zeros_like(gsum)

    @pl.loop(0, FLAT // 64)
    def _(step):
        at = pl.ds(step * 64, 64)
        sf = stream[at, :].astype(F32)
        inverse = lax.rsqrt(jnp.mean(sf * sf, axis=-1, keepdims=True) + 1e-06)
        normed = sf * inverse
        d_scaled = field[at, :]
        gsum[...] += jnp.sum(d_scaled * normed, axis=0, keepdims=True)
        gained = d_scaled * gain[...]
        ds = cpad[at, :].astype(F32) + inverse * (
            gained - normed * jnp.mean(gained * normed, axis=-1, keepdims=True)
        )
        dstream[at, :] = ds
        dstream16[at, :] = ds.astype(BF16)

    field[...] = dot_transpose(dstream16[...], wmix[...])
    pack(field, 2)
    start_exchange(2)
    keep_own(2)

    field[...] = dot(hidden[...], wdown[...])
    for i in range(ROWS):
        at = slice(i * BLK, i * BLK + BLK)
        out[i] = (stream[at, :].astype(F32) + field[at, :])[0:COLS].astype(BF16)
    term = dot_rows(conv[...], dstream16[...])
    for h in range(2):
        part[h * 256 : h * 256 + 256, :] = term[:, h * 128 : h * 128 + 128]
    term = dot_rows(scaled[...], dbef[...])
    for h in range(8):
        part[512 + h * 256 : 768 + h * 256, :] = term[:, h * 128 : h * 128 + 128]
    term = dot_rows(hidden[...], cpad[...])
    for h in range(2):
        part[2560 + h * 1024 : 3584 + h * 1024, :] = term[:, h * 128 : h * 128 + 128]
    part[gain_rows, :] = jnp.zeros((TILE, 128), F32)
    for h in range(2):
        part[GAIN_AT + h : GAIN_AT + h + 1, :] = gsum[:, h * 128 : h * 128 + 128]
    sum_over_cores_start()

    gather_with_halo(2, 1)
    scatter_first()
    to_modes(2)
    scatter_second()
    band_sum(dcoef)
    scatter_z()
    to_grid_and_send(3)
    gather_z()
    gather_first()
    gather_second()
    for s in range(1, LON):
        arrived(3, lax.rem(me + s, LON))

    def put_field(i, at, half, block):
        rows = pl.ds(i * BLK + at, 64)
        lanes = slice(half * 128, half * 128 + 128)
        field[rows, lanes] = block + dstream[rows, lanes]

    unpack(3, put_field)
    for i in range(ROWS):
        grad[i] = field[i * BLK : i * BLK + BLK, :][0:COLS].astype(BF16)

    gather_over_cores()
    write_sums()

    core_copy(0).wait_send()
    core_copy(1).wait_send()
    for kind in range(4):
        ring_sent("x", kind)
        ring_sent("y", kind)
    for kind in range(2):
        ring_sent("z", kind)
    for ph in range(4):
        for s in range(1, LON):
            exchange(ph, lax.rem(me + s, LON)).wait_send()
    for hp in range(2):
        for g in range(PAIRS):
            halo_copy(hp, 0, g).wait_send()
            halo_copy(hp, 1, g).wait_send()


def local(grid_in, grid_cotangent, support_filter, band_half, w_mix, norm_gain, w_up, w_down):
    table, turned = fourier_tables()
    efwd, ebwd = expansion()
    vmem = pl.BlockSpec(memory_space=pltpu.VMEM)
    smem = pl.BlockSpec(memory_space=pltpu.SMEM)
    anywhere = pl.BlockSpec(memory_space=pl.ANY)
    outs = pl.pallas_call(
        kernel,
        out_shape=(
            jax.ShapeDtypeStruct((ROWS, COLS, CH), BF16),
            jax.ShapeDtypeStruct((ROWS, COLS, CH), BF16),
            jax.ShapeDtypeStruct((CH, CH), F32),
            jax.ShapeDtypeStruct((1, CH), F32),
            jax.ShapeDtypeStruct((CH, HID), F32),
            jax.ShapeDtypeStruct((HID, CH), F32),
        ),
        in_specs=[vmem, vmem, vmem, smem] + [vmem] * 6 + [anywhere] * 2,
        out_specs=[vmem] * 6,
        scratch_shapes=[
            pltpu.VMEM((MODES, MODES), BF16),
            pltpu.VMEM((MODES, MODES), BF16),
            pltpu.VMEM((FLAT, CH), BF16),
            pltpu.VMEM((FLAT, CH), BF16),
            pltpu.VMEM((4, LON, BLK, 128), BF16),
            pltpu.VMEM((4, LON, BLK, 128), BF16),
            pltpu.VMEM((2, 2, PAIRS, BLK, 128), BF16),
            pltpu.VMEM((2, 2, PAIRS, BLK, 128), BF16),
            pltpu.VMEM((LON, BLK, 128), BF16),
            pltpu.VMEM((32, MODES), F32),
            pltpu.VMEM((32, MODES), BF16),
            pltpu.VMEM((2, 16, MODES), BF16),
            pltpu.VMEM((MODES, TAPS * 128), F32),
            pltpu.VMEM((MODES, TAPS * 128), F32),
            pltpu.VMEM((MODES, 256), F32),
            pltpu.VMEM((MODES, 128), BF16),
            pltpu.VMEM((FLAT, CH), BF16),
            pltpu.VMEM((FLAT, CH), F32),
            pltpu.VMEM((FLAT, CH), BF16),
            pltpu.VMEM((FLAT, CH), BF16),
            pltpu.VMEM((FLAT, HID), F32),
            pltpu.VMEM((FLAT, HID), F32),
            pltpu.VMEM((FLAT, HID), BF16),
            pltpu.VMEM((FLAT, HID), BF16),
            pltpu.VMEM((FLAT, CH), F32),
            pltpu.VMEM((FLAT, CH), BF16),
            pltpu.VMEM((1, CH), F32),
            pltpu.VMEM((2 * HALF + TILE, 128), F32),
            pltpu.VMEM((HALF + TILE, 128), BF16),
            pltpu.VMEM((HALF + TILE, 128), BF16),
            pltpu.VMEM((4, XA + TILE, 128), BF16),
            pltpu.VMEM((4, XA + TILE, 128), BF16),
            pltpu.VMEM((4, YB, 128), BF16),
            pltpu.VMEM((4, YB, 128), BF16),
            pltpu.VMEM((XA + TILE, 128), F32),
            pltpu.VMEM((YB, 128), F32),
            pltpu.VMEM((4, YA + TILE, 128), BF16),
            pltpu.VMEM((4, YA + TILE, 128), BF16),
            pltpu.VMEM((4, XB, 128), BF16),
            pltpu.VMEM((4, XB, 128), BF16),
            pltpu.VMEM((8 * Z_ROWS, 128), F32),
            pltpu.VMEM((8 * Z_ROWS, 128), BF16),
            pltpu.VMEM((8, Z_ROWS, 128), BF16),
            pltpu.VMEM((8 * Z_ROWS, 128), BF16),
            pltpu.VMEM((4 * YA, 128), BF16),
            pltpu.VMEM((4 * XB, 128), BF16),
            pltpu.VMEM((2 * HALF, 128), BF16),
            pltpu.SemaphoreType.DMA((2,)),
            pltpu.SemaphoreType.DMA((4, LON)),
            pltpu.SemaphoreType.DMA((4, LON)),
            pltpu.SemaphoreType.DMA((2, 2, PAIRS)),
            pltpu.SemaphoreType.DMA((2, 2, PAIRS)),
            pltpu.SemaphoreType.DMA((2,)),
            pltpu.SemaphoreType.DMA((2,)),
            pltpu.SemaphoreType.DMA((2,)),
            pltpu.SemaphoreType.DMA((2,)),
            pltpu.SemaphoreType.DMA((4, 4)),
            pltpu.SemaphoreType.DMA((4, 4)),
            pltpu.SemaphoreType.DMA((4, 4)),
            pltpu.SemaphoreType.DMA((4, 4)),
            pltpu.SemaphoreType.DMA((2, 8)),
            pltpu.SemaphoreType.DMA((2, 8)),
        ],
        compiler_params=pltpu.CompilerParams(
            collective_id=0, has_side_effects=True, vmem_limit_bytes=60 * 1024 * 1024
        ),
        cost_estimate=pl.CostEstimate(flops=4_700_000_000, bytes_accessed=14_000_000, transcendentals=800_000),
    )(
        grid_in, grid_cotangent, support_filter, band_half, w_mix, norm_gain.reshape(1, CH), w_up, w_down,
        jnp.asarray(efwd), jnp.asarray(ebwd), jnp.asarray(table), jnp.asarray(turned),
    )
    grid_out, grid_grad, mix_term, gain_term, up_term, down_term = outs
    return (grid_out, grid_grad, mix_term, gain_term.reshape(CH), up_term, down_term)


def solution(mesh):
    return jax.shard_map(
        local,
        mesh=mesh,
        in_specs=(
            P("lat", "lon", None),
            P("lat", "lon", None),
            P("lat", None, None),
            P("lat"),
            P(),
            P(),
            P(),
            P(),
        ),
        out_specs=(P("lat", "lon", None), P("lat", "lon", None), P(), P(), P(), P()),
        check_vma=False,
    )
```

```python
import jax
import jax.numpy as jnp
import ml_dtypes
import numpy as np
from jax import lax
from jax.experimental import pallas as pl
from jax.experimental.pallas import tpu as pltpu
from jax.sharding import PartitionSpec as P

SQRT_TWO_PI = 0.7978845608028654
CUBIC = 0.044715
MESH = pl.DeviceIdType.MESH
BF16 = jnp.bfloat16
F32 = jnp.float32

LAT = 32
LON = 8
PAIRS = LON // 2
ROWS = 4
COLS = 180
CUT = 64
CHUNKS = 3
BLK = CUT * CHUNKS
NLON = LON * COLS
MODES = LON * BLK
WIDE = LON * CUT
CH = 256
HID = 1024
TAPS = 5
FLAT = ROWS * BLK
PART = ROWS * CUT

HALF = 2304
UP_AT, DOWN_AT = 256, 1280
GAIN_AT = 2 * HALF
PLANE = 16
SHARE = HALF // PLANE
TILE = 16
Z_ROWS = 32
NORM_SCALE = float(LAT * ROWS * NLON) ** (-0.5)


def fourier_tables():
    modes = np.arange(NLON)
    freq = np.where(modes < NLON // 2, modes, modes - NLON // 2)
    phase = (freq[:, None] * modes[None, :]) % NLON
    angle = phase * (2.0 * np.pi / NLON)
    values = np.where((modes < NLON // 2)[:, None], np.cos(angle), np.sin(angle))
    table = np.zeros((MODES, LON, BLK), np.float32)
    table[:NLON, :, :COLS] = values.reshape(NLON, LON, COLS)
    table = table.reshape(MODES, LON, CHUNKS, CUT).astype(ml_dtypes.bfloat16)
    forward = np.ascontiguousarray(table.transpose(2, 0, 1, 3)).reshape(CHUNKS, MODES, WIDE)
    inverse = np.ascontiguousarray(table.transpose(2, 1, 3, 0)).reshape(CHUNKS, WIDE, MODES)
    return forward, inverse


def expansion():
    fwd = np.zeros((32, TAPS, ROWS, 32), np.float32)
    bwd = np.zeros((64, TAPS, ROWS, 32), np.float32)
    for w in range(TAPS):
        for i in range(ROWS):
            fwd[8 * i + w, w, i] = 1.0
            bwd[8 * (i + w) + 4 - w, w, i] = 1.0
    fwd = fwd.reshape(32, TAPS * 128)
    bwd = bwd.reshape(64, TAPS * 128)
    return fwd.astype(ml_dtypes.bfloat16), bwd.astype(ml_dtypes.bfloat16)


def dot(a, b):
    return jnp.dot(a, b, preferred_element_type=F32)


def dot_rows(a, b):
    return lax.dot_general(a, b, (((0,), (0,)), ((), ())), preferred_element_type=F32)


def dot_transpose(a, b):
    return lax.dot_general(a, b, (((1,), (1,)), ((), ())), preferred_element_type=F32)


def lanes_of(shape):
    return lax.broadcasted_iota(jnp.int32, shape, 1)


def turn_groups(parts):
    lane = lanes_of(parts[0].shape)
    low = lane < 64
    a, b, c, d = parts
    a, c = jnp.where(low, a, pltpu.roll(c, 64, 1)), jnp.where(low, pltpu.roll(a, 64, 1), c)
    b, d = jnp.where(low, b, pltpu.roll(d, 64, 1)), jnp.where(low, pltpu.roll(b, 64, 1), d)
    even = (lane % 64) < 32
    a, b = jnp.where(even, a, pltpu.roll(b, 32, 1)), jnp.where(even, pltpu.roll(a, 96, 1), b)
    c, d = jnp.where(even, c, pltpu.roll(d, 32, 1)), jnp.where(even, pltpu.roll(c, 96, 1), d)
    return a, b, c, d


def kernel(
    gin_hbm, cot_hbm, filt_hbm, band, wmix_hbm, gain_hbm, wup_hbm, wdown_hbm, efwd_hbm, ebwd_hbm, fwd_hbm, inv_hbm,
    out, grad, sums,
    fwd, inv, gf, cflat, send, recv, hsend, hrecv, halo, fstage, fown, fhalo, coef, dcoef,
    spec, banded, cf, conv, field, stream, scaled, before, dhid, hidden, dbef, ds, ds16, res, gres,
    gsum, part, csend, crecv, ps, pr, zf, zs, zr, zall, fin,
    gin, cot, filt, wmix, gain, wup, wdown, efwd, ebwd,
    isem, osem, ssem, rsem, hssem, hrsem, fssem, frsem, cssem, crsem, pssem, prsem, zssem, zrsem,
):
    lat = lax.axis_index("lat")
    me = lax.axis_index("lon")
    pair = me // 2
    after = lax.rem(lat + 1, LAT)
    ahead = lax.rem(lat + LAT - 1, LAT)
    core = me - 2 * pair
    x = lat // 8
    z_lo = lat // 4 - 2 * x
    y = lat - 8 * x - 4 * z_lo
    z = 2 * pair + z_lo
    mine = pl.multiple_of(core * HALF, HALF)

    plane = 4 * x + y

    def plane_peer(to):
        return {"lat": to // 4 * 8 + z_lo * 4 + (to - to // 4 * 4)}

    def z_peer(to):
        return {"lat": x * 8 + (to - to // 2 * 2) * 4 + y, "lon": to // 2 * 2 + core}

    inputs = (
        (gin_hbm, gin), (filt_hbm, filt), (efwd_hbm, efwd), (cot_hbm, cot), (wdown_hbm, wdown), (fwd_hbm, fwd),
        (inv_hbm, inv), (ebwd_hbm, ebwd), (wmix_hbm, wmix), (gain_hbm, gain), (wup_hbm, wup),
    )
    gets = [pltpu.make_async_copy(src, dst, isem.at[k]) for k, (src, dst) in enumerate(inputs)]
    gets[0].start()

    barrier = pltpu.get_barrier_semaphore()
    for s in range(1, LON):
        pl.semaphore_signal(barrier, inc=1, device_id={"lon": lax.rem(me + s, LON)}, device_id_type=MESH)
    for there in (after, ahead):
        pl.semaphore_signal(barrier, inc=1, device_id={"lat": there}, device_id_type=MESH)
    for s in range(1, PLANE):
        there = plane_peer(lax.rem(plane + s, PLANE))
        pl.semaphore_signal(barrier, inc=1, device_id=there, device_id_type=MESH)
    for s in range(1, 8):
        pl.semaphore_signal(barrier, inc=1, device_id=z_peer(lax.rem(z + s, 8)), device_id_type=MESH)

    for get in gets[1:]:
        get.start()

    def exchange(ph, c, to, own):
        return pltpu.make_async_remote_copy(
            src_ref=send.at[ph, c, to], dst_ref=recv.at[ph, c, own],
            send_sem=ssem.at[ph, c, to], recv_sem=rsem.at[ph, c, own],
            device_id={"lon": to}, device_id_type=MESH,
        )

    def start_exchange(ph, c):
        for s in (4, 3, 5, 2, 6, 7, 1):
            exchange(ph, c, lax.rem(me + s, LON), me).start()
        recv[ph, c, me] = send[ph, c, me]

    def arrived(ph, c):
        for s in range(1, LON):
            there = lax.rem(me + s, LON)
            exchange(ph, c, there, there).wait_recv()

    def halo_copy(hp, side, c):
        return pltpu.make_async_remote_copy(
            src_ref=hsend.at[hp, side, c], dst_ref=hrecv.at[hp, side, c],
            send_sem=hssem.at[hp, side, c], recv_sem=hrsem.at[hp, side, c],
            device_id={"lat": after if side == 0 else ahead}, device_id_type=MESH,
        )

    def filter_copy(side):
        return pltpu.make_async_remote_copy(
            src_ref=fown.at[pl.ds(16 if side == 0 else 0, 16)], dst_ref=fhalo.at[side],
            send_sem=fssem.at[side], recv_sem=frsem.at[side],
            device_id={"lat": after if side == 0 else ahead}, device_id_type=MESH,
        )

    def pack(src, ph, c):
        for half in range(2):
            parts = [src[half, pl.ds(c * PART + i, CUT, stride=ROWS), :] for i in range(ROWS)]
            for g, block in enumerate(turn_groups(parts)):
                send[ph, c, half * 4 + g] = block.astype(BF16)

    def unpack(ph, c, put):
        for half in range(2):
            parts = [recv[ph, c, half * 4 + g].astype(F32) for g in range(4)]
            for i, block in enumerate(turn_groups(parts)):
                put(half, pl.ds(c * PART + i, CUT, stride=ROWS), block)

    def pass_halo(ph, hp, c):
        arrived(ph, c)
        for g in range(PAIRS):
            one = recv[ph, c, 2 * g].astype(F32)
            two = recv[ph, c, 2 * g + 1].astype(F32)
            low = lanes_of(one.shape) < 64
            hsend[hp, 0, c, g] = jnp.where(low, pltpu.roll(one, 64, 1), two).astype(BF16)
            hsend[hp, 1, c, g] = jnp.where(low, one, pltpu.roll(two, 64, 1)).astype(BF16)
        halo_copy(hp, 0, c).start()
        halo_copy(hp, 1, c).start()

    def to_modes(ph, hp, c):
        halo_copy(hp, 0, c).wait_recv()
        halo_copy(hp, 1, c).wait_recv()
        for g in range(PAIRS):
            one = hrecv[hp, 0, c, g].astype(F32)
            two = hrecv[hp, 1, c, g].astype(F32)
            low = lanes_of(one.shape) < 64
            halo[c, 2 * g] = jnp.where(low, one, pltpu.roll(two, 64, 1)).astype(BF16)
            halo[c, 2 * g + 1] = jnp.where(low, pltpu.roll(one, 64, 1), two).astype(BF16)

        @pl.loop(0, MODES // 512)
        def _(step):
            at = pl.ds(pl.multiple_of(step * 512, 512), 512)
            both = jnp.concatenate(
                [recv[ph, c].reshape(WIDE, 128), halo[c].reshape(WIDE, 128)], axis=1
            )
            term = dot(fwd[c, at, :], both)
            spec[at, :] = term if c == 0 else spec[at, :] + term

    def band_sum(weights, first, last):
        @pl.loop(first, last)
        def _(step):
            at = pl.ds(pl.multiple_of(step * 128, 128), 128)
            own = spec[at, 0:128]
            edge = spec[at, 128:256]
            lane = lanes_of(own.shape)
            half = pltpu.roll(own, 64, 1)
            windows = (
                jnp.where(lane < 64, edge, half),
                jnp.where(lane < 32, pltpu.roll(edge, 96, 1), pltpu.roll(own, 32, 1)),
                own,
                jnp.where(lane >= 96, pltpu.roll(edge, 32, 1), pltpu.roll(own, 96, 1)),
                jnp.where(lane >= 64, edge, half),
            )
            total = windows[0] * weights[at, 0:128]
            for w in range(1, TAPS):
                total = total + windows[w] * weights[at, w * 128 : w * 128 + 128]
            banded[at, :] = total.astype(BF16)

    def to_grid(ph, c):
        block = dot(inv[c], banded[...]).astype(BF16)
        for q in range(LON):
            send[ph, c, q] = block[q * CUT : q * CUT + CUT]
        start_exchange(ph, c)

    theirs = pl.multiple_of((1 - core) * HALF, HALF)
    other_core = {"lon": me + 1 - 2 * core}
    gain_rows = pl.ds(GAIN_AT, TILE)

    def core_copy(kind):
        rows = pl.ds(0, DOWN_AT) if kind == 0 else pl.ds(DOWN_AT, HALF + TILE - DOWN_AT)
        return pltpu.make_async_remote_copy(
            src_ref=csend.at[rows], dst_ref=crecv.at[rows], send_sem=cssem.at[kind], recv_sem=crsem.at[kind],
            device_id=other_core, device_id_type=MESH,
        )

    def core_gather(base, k):
        rows = pl.ds(base + k * SHARE, SHARE)
        return pltpu.make_async_remote_copy(
            src_ref=fin.at[rows], dst_ref=fin.at[rows], send_sem=cssem.at[2 + k], recv_sem=crsem.at[2 + k],
            device_id=other_core, device_id_type=MESH,
        )

    def plane_copy(kind, to, own):
        src, dst = (
            (ps.at[to], pr.at[own]),
            (zall.at[pl.ds(0, SHARE)], fin.at[pl.ds(mine + own * SHARE, SHARE)]),
        )[kind]
        return src, dst

    def z_copy(kind, to, own):
        src, dst = (
            (zs.at[pl.ds(to * Z_ROWS, Z_ROWS)], zr.at[own]),
            (zall.at[pl.ds(own * Z_ROWS, Z_ROWS)], zall.at[pl.ds(own * Z_ROWS, Z_ROWS)]),
        )[kind]
        return src, dst

    rings = {
        "plane": (plane, PLANE, plane_copy, plane_peer, pssem, prsem),
        "z": (z, 8, z_copy, z_peer, zssem, zrsem),
    }

    def ring_copy(axis, kind, to, own):
        _, _, copy, peer, send_sems, recv_sems = rings[axis]
        src, dst = copy(kind, to, own)
        return pltpu.make_async_remote_copy(
            src_ref=src, dst_ref=dst, send_sem=send_sems.at[kind, to], recv_sem=recv_sems.at[kind, own],
            device_id=peer(to), device_id_type=MESH,
        )

    def ring_start(axis, kind):
        here, count = rings[axis][:2]
        for s in range(1, count):
            ring_copy(axis, kind, lax.rem(here + s, count), here).start()

    def ring_arrived(axis, kind):
        here, count = rings[axis][:2]
        for s in range(1, count):
            there = lax.rem(here + s, count)
            ring_copy(axis, kind, there, there).wait_recv()

    def ring_sent(axis, kind):
        here, count = rings[axis][:2]
        for s in range(1, count):
            ring_copy(axis, kind, lax.rem(here + s, count), here).wait_send()

    def others(ref, here, count, rows):
        total = ref[lax.rem(here + 1, count), rows, :].astype(F32)
        for s in range(2, count):
            total = total + ref[lax.rem(here + s, count), rows, :].astype(F32)
        return total

    def send_half(first, last):
        @pl.loop(first // 256, last // 256)
        def _(step):
            csend[pl.ds(step * 256, 256), :] = part[pl.ds(theirs + step * 256, 256), :].astype(BF16)

    def scatter_plane():
        core_copy(0).wait_recv()
        core_copy(1).wait_recv()
        g = part[gain_rows, :] + crecv[HALF:, :].astype(F32)
        part[gain_rows, :] = g

        @pl.loop(0, PLANE)
        def _(to):
            v = part[pl.ds(mine + to * SHARE, SHARE), :] + crecv[pl.ds(to * SHARE, SHARE), :].astype(F32)
            part[pl.ds(mine + to * SHARE, SHARE), :] = v
            ps[to, 0:SHARE, :] = v.astype(BF16)
            ps[to, SHARE:, :] = g.astype(BF16)

        ring_start("plane", 0)

    def scatter_z():
        ring_arrived("plane", 0)
        zf[SHARE + TILE :, :] = jnp.zeros((8 * Z_ROWS - SHARE - TILE, 128), F32)
        zf[0:SHARE, :] = part[pl.ds(mine + plane * SHARE, SHARE), :] + others(pr, plane, PLANE, pl.ds(0, SHARE))
        zf[SHARE : SHARE + TILE, :] = part[gain_rows, :] + others(pr, plane, PLANE, pl.ds(SHARE, TILE))
        zs[...] = zf[...].astype(BF16)
        ring_start("z", 0)

    def gather_z():
        ring_arrived("z", 0)
        rows = pl.ds(pl.multiple_of(z * Z_ROWS, Z_ROWS), Z_ROWS)
        zall[rows, :] = (zf[rows, :] + others(zr, z, 8, pl.ds(0, Z_ROWS))).astype(BF16)
        ring_start("z", 1)

    def gather_plane():
        ring_arrived("z", 1)
        ring_start("plane", 1)
        fin[pl.ds(mine + plane * SHARE, SHARE), :] = zall[0:SHARE, :]
        core_gather(mine, plane).start()

    def gather_core():
        for s in range(1, PLANE):
            there = lax.rem(plane + s, PLANE)
            ring_copy("plane", 1, there, there).wait_recv()
            core_gather(mine, there).start()

    gets[0].wait()
    for half in range(2):
        gf[half, ROWS * COLS :, :] = jnp.zeros((FLAT - ROWS * COLS, 128), F32)
    for c in range(CHUNKS):
        count = min(CUT, COLS - c * CUT)
        rows = gin[c * CUT : c * CUT + count].astype(F32).reshape(ROWS * count, CH)
        for half in range(2):
            gf[half, c * PART : c * PART + ROWS * count, :] = rows[:, half * 128 : half * 128 + 128]
    pack(gf, 0, 0)
    pl.semaphore_wait(barrier, LON - 1 + 2 + PLANE - 1 + 7)
    start_exchange(0, 0)
    for c in range(1, CHUNKS):
        pack(gf, 0, c)
        start_exchange(0, c)

    gets[1].wait()
    gets[2].wait()
    fstage[...] = jnp.zeros_like(fstage)
    row = lax.broadcasted_iota(jnp.int32, (ROWS, NLON), 0)
    mode = lax.broadcasted_iota(jnp.int32, (ROWS, NLON), 1)
    scale = jnp.where(mode == 0, 1.0 / NLON, 2.0 / NLON)
    reach = jnp.where(row == 0, band[0], jnp.where(row == 1, band[1], jnp.where(row == 2, band[2], band[3])))
    for t in range(TAPS):
        at = lat * ROWS + row + (t - 2)
        keep = (reach >= abs(t - 2)) & (at >= 0) & (at < LAT * ROWS)
        kept = jnp.where(keep, filt[t] * scale, 0.0)
        for i in range(ROWS):
            fstage[8 * i + t : 8 * i + t + 1, 0:NLON] = kept[i : i + 1, :]
    fown[...] = fstage[...].astype(BF16)
    filter_copy(0).start()
    filter_copy(1).start()

    @pl.loop(0, MODES // 256)
    def _(step):
        at = pl.ds(pl.multiple_of(step * 256, 256), 256)
        coef[at, :] = dot_rows(fown[:, at], efwd[...])

    gets[3].wait()
    gets[4].wait()
    cflat[ROWS * COLS :, :] = jnp.zeros((FLAT - ROWS * COLS, CH), BF16)
    cflat[0 : ROWS * COLS, :] = cot[...].reshape(ROWS * COLS, CH)
    dhid[...] = dot_transpose(cflat[...], wdown[...])
    gsum[...] = jnp.zeros_like(gsum)

    for c in range(CHUNKS):
        pass_halo(0, 0, c)
    gets[5].wait()
    for c in range(CHUNKS):
        to_modes(0, 0, c)
    band_sum(coef, 0, MODES // 128)
    gets[6].wait()
    for c in range(CHUNKS):
        to_grid(1, c)

    for get in gets[7:]:
        get.wait()
    filter_copy(0).wait()
    filter_copy(1).wait()

    @pl.loop(0, MODES // 256)
    def _(step):
        at = pl.ds(pl.multiple_of(step * 256, 256), 256)
        rows = jnp.concatenate([fhalo[0, :, at], fown[:, at], fhalo[1, :, at]], axis=0)
        dcoef[at, :] = dot_rows(rows, ebwd[...])

    def put_conv(half, rows, block):
        cf[half, rows, :] = block

    def tail(c):
        arrived(1, c)
        unpack(1, c, put_conv)
        all_rows = pl.ds(c * PART, PART)
        conv[all_rows, :] = jnp.concatenate([cf[0, all_rows, :], cf[1, all_rows, :]], axis=1).astype(BF16)
        field[all_rows, :] = dot(conv[all_rows, :], wmix[...])

        @pl.loop(0, PART // 128)
        def _(step):
            at = pl.ds(c * PART + step * 128, 128)
            mixed = field[at, :] + jnp.concatenate([gf[0, at, :], gf[1, at, :]], axis=1)
            s16 = mixed.astype(BF16)
            stream[at, :] = s16
            sf = s16.astype(F32)
            inverse = lax.rsqrt(jnp.mean(sf * sf, axis=-1, keepdims=True) + 1e-06)
            scaled[at, :] = (sf * inverse * gain[...]).astype(BF16)

        before[all_rows, :] = dot(scaled[all_rows, :], wup[...])

        @pl.loop(0, PART // 16)
        def _(step):
            at = pl.ds(c * PART + step * 16, 16)
            u = before[at, :]
            u2 = u * u
            tangent = jnp.tanh(u * (SQRT_TWO_PI + (SQRT_TWO_PI * CUBIC) * u2))
            h = 0.5 * u
            hidden[at, :] = (h + h * tangent).astype(BF16)
            slope = (0.5 + 0.5 * tangent) + (h * (1.0 - tangent * tangent)) * (
                SQRT_TWO_PI + (3.0 * SQRT_TWO_PI * CUBIC) * u2
            )
            dbef[at, :] = (dhid[at, :] * slope).astype(BF16)

        field[all_rows, :] = dot_transpose(dbef[all_rows, :], wup[...])

        @pl.loop(0, PART // 128)
        def _(step):
            at = pl.ds(c * PART + step * 128, 128)
            sf = stream[at, :].astype(F32)
            inverse = lax.rsqrt(jnp.mean(sf * sf, axis=-1, keepdims=True) + 1e-06)
            normed = sf * inverse
            d_scaled = field[at, :]
            gsum[...] += jnp.sum(d_scaled * normed, axis=0, keepdims=True)
            gained = d_scaled * gain[...]
            value = cflat[at, :].astype(F32) + inverse * (
                gained - normed * jnp.mean(gained * normed, axis=-1, keepdims=True)
            )
            for half in range(2):
                ds[half, at, :] = value[:, half * 128 : half * 128 + 128]
            ds16[at, :] = value.astype(BF16)

        d_conv = dot_transpose(ds16[all_rows, :], wmix[...])
        for half in range(2):
            cf[half, all_rows, :] = d_conv[:, half * 128 : half * 128 + 128]
        pack(cf, 2, c)
        start_exchange(2, c)

    for c in range(CHUNKS):
        tail(c)

    term = dot_rows(conv[...], ds16[...])
    for h in range(2):
        part[h * HALF : h * HALF + UP_AT, :] = term[:, h * 128 : h * 128 + 128]
    term = dot_rows(scaled[...], dbef[...])
    for h in range(8):
        at = h // 4 * HALF + UP_AT + h % 4 * 256
        part[at : at + 256, :] = term[:, h * 128 : h * 128 + 128]
    send_half(0, DOWN_AT)
    core_copy(0).start()
    term = dot_rows(hidden[...], cflat[...])
    for h in range(2):
        part[h * HALF + DOWN_AT : (h + 1) * HALF, :] = term[:, h * 128 : h * 128 + 128]
    part[gain_rows, :] = jnp.zeros((TILE, 128), F32)
    for h in range(2):
        part[GAIN_AT + h : GAIN_AT + h + 1, :] = gsum[:, h * 128 : h * 128 + 128]
    send_half(DOWN_AT, HALF)
    csend[HALF:, :] = part[gain_rows, :].astype(BF16)
    core_copy(1).start()

    result = stream[...].astype(F32) + dot(hidden[...], wdown[...])
    res[...] = result[0 : ROWS * COLS].reshape(COLS, ROWS, CH).astype(BF16)
    put_out = pltpu.make_async_copy(res, out, osem.at[0])
    put_out.start()
    scatter_plane()

    for c in range(CHUNKS):
        pass_halo(2, 1, c)
    for c in range(CHUNKS):
        to_modes(2, 1, c)
    scatter_z()
    band_sum(dcoef, 0, MODES // 128)
    for c in range(CHUNKS):
        to_grid(3, c)
    gather_z()

    def put_grad(half, rows, block):
        ds[half, rows, :] = block + ds[half, rows, :]

    gather_plane()
    for c in range(CHUNKS):
        arrived(3, c)
        unpack(3, c, put_grad)
        count = min(CUT, COLS - c * CUT)
        rows = pl.ds(c * PART, ROWS * count)
        both = jnp.concatenate([ds[0, rows, :], ds[1, rows, :]], axis=1)
        gres[c * CUT : c * CUT + count] = both.reshape(count, ROWS, CH).astype(BF16)
    put_grad_out = pltpu.make_async_copy(gres, grad, osem.at[1])
    put_grad_out.start()
    gather_core()
    put_gain = pltpu.make_async_copy(zall.at[pl.ds(SHARE, TILE)], sums.at[pl.ds(GAIN_AT, TILE)], osem.at[2])
    put_own = pltpu.make_async_copy(fin.at[pl.ds(mine, HALF)], sums.at[pl.ds(mine, HALF)], osem.at[3])
    put_other = pltpu.make_async_copy(fin.at[pl.ds(theirs, HALF)], sums.at[pl.ds(theirs, HALF)], osem.at[4])
    put_gain.start()
    put_own.start()
    for k in range(PLANE):
        core_gather(theirs, k).wait_recv()
    put_other.start()

    core_copy(0).wait_send()
    core_copy(1).wait_send()
    for k in range(PLANE):
        core_gather(mine, k).wait_send()
    for kind in range(2):
        ring_sent("plane", kind)
        ring_sent("z", kind)
    for ph in range(4):
        for c in range(CHUNKS):
            for s in range(1, LON):
                exchange(ph, c, lax.rem(me + s, LON), me).wait_send()
    for hp in range(2):
        for c in range(CHUNKS):
            halo_copy(hp, 0, c).wait_send()
            halo_copy(hp, 1, c).wait_send()
    put_out.wait()
    put_grad_out.wait()
    put_gain.wait()
    put_own.wait()
    put_other.wait()


def finish(res, gres, sums, out, grad, mix_o, gain_o, up_o, down_o):
    out[...] = res[...]
    grad[...] = gres[...]
    for h in range(2):
        lanes = slice(h * 128, h * 128 + 128)
        at = h * HALF
        mix_o[:, lanes] = sums[at : at + UP_AT, :].astype(F32) * NORM_SCALE
        down_o[:, lanes] = sums[at + DOWN_AT : at + HALF, :].astype(F32) * NORM_SCALE
        gain_o[:, lanes] = sums[GAIN_AT : GAIN_AT + TILE, :].astype(F32)[h : h + 1, :] * NORM_SCALE
    for h in range(8):
        at = h // 4 * HALF + UP_AT + h % 4 * 256
        up_o[:, h * 128 : h * 128 + 128] = sums[at : at + 256, :].astype(F32) * NORM_SCALE


def local(grid_in, grid_cotangent, support_filter, band_half, w_mix, norm_gain, w_up, w_down):
    forward, inverse = fourier_tables()
    efwd, ebwd = expansion()
    vmem = pl.BlockSpec(memory_space=pltpu.VMEM)
    smem = pl.BlockSpec(memory_space=pltpu.SMEM)
    anywhere = pl.BlockSpec(memory_space=pl.ANY)
    field = jax.ShapeDtypeStruct((COLS, ROWS, CH), BF16)
    res, gres, sums = pl.pallas_call(
        kernel,
        out_shape=(field, field, jax.ShapeDtypeStruct((2 * HALF + TILE, 128), BF16)),
        in_specs=[anywhere] * 3 + [smem] + [anywhere] * 8,
        out_specs=[anywhere] * 3,
        scratch_shapes=[
            pltpu.VMEM((CHUNKS, MODES, WIDE), BF16),
            pltpu.VMEM((CHUNKS, WIDE, MODES), BF16),
            pltpu.VMEM((2, FLAT, 128), F32),
            pltpu.VMEM((FLAT, CH), BF16),
            pltpu.VMEM((4, CHUNKS, LON, CUT, 128), BF16),
            pltpu.VMEM((4, CHUNKS, LON, CUT, 128), BF16),
            pltpu.VMEM((2, 2, CHUNKS, PAIRS, CUT, 128), BF16),
            pltpu.VMEM((2, 2, CHUNKS, PAIRS, CUT, 128), BF16),
            pltpu.VMEM((CHUNKS, LON, CUT, 128), BF16),
            pltpu.VMEM((32, MODES), F32),
            pltpu.VMEM((32, MODES), BF16),
            pltpu.VMEM((2, 16, MODES), BF16),
            pltpu.VMEM((MODES, TAPS * 128), F32),
            pltpu.VMEM((MODES, TAPS * 128), F32),
            pltpu.VMEM((MODES, 256), F32),
            pltpu.VMEM((MODES, 128), BF16),
            pltpu.VMEM((2, FLAT, 128), F32),
            pltpu.VMEM((FLAT, CH), BF16),
            pltpu.VMEM((FLAT, CH), F32),
            pltpu.VMEM((FLAT, CH), BF16),
            pltpu.VMEM((FLAT, CH), BF16),
            pltpu.VMEM((FLAT, HID), F32),
            pltpu.VMEM((FLAT, HID), F32),
            pltpu.VMEM((FLAT, HID), BF16),
            pltpu.VMEM((FLAT, HID), BF16),
            pltpu.VMEM((2, FLAT, 128), F32),
            pltpu.VMEM((FLAT, CH), BF16),
            pltpu.VMEM((COLS, ROWS, CH), BF16),
            pltpu.VMEM((COLS, ROWS, CH), BF16),
            pltpu.VMEM((1, CH), F32),
            pltpu.VMEM((2 * HALF + TILE, 128), F32),
            pltpu.VMEM((HALF + TILE, 128), BF16),
            pltpu.VMEM((HALF + TILE, 128), BF16),
            pltpu.VMEM((PLANE, SHARE + TILE, 128), BF16),
            pltpu.VMEM((PLANE, SHARE + TILE, 128), BF16),
            pltpu.VMEM((8 * Z_ROWS, 128), F32),
            pltpu.VMEM((8 * Z_ROWS, 128), BF16),
            pltpu.VMEM((8, Z_ROWS, 128), BF16),
            pltpu.VMEM((8 * Z_ROWS, 128), BF16),
            pltpu.VMEM((2 * HALF, 128), BF16),
            pltpu.VMEM((COLS, ROWS, CH), BF16),
            pltpu.VMEM((COLS, ROWS, CH), BF16),
            pltpu.VMEM((TAPS, ROWS, NLON), F32),
            pltpu.VMEM((CH, CH), BF16),
            pltpu.VMEM((1, CH), F32),
            pltpu.VMEM((CH, HID), BF16),
            pltpu.VMEM((HID, CH), BF16),
            pltpu.VMEM((32, TAPS * 128), BF16),
            pltpu.VMEM((64, TAPS * 128), BF16),
            pltpu.SemaphoreType.DMA((11,)),
            pltpu.SemaphoreType.DMA((5,)),
            pltpu.SemaphoreType.DMA((4, CHUNKS, LON)),
            pltpu.SemaphoreType.DMA((4, CHUNKS, LON)),
            pltpu.SemaphoreType.DMA((2, 2, CHUNKS)),
            pltpu.SemaphoreType.DMA((2, 2, CHUNKS)),
            pltpu.SemaphoreType.DMA((2,)),
            pltpu.SemaphoreType.DMA((2,)),
            pltpu.SemaphoreType.DMA((2 + PLANE,)),
            pltpu.SemaphoreType.DMA((2 + PLANE,)),
            pltpu.SemaphoreType.DMA((2, PLANE)),
            pltpu.SemaphoreType.DMA((2, PLANE)),
            pltpu.SemaphoreType.DMA((2, 8)),
            pltpu.SemaphoreType.DMA((2, 8)),
        ],
        compiler_params=pltpu.CompilerParams(
            collective_id=0, has_side_effects=True, vmem_limit_bytes=60 * 1024 * 1024
        ),
        cost_estimate=pl.CostEstimate(flops=4_700_000_000, bytes_accessed=14_000_000, transcendentals=800_000),
    )(
        jnp.transpose(grid_in, (1, 0, 2)), jnp.transpose(grid_cotangent, (1, 0, 2)),
        jnp.transpose(support_filter, (1, 0, 2)), band_half, w_mix, norm_gain.reshape(1, CH), w_up, w_down,
        jnp.asarray(efwd), jnp.asarray(ebwd), jnp.asarray(forward), jnp.asarray(inverse),
    )
    grid_out, grid_grad, mix_grad, gain_grad, up_grad, down_grad = pl.pallas_call(
        finish,
        out_shape=(
            field,
            field,
            jax.ShapeDtypeStruct((CH, CH), F32),
            jax.ShapeDtypeStruct((1, CH), F32),
            jax.ShapeDtypeStruct((CH, HID), F32),
            jax.ShapeDtypeStruct((HID, CH), F32),
        ),
        in_specs=[vmem] * 3,
        out_specs=[vmem] * 6,
        compiler_params=pltpu.CompilerParams(vmem_limit_bytes=60 * 1024 * 1024),
    )(res, gres, sums)
    return (
        jnp.transpose(grid_out, (1, 0, 2)),
        jnp.transpose(grid_grad, (1, 0, 2)),
        mix_grad,
        gain_grad.reshape(CH),
        up_grad,
        down_grad,
    )


def solution(mesh):
    return jax.shard_map(
        local,
        mesh=mesh,
        in_specs=(
            P("lat", "lon", None),
            P("lat", "lon", None),
            P("lat", None, None),
            P("lat"),
            P(),
            P(),
            P(),
            P(),
        ),
        out_specs=(P("lat", "lon", None), P("lat", "lon", None), P(), P(), P(), P()),
        check_vma=False,
    )
```

```python
import jax
import jax.numpy as jnp
import ml_dtypes
import numpy as np
from jax import lax
from jax.experimental import pallas as pl
from jax.experimental.pallas import tpu as pltpu
from jax.sharding import PartitionSpec as P

SQRT_TWO_PI = 0.7978845608028654
CUBIC = 0.044715
MESH = pl.DeviceIdType.MESH
BF16 = jnp.bfloat16
F32 = jnp.float32

LAT = 32
LON = 8
PAIRS = LON // 2
ROWS = 4
COLS = 180
CUT = 64
CHUNKS = 3
BLK = CUT * CHUNKS
NLON = LON * COLS
MODES = LON * BLK
WIDE = LON * CUT
CH = 256
HID = 1024
TAPS = 5
FLAT = ROWS * BLK
PART = ROWS * CUT

HALF = 2304
UP_AT, DOWN_AT = 256, 1280
GAIN_AT = 2 * HALF
PLANE = 16
SHARE = HALF // PLANE
GROUP = 5
TILE = 16
Z_ROWS = 32
NORM_SCALE = float(LAT * ROWS * NLON) ** (-0.5)


def fourier_tables():
    modes = np.arange(NLON)
    freq = np.where(modes < NLON // 2, modes, modes - NLON // 2)
    phase = (freq[:, None] * modes[None, :]) % NLON
    angle = phase * (2.0 * np.pi / NLON)
    values = np.where((modes < NLON // 2)[:, None], np.cos(angle), np.sin(angle))
    table = np.zeros((MODES, LON, BLK), np.float32)
    table[:NLON, :, :COLS] = values.reshape(NLON, LON, COLS)
    table = table.reshape(MODES, LON, CHUNKS, CUT).astype(ml_dtypes.bfloat16)
    forward = np.ascontiguousarray(table.transpose(2, 0, 1, 3)).reshape(CHUNKS, MODES, WIDE)
    inverse = np.ascontiguousarray(table.transpose(2, 1, 3, 0)).reshape(CHUNKS, WIDE, MODES)
    return forward, inverse


def expansion():
    fwd = np.zeros((32, TAPS, ROWS, 32), np.float32)
    bwd = np.zeros((64, TAPS, ROWS, 32), np.float32)
    for w in range(TAPS):
        for i in range(ROWS):
            fwd[8 * i + w, w, i] = 1.0
            bwd[8 * (i + w) + 4 - w, w, i] = 1.0
    fwd = fwd.reshape(32, TAPS * 128)
    bwd = bwd.reshape(64, TAPS * 128)
    return fwd.astype(ml_dtypes.bfloat16), bwd.astype(ml_dtypes.bfloat16)


def dot(a, b):
    return jnp.dot(a, b, preferred_element_type=F32)


def dot_rows(a, b):
    return lax.dot_general(a, b, (((0,), (0,)), ((), ())), preferred_element_type=F32)


def dot_transpose(a, b):
    return lax.dot_general(a, b, (((1,), (1,)), ((), ())), preferred_element_type=F32)


def lanes_of(shape):
    return lax.broadcasted_iota(jnp.int32, shape, 1)


def turn_groups(parts):
    lane = lanes_of(parts[0].shape)
    low = lane < 64
    a, b, c, d = parts
    a, c = jnp.where(low, a, pltpu.roll(c, 64, 1)), jnp.where(low, pltpu.roll(a, 64, 1), c)
    b, d = jnp.where(low, b, pltpu.roll(d, 64, 1)), jnp.where(low, pltpu.roll(b, 64, 1), d)
    even = (lane % 64) < 32
    a, b = jnp.where(even, a, pltpu.roll(b, 32, 1)), jnp.where(even, pltpu.roll(a, 96, 1), b)
    c, d = jnp.where(even, c, pltpu.roll(d, 32, 1)), jnp.where(even, pltpu.roll(c, 96, 1), d)
    return a, b, c, d


def kernel(
    gin_hbm, cot_hbm, filt_hbm, band_hbm, wmix_hbm, gain_hbm, wup_hbm, wdown_hbm, efwd_hbm, ebwd_hbm, fwd_hbm, inv_hbm,
    out, grad, sums,
    fwd, inv, gf, cflat, send, recv, hsend, hrecv, halo, fstage, fown, fhalo, coef, dcoef,
    spec, banded, cf, conv, field, stream, scaled, before, dhid, hidden, dbef, ds, ds16, res, gres,
    gsum, part, csend, crecv, ps, pr, zf, zs, zr, zall, fin,
    gin, cot, filt, band, wmix, gain, wup, wdown, efwd, ebwd,
    isem, osem, ssem, rsem, hssem, hrsem, fssem, frsem, cssem, crsem, pssem, prsem, zssem, zrsem,
):
    lat = lax.axis_index("lat")
    me = lax.axis_index("lon")
    pair = me // 2
    after = lax.rem(lat + 1, LAT)
    ahead = lax.rem(lat + LAT - 1, LAT)
    core = me - 2 * pair
    x = lat // 8
    z_lo = lat // 4 - 2 * x
    y = lat - 8 * x - 4 * z_lo
    z = 2 * pair + z_lo
    mine = pl.multiple_of(core * HALF, HALF)

    plane = 4 * x + y

    def plane_peer(to):
        return {"lat": to // 4 * 8 + z_lo * 4 + (to - to // 4 * 4)}

    def z_peer(to):
        return {"lat": x * 8 + (to - to // 2 * 2) * 4 + y, "lon": to // 2 * 2 + core}

    inputs = (
        (gin_hbm, gin), (filt_hbm, filt), (efwd_hbm, efwd), (cot_hbm, cot), (wdown_hbm, wdown), (fwd_hbm, fwd),
        (inv_hbm, inv), (ebwd_hbm, ebwd), (wmix_hbm, wmix), (gain_hbm, gain), (wup_hbm, wup), (band_hbm, band),
    )
    gets = [pltpu.make_async_copy(src, dst, isem.at[k]) for k, (src, dst) in enumerate(inputs)]
    gets[0].start()

    barrier = pltpu.get_barrier_semaphore()
    for s in range(1, LON):
        pl.semaphore_signal(barrier, inc=1, device_id={"lon": lax.rem(me + s, LON)}, device_id_type=MESH)
    for there in (after, ahead):
        pl.semaphore_signal(barrier, inc=1, device_id={"lat": there}, device_id_type=MESH)
    for s in range(1, PLANE):
        there = plane_peer(lax.rem(plane + s, PLANE))
        pl.semaphore_signal(barrier, inc=1, device_id=there, device_id_type=MESH)
    for s in range(1, 8):
        pl.semaphore_signal(barrier, inc=1, device_id=z_peer(lax.rem(z + s, 8)), device_id_type=MESH)

    for get in gets[1:]:
        get.start()

    def exchange(ph, c, to, own):
        return pltpu.make_async_remote_copy(
            src_ref=send.at[ph, c, to], dst_ref=recv.at[ph, c, own],
            send_sem=ssem.at[ph], recv_sem=rsem.at[ph, c],
            device_id={"lon": to}, device_id_type=MESH,
        )

    def start_exchange(ph, c):
        for s in (4, 3, 5, 2, 6, 7, 1):
            exchange(ph, c, lax.rem(me + s, LON), me).start()
        recv[ph, c, me] = send[ph, c, me]

    def all_of(ref, sem):
        return pltpu.make_async_remote_copy(
            src_ref=ref, dst_ref=ref, send_sem=sem, recv_sem=sem,
            device_id={"lon": lax.rem(me + 1, LON)}, device_id_type=MESH,
        )

    def arrived(ph, c):
        all_of(recv.at[ph, c, pl.ds(0, LON - 1)], rsem.at[ph, c]).wait_recv()

    def halo_copy(hp, side, c):
        return pltpu.make_async_remote_copy(
            src_ref=hsend.at[hp, c, side], dst_ref=hrecv.at[hp, c, side],
            send_sem=hssem.at[hp], recv_sem=hrsem.at[hp, c],
            device_id={"lat": after if side == 0 else ahead}, device_id_type=MESH,
        )

    def filter_copy(side):
        return pltpu.make_async_remote_copy(
            src_ref=fown.at[pl.ds(16 if side == 0 else 0, 16)], dst_ref=fhalo.at[side],
            send_sem=fssem, recv_sem=frsem,
            device_id={"lat": after if side == 0 else ahead}, device_id_type=MESH,
        )

    def pack(src, ph, c):
        for half in range(2):
            parts = [src[half, pl.ds(c * PART + i, CUT, stride=ROWS), :] for i in range(ROWS)]
            for g, block in enumerate(turn_groups(parts)):
                send[ph, c, half * 4 + g] = block.astype(BF16)

    def unpack(ph, c, put):
        for half in range(2):
            parts = [recv[ph, c, half * 4 + g].astype(F32) for g in range(4)]
            for i, block in enumerate(turn_groups(parts)):
                put(half, pl.ds(c * PART + i, CUT, stride=ROWS), block)

    def pass_halo(ph, hp, c):
        arrived(ph, c)
        for g in range(PAIRS):
            one = recv[ph, c, 2 * g].astype(F32)
            two = recv[ph, c, 2 * g + 1].astype(F32)
            low = lanes_of(one.shape) < 64
            hsend[hp, c, 0, g] = jnp.where(low, pltpu.roll(one, 64, 1), two).astype(BF16)
            hsend[hp, c, 1, g] = jnp.where(low, one, pltpu.roll(two, 64, 1)).astype(BF16)
        halo_copy(hp, 0, c).start()
        halo_copy(hp, 1, c).start()

    def to_modes(ph, hp, c):
        all_of(hrecv.at[hp, c], hrsem.at[hp, c]).wait_recv()
        for g in range(PAIRS):
            one = hrecv[hp, c, 0, g].astype(F32)
            two = hrecv[hp, c, 1, g].astype(F32)
            low = lanes_of(one.shape) < 64
            halo[c, 2 * g] = jnp.where(low, one, pltpu.roll(two, 64, 1)).astype(BF16)
            halo[c, 2 * g + 1] = jnp.where(low, pltpu.roll(one, 64, 1), two).astype(BF16)

        @pl.loop(0, MODES // 512)
        def _(step):
            at = pl.ds(pl.multiple_of(step * 512, 512), 512)
            both = jnp.concatenate(
                [recv[ph, c].reshape(WIDE, 128), halo[c].reshape(WIDE, 128)], axis=1
            )
            term = dot(fwd[c, at, :], both)
            spec[at, :] = term if c == 0 else spec[at, :] + term

    def band_sum(weights, first, last):
        @pl.loop(first, last)
        def _(step):
            at = pl.ds(pl.multiple_of(step * 128, 128), 128)
            own = spec[at, 0:128]
            edge = spec[at, 128:256]
            lane = lanes_of(own.shape)
            half = pltpu.roll(own, 64, 1)
            windows = (
                jnp.where(lane < 64, edge, half),
                jnp.where(lane < 32, pltpu.roll(edge, 96, 1), pltpu.roll(own, 32, 1)),
                own,
                jnp.where(lane >= 96, pltpu.roll(edge, 32, 1), pltpu.roll(own, 96, 1)),
                jnp.where(lane >= 64, edge, half),
            )
            total = windows[0] * weights[at, 0:128]
            for w in range(1, TAPS):
                total = total + windows[w] * weights[at, w * 128 : w * 128 + 128]
            banded[at, :] = total.astype(BF16)

    def to_grid(ph, c):
        block = dot(inv[c], banded[...]).astype(BF16)
        for q in range(LON):
            send[ph, c, q] = block[q * CUT : q * CUT + CUT]

    theirs = pl.multiple_of((1 - core) * HALF, HALF)
    other_core = {"lon": me + 1 - 2 * core}
    gain_rows = pl.ds(GAIN_AT, TILE)

    def core_copy(kind):
        rows = pl.ds(0, TILE + DOWN_AT) if kind == 0 else pl.ds(TILE + DOWN_AT, HALF - DOWN_AT)
        return pltpu.make_async_remote_copy(
            src_ref=csend.at[rows], dst_ref=crecv.at[rows], send_sem=cssem.at[kind], recv_sem=crsem.at[kind],
            device_id=other_core, device_id_type=MESH,
        )

    def core_gather(k):
        rows = pl.ds(mine + k * SHARE, SHARE)
        return pltpu.make_async_remote_copy(
            src_ref=fin.at[rows], dst_ref=fin.at[rows], send_sem=cssem.at[2], recv_sem=crsem.at[2],
            device_id=other_core, device_id_type=MESH,
        )

    def plane_scatter(to):
        return pltpu.make_async_remote_copy(
            src_ref=ps.at[to], dst_ref=pr.at[plane], send_sem=pssem.at[0], recv_sem=prsem.at[0],
            device_id=plane_peer(to), device_id_type=MESH,
        )

    def plane_gather(s):
        return pltpu.make_async_remote_copy(
            src_ref=zall.at[pl.ds(0, SHARE)], dst_ref=fin.at[pl.ds(mine + plane * SHARE, SHARE)],
            send_sem=pssem.at[1], recv_sem=prsem.at[1 + (PLANE - s - 1) // GROUP],
            device_id=plane_peer(lax.rem(plane + s, PLANE)), device_id_type=MESH,
        )

    def z_copy(kind, to):
        src, dst = (
            (zs.at[pl.ds(to * Z_ROWS, Z_ROWS)], zr.at[z]),
            (zall.at[pl.ds(z * Z_ROWS, Z_ROWS)], zall.at[pl.ds(z * Z_ROWS, Z_ROWS)]),
        )[kind]
        return pltpu.make_async_remote_copy(
            src_ref=src, dst_ref=dst, send_sem=zssem.at[kind], recv_sem=zrsem.at[kind],
            device_id=z_peer(to), device_id_type=MESH,
        )

    def z_start(kind):
        for s in range(1, 8):
            z_copy(kind, lax.rem(z + s, 8)).start()

    def others(ref, here, count, rows):
        total = ref[lax.rem(here + 1, count), rows, :].astype(F32)
        for s in range(2, count):
            total = total + ref[lax.rem(here + s, count), rows, :].astype(F32)
        return total

    def send_half(first, last):
        @pl.loop(first // 256, last // 256)
        def _(step):
            csend[pl.ds(TILE + step * 256, 256), :] = part[pl.ds(theirs + step * 256, 256), :].astype(BF16)

    def scatter_plane(half):
        core_copy(half).wait_recv()
        if half == 0:
            part[gain_rows, :] += crecv[0:TILE, :].astype(F32)
        g16 = part[gain_rows, :].astype(BF16)

        @pl.loop(half * 8, half * 8 + 8)
        def _(to):
            rows = pl.ds(mine + to * SHARE, SHARE)
            v = part[rows, :] + crecv[pl.ds(TILE + to * SHARE, SHARE), :].astype(F32)
            part[rows, :] = v
            ps[to, 0:SHARE, :] = v.astype(BF16)
            ps[to, SHARE:, :] = g16

        for s in range(8):
            to = half * 8 + lax.rem(plane + s, 8)

            @pl.when(to != plane)
            def _():
                plane_scatter(to).start()

    def scatter_z():
        all_of(pr.at[pl.ds(0, PLANE - 1)], prsem.at[0]).wait_recv()
        zf[SHARE + TILE :, :] = jnp.zeros((8 * Z_ROWS - SHARE - TILE, 128), F32)
        zf[0:SHARE, :] = part[pl.ds(mine + plane * SHARE, SHARE), :] + others(pr, plane, PLANE, pl.ds(0, SHARE))
        zf[SHARE : SHARE + TILE, :] = part[gain_rows, :] + others(pr, plane, PLANE, pl.ds(SHARE, TILE))
        zs[...] = zf[...].astype(BF16)
        z_start(0)

    def gather_z():
        all_of(zr.at[pl.ds(0, 7)], zrsem.at[0]).wait_recv()
        rows = pl.ds(pl.multiple_of(z * Z_ROWS, Z_ROWS), Z_ROWS)
        zall[rows, :] = (zf[rows, :] + others(zr, z, 8, pl.ds(0, Z_ROWS))).astype(BF16)
        z_start(1)

    def gather_plane():
        all_of(zall.at[pl.ds(0, 7 * Z_ROWS)], zrsem.at[1]).wait_recv()
        for s in range(1, PLANE):
            plane_gather(s).start()
        fin[pl.ds(mine + plane * SHARE, SHARE), :] = zall[0:SHARE, :]
        core_gather(plane).start()

    def gather_core():
        for group in range((PLANE - 1) // GROUP):
            all_of(fin.at[pl.ds(0, GROUP * SHARE)], prsem.at[1 + group]).wait_recv()
            for s in range(1 + group * GROUP, 1 + (group + 1) * GROUP):
                core_gather(lax.rem(plane + s, PLANE)).start()

    gets[0].wait()
    for half in range(2):
        gf[half, ROWS * COLS :, :] = jnp.zeros((FLAT - ROWS * COLS, 128), F32)
    for c in range(CHUNKS):
        count = min(CUT, COLS - c * CUT)
        rows = gin[c * CUT : c * CUT + count].astype(F32).reshape(ROWS * count, CH)
        for half in range(2):
            gf[half, c * PART : c * PART + ROWS * count, :] = rows[:, half * 128 : half * 128 + 128]
    pack(gf, 0, 0)
    pl.semaphore_wait(barrier, LON - 1 + 2 + PLANE - 1 + 7)
    start_exchange(0, 0)
    for c in range(1, CHUNKS):
        pack(gf, 0, c)
        start_exchange(0, c)

    gets[1].wait()
    gets[2].wait()
    gets[11].wait()
    fstage[...] = jnp.zeros_like(fstage)
    row = lax.broadcasted_iota(jnp.int32, (ROWS, NLON), 0)
    mode = lax.broadcasted_iota(jnp.int32, (ROWS, NLON), 1)
    scale = jnp.where(mode == 0, 1.0 / NLON, 2.0 / NLON)
    reach = jnp.where(row == 0, band[0], jnp.where(row == 1, band[1], jnp.where(row == 2, band[2], band[3])))
    for t in range(TAPS):
        at = lat * ROWS + row + (t - 2)
        keep = (reach >= abs(t - 2)) & (at >= 0) & (at < LAT * ROWS)
        kept = jnp.where(keep, filt[t] * scale, 0.0)
        for i in range(ROWS):
            fstage[8 * i + t : 8 * i + t + 1, 0:NLON] = kept[i : i + 1, :]
    fown[...] = fstage[...].astype(BF16)
    filter_copy(0).start()
    filter_copy(1).start()

    @pl.loop(0, MODES // 256)
    def _(step):
        at = pl.ds(pl.multiple_of(step * 256, 256), 256)
        coef[at, :] = dot_rows(fown[:, at], efwd[...])

    gets[3].wait()
    gets[4].wait()
    cflat[ROWS * COLS :, :] = jnp.zeros((FLAT - ROWS * COLS, CH), BF16)
    cflat[0 : ROWS * COLS, :] = cot[...].reshape(ROWS * COLS, CH)
    dhid[...] = dot_transpose(cflat[...], wdown[...])
    gsum[...] = jnp.zeros_like(gsum)

    for c in range(CHUNKS):
        pass_halo(0, 0, c)
    gets[5].wait()
    for c in range(CHUNKS):
        to_modes(0, 0, c)
    band_sum(coef, 0, MODES // 128)
    gets[6].wait()
    for c in range(CHUNKS):
        to_grid(1, c)
        start_exchange(1, c)

    for get in gets[7:11]:
        get.wait()
    all_of(fhalo, fssem).wait_send()
    all_of(fhalo, frsem).wait_recv()

    @pl.loop(0, MODES // 256)
    def _(step):
        at = pl.ds(pl.multiple_of(step * 256, 256), 256)
        rows = jnp.concatenate([fhalo[0, :, at], fown[:, at], fhalo[1, :, at]], axis=0)
        dcoef[at, :] = dot_rows(rows, ebwd[...])

    def put_conv(half, rows, block):
        cf[half, rows, :] = block

    def tail(c):
        arrived(1, c)
        unpack(1, c, put_conv)
        all_rows = pl.ds(c * PART, PART)
        conv[all_rows, :] = jnp.concatenate([cf[0, all_rows, :], cf[1, all_rows, :]], axis=1).astype(BF16)
        field[all_rows, :] = dot(conv[all_rows, :], wmix[...])

        @pl.loop(0, PART // 128)
        def _(step):
            at = pl.ds(c * PART + step * 128, 128)
            mixed = field[at, :] + jnp.concatenate([gf[0, at, :], gf[1, at, :]], axis=1)
            s16 = mixed.astype(BF16)
            stream[at, :] = s16
            sf = s16.astype(F32)
            inverse = lax.rsqrt(jnp.mean(sf * sf, axis=-1, keepdims=True) + 1e-06)
            scaled[at, :] = (sf * inverse * gain[...]).astype(BF16)

        before[all_rows, :] = dot(scaled[all_rows, :], wup[...])

        @pl.loop(0, PART // 16)
        def _(step):
            at = pl.ds(c * PART + step * 16, 16)
            u = before[at, :]
            u2 = u * u
            tangent = jnp.tanh(u * (SQRT_TWO_PI + (SQRT_TWO_PI * CUBIC) * u2))
            e = 0.5 * tangent + 0.5
            value = u * e
            hidden[at, :] = value.astype(BF16)
            slope = e + value * (1.0 - e) * (2.0 * SQRT_TWO_PI + (6.0 * SQRT_TWO_PI * CUBIC) * u2)
            dbef[at, :] = (dhid[at, :] * slope).astype(BF16)

        field[all_rows, :] = dot_transpose(dbef[all_rows, :], wup[...])

        @pl.loop(0, PART // 128)
        def _(step):
            at = pl.ds(c * PART + step * 128, 128)
            sf = stream[at, :].astype(F32)
            inverse = lax.rsqrt(jnp.mean(sf * sf, axis=-1, keepdims=True) + 1e-06)
            normed = sf * inverse
            d_scaled = field[at, :]
            gsum[...] += jnp.sum((d_scaled * normed).reshape(16, 8, CH), axis=0)
            gained = d_scaled * gain[...]
            value = cflat[at, :].astype(F32) + inverse * (
                gained - normed * jnp.mean(gained * normed, axis=-1, keepdims=True)
            )
            for half in range(2):
                ds[half, at, :] = value[:, half * 128 : half * 128 + 128]
            ds16[at, :] = value.astype(BF16)

        d_conv = dot_transpose(ds16[all_rows, :], wmix[...])
        for half in range(2):
            cf[half, all_rows, :] = d_conv[:, half * 128 : half * 128 + 128]
        pack(cf, 2, c)
        start_exchange(2, c)

    for c in range(CHUNKS):
        tail(c)

    term = dot_rows(conv[...], ds16[...])
    for h in range(2):
        part[h * HALF : h * HALF + UP_AT, :] = term[:, h * 128 : h * 128 + 128]
    term = dot_rows(scaled[...], dbef[...])
    for h in range(8):
        at = h // 4 * HALF + UP_AT + h % 4 * 256
        part[at : at + 256, :] = term[:, h * 128 : h * 128 + 128]
    part[gain_rows, :] = jnp.zeros((TILE, 128), F32)
    total = jnp.sum(gsum[...], axis=0, keepdims=True)
    for h in range(2):
        part[GAIN_AT + h : GAIN_AT + h + 1, :] = total[:, h * 128 : h * 128 + 128]
    csend[0:TILE, :] = part[gain_rows, :].astype(BF16)
    send_half(0, DOWN_AT)
    core_copy(0).start()
    term = dot_rows(hidden[...], cflat[...])
    for h in range(2):
        part[h * HALF + DOWN_AT : (h + 1) * HALF, :] = term[:, h * 128 : h * 128 + 128]
    send_half(DOWN_AT, HALF)
    core_copy(1).start()
    scatter_plane(0)
    scatter_plane(1)
    result = stream[...].astype(F32) + dot(hidden[...], wdown[...])
    res[...] = result[0 : ROWS * COLS].reshape(COLS, ROWS, CH).astype(BF16)
    put_out = pltpu.make_async_copy(res, out, osem.at[0])
    put_out.start()

    for c in range(CHUNKS):
        pass_halo(2, 1, c)
    scatter_z()
    for c in range(CHUNKS):
        to_modes(2, 1, c)
    gather_z()
    band_sum(dcoef, 0, MODES // 128)
    for c in range(CHUNKS):
        to_grid(3, c)
        start_exchange(3, c)

    def put_grad(half, rows, block):
        ds[half, rows, :] = block + ds[half, rows, :]

    gather_plane()
    for c in range(CHUNKS):
        arrived(3, c)
        unpack(3, c, put_grad)
        count = min(CUT, COLS - c * CUT)
        rows = pl.ds(c * PART, ROWS * count)
        both = jnp.concatenate([ds[0, rows, :], ds[1, rows, :]], axis=1)
        gres[c * CUT : c * CUT + count] = both.reshape(count, ROWS, CH).astype(BF16)
    put_grad_out = pltpu.make_async_copy(gres, grad, osem.at[1])
    put_grad_out.start()
    gather_core()
    put_gain = pltpu.make_async_copy(zall.at[pl.ds(SHARE, TILE)], sums.at[pl.ds(GAIN_AT, TILE)], osem.at[2])
    put_own = pltpu.make_async_copy(fin.at[pl.ds(mine, HALF)], sums.at[pl.ds(mine, HALF)], osem.at[3])
    put_other = pltpu.make_async_copy(fin.at[pl.ds(theirs, HALF)], sums.at[pl.ds(theirs, HALF)], osem.at[4])
    put_gain.start()
    put_own.start()
    all_of(fin.at[pl.ds(0, HALF)], crsem.at[2]).wait_recv()
    put_other.start()

    core_copy(0).wait_send()
    core_copy(1).wait_send()
    all_of(fin.at[pl.ds(0, HALF)], cssem.at[2]).wait_send()
    all_of(ps.at[pl.ds(0, PLANE - 1)], pssem.at[0]).wait_send()
    all_of(fin.at[pl.ds(0, (PLANE - 1) * SHARE)], pssem.at[1]).wait_send()
    for kind in range(2):
        all_of(zs.at[pl.ds(0, 7 * Z_ROWS)], zssem.at[kind]).wait_send()
    for ph in range(4):
        all_of(send.at[ph, :, pl.ds(0, LON - 1)], ssem.at[ph]).wait_send()
    for hp in range(2):
        all_of(hsend.at[hp], hssem.at[hp]).wait_send()
    put_out.wait()
    put_grad_out.wait()
    put_gain.wait()
    put_own.wait()
    put_other.wait()


def finish(res, gres, sums, out, grad, mix_o, gain_o, up_o, down_o, first, second, half, mix, gain, up, down, sem):
    fields = [pltpu.make_async_copy(res, first, sem.at[0]), pltpu.make_async_copy(gres, second, sem.at[1])]
    puts = [pltpu.make_async_copy(first, out, sem.at[4]), pltpu.make_async_copy(second, grad, sem.at[5])]
    gets = [
        pltpu.make_async_copy(
            sums.at[pl.ds(h * HALF, HALF + h * TILE)], half.at[pl.ds(h * HALF, HALF + h * TILE)], sem.at[2 + h]
        )
        for h in range(2)
    ]
    for copy in gets + fields:
        copy.start()
    for h in range(2):
        gets[h].wait()
        lanes = slice(h * 128, h * 128 + 128)
        at = h * HALF
        mix[:, lanes] = half[at : at + UP_AT, :].astype(F32) * NORM_SCALE
        for b in range(4):
            start = at + UP_AT + b * 256
            up[:, h * 512 + b * 128 : h * 512 + b * 128 + 128] = half[start : start + 256, :].astype(F32) * NORM_SCALE
        down[:, lanes] = half[at + DOWN_AT : at + HALF, :].astype(F32) * NORM_SCALE
        fields[h].wait()
        puts[h].start()
    for h in range(2):
        gain[:, h * 128 : h * 128 + 128] = half[GAIN_AT : GAIN_AT + TILE, :].astype(F32)[h : h + 1, :] * NORM_SCALE
    for k, (src, dst) in enumerate(((up, up_o), (down, down_o), (mix, mix_o), (gain, gain_o))):
        puts.append(pltpu.make_async_copy(src, dst, sem.at[6 + k]))
        puts[-1].start()
    for copy in puts:
        copy.wait()


def local(grid_in, grid_cotangent, support_filter, band_half, w_mix, norm_gain, w_up, w_down):
    forward, inverse = fourier_tables()
    efwd, ebwd = expansion()
    anywhere = pl.BlockSpec(memory_space=pl.ANY)
    field = jax.ShapeDtypeStruct((COLS, ROWS, CH), BF16)
    res, gres, sums = pl.pallas_call(
        kernel,
        out_shape=(field, field, jax.ShapeDtypeStruct((2 * HALF + TILE, 128), BF16)),
        in_specs=[anywhere] * 12,
        out_specs=[anywhere] * 3,
        scratch_shapes=[
            pltpu.VMEM((CHUNKS, MODES, WIDE), BF16),
            pltpu.VMEM((CHUNKS, WIDE, MODES), BF16),
            pltpu.VMEM((2, FLAT, 128), F32),
            pltpu.VMEM((FLAT, CH), BF16),
            pltpu.VMEM((4, CHUNKS, LON, CUT, 128), BF16),
            pltpu.VMEM((4, CHUNKS, LON, CUT, 128), BF16),
            pltpu.VMEM((2, CHUNKS, 2, PAIRS, CUT, 128), BF16),
            pltpu.VMEM((2, CHUNKS, 2, PAIRS, CUT, 128), BF16),
            pltpu.VMEM((CHUNKS, LON, CUT, 128), BF16),
            pltpu.VMEM((32, MODES), F32),
            pltpu.VMEM((32, MODES), BF16),
            pltpu.VMEM((2, 16, MODES), BF16),
            pltpu.VMEM((MODES, TAPS * 128), F32),
            pltpu.VMEM((MODES, TAPS * 128), F32),
            pltpu.VMEM((MODES, 256), F32),
            pltpu.VMEM((MODES, 128), BF16),
            pltpu.VMEM((2, FLAT, 128), F32),
            pltpu.VMEM((FLAT, CH), BF16),
            pltpu.VMEM((FLAT, CH), F32),
            pltpu.VMEM((FLAT, CH), BF16),
            pltpu.VMEM((FLAT, CH), BF16),
            pltpu.VMEM((FLAT, HID), F32),
            pltpu.VMEM((FLAT, HID), F32),
            pltpu.VMEM((FLAT, HID), BF16),
            pltpu.VMEM((FLAT, HID), BF16),
            pltpu.VMEM((2, FLAT, 128), F32),
            pltpu.VMEM((FLAT, CH), BF16),
            pltpu.VMEM((COLS, ROWS, CH), BF16),
            pltpu.VMEM((COLS, ROWS, CH), BF16),
            pltpu.VMEM((8, CH), F32),
            pltpu.VMEM((2 * HALF + TILE, 128), F32),
            pltpu.VMEM((HALF + TILE, 128), BF16),
            pltpu.VMEM((HALF + TILE, 128), BF16),
            pltpu.VMEM((PLANE, SHARE + TILE, 128), BF16),
            pltpu.VMEM((PLANE, SHARE + TILE, 128), BF16),
            pltpu.VMEM((8 * Z_ROWS, 128), F32),
            pltpu.VMEM((8 * Z_ROWS, 128), BF16),
            pltpu.VMEM((8, Z_ROWS, 128), BF16),
            pltpu.VMEM((8 * Z_ROWS, 128), BF16),
            pltpu.VMEM((2 * HALF, 128), BF16),
            pltpu.VMEM((COLS, ROWS, CH), BF16),
            pltpu.VMEM((COLS, ROWS, CH), BF16),
            pltpu.VMEM((TAPS, ROWS, NLON), F32),
            pltpu.SMEM((ROWS,), jnp.int32),
            pltpu.VMEM((CH, CH), BF16),
            pltpu.VMEM((1, CH), F32),
            pltpu.VMEM((CH, HID), BF16),
            pltpu.VMEM((HID, CH), BF16),
            pltpu.VMEM((32, TAPS * 128), BF16),
            pltpu.VMEM((64, TAPS * 128), BF16),
            pltpu.SemaphoreType.DMA((12,)),
            pltpu.SemaphoreType.DMA((5,)),
            pltpu.SemaphoreType.DMA((4,)),
            pltpu.SemaphoreType.DMA((4, CHUNKS)),
            pltpu.SemaphoreType.DMA((2,)),
            pltpu.SemaphoreType.DMA((2, CHUNKS)),
            pltpu.SemaphoreType.DMA,
            pltpu.SemaphoreType.DMA,
            pltpu.SemaphoreType.DMA((3,)),
            pltpu.SemaphoreType.DMA((3,)),
            pltpu.SemaphoreType.DMA((2,)),
            pltpu.SemaphoreType.DMA((1 + (PLANE - 1) // GROUP,)),
            pltpu.SemaphoreType.DMA((2,)),
            pltpu.SemaphoreType.DMA((2,)),
        ],
        compiler_params=pltpu.CompilerParams(
            collective_id=0, has_side_effects=True, vmem_limit_bytes=60 * 1024 * 1024
        ),
        cost_estimate=pl.CostEstimate(flops=4_700_000_000, bytes_accessed=14_000_000, transcendentals=800_000),
    )(
        jnp.transpose(grid_in, (1, 0, 2)), jnp.transpose(grid_cotangent, (1, 0, 2)),
        jnp.transpose(support_filter, (1, 0, 2)), band_half, w_mix, norm_gain.reshape(1, CH), w_up, w_down,
        jnp.asarray(efwd), jnp.asarray(ebwd), jnp.asarray(forward), jnp.asarray(inverse),
    )
    grid_out, grid_grad, mix_grad, gain_grad, up_grad, down_grad = pl.pallas_call(
        finish,
        out_shape=(
            field,
            field,
            jax.ShapeDtypeStruct((CH, CH), F32),
            jax.ShapeDtypeStruct((1, CH), F32),
            jax.ShapeDtypeStruct((CH, HID), F32),
            jax.ShapeDtypeStruct((HID, CH), F32),
        ),
        in_specs=[anywhere] * 3,
        out_specs=[anywhere] * 6,
        scratch_shapes=[
            pltpu.VMEM((COLS, ROWS, CH), BF16),
            pltpu.VMEM((COLS, ROWS, CH), BF16),
            pltpu.VMEM((2 * HALF + TILE, 128), BF16),
            pltpu.VMEM((CH, CH), F32),
            pltpu.VMEM((1, CH), F32),
            pltpu.VMEM((CH, HID), F32),
            pltpu.VMEM((HID, CH), F32),
            pltpu.SemaphoreType.DMA((10,)),
        ],
        compiler_params=pltpu.CompilerParams(vmem_limit_bytes=60 * 1024 * 1024),
    )(res, gres, sums)
    return (
        jnp.transpose(grid_out, (1, 0, 2)),
        jnp.transpose(grid_grad, (1, 0, 2)),
        mix_grad,
        gain_grad.reshape(CH),
        up_grad,
        down_grad,
    )


def solution(mesh):
    return jax.shard_map(
        local,
        mesh=mesh,
        in_specs=(
            P("lat", "lon", None),
            P("lat", "lon", None),
            P("lat", None, None),
            P("lat"),
            P(),
            P(),
            P(),
            P(),
        ),
        out_specs=(P("lat", "lon", None), P("lat", "lon", None), P(), P(), P(), P()),
        check_vma=False,
    )
```

```python
import jax
import jax.numpy as jnp
import ml_dtypes
import numpy as np
from jax import lax
from jax.experimental import pallas as pl
from jax.experimental.pallas import tpu as pltpu
from jax.sharding import PartitionSpec as P

SQRT_TWO_PI = 0.7978845608028654
CUBIC = 0.044715
MESH = pl.DeviceIdType.MESH
BF16 = jnp.bfloat16
F32 = jnp.float32

LAT = 32
LON = 8
PAIRS = LON // 2
ROWS = 4
COLS = 180
CUT = 64
CHUNKS = 3
BLK = CUT * CHUNKS
NLON = LON * COLS
MODES = LON * BLK
WIDE = LON * CUT
CH = 256
HID = 1024
TAPS = 5
FLAT = ROWS * BLK
PART = ROWS * CUT
BAND_STEP = 512
NORM_STEP = 256
GELU_STEP = 32

HALF = 2304
UP_AT, DOWN_AT = 256, 1280
GAIN_AT = 2 * HALF
PLANE = 16
SHARE = HALF // PLANE
GROUP = 5
TILE = 16
Z_ROWS = 32
NORM_SCALE = float(LAT * ROWS * NLON) ** (-0.5)


def fourier_tables():
    modes = np.arange(NLON)
    freq = np.where(modes < NLON // 2, modes, modes - NLON // 2)
    phase = (freq[:, None] * modes[None, :]) % NLON
    angle = phase * (2.0 * np.pi / NLON)
    values = np.where((modes < NLON // 2)[:, None], np.cos(angle), np.sin(angle))
    table = np.zeros((MODES, LON, BLK), np.float32)
    table[:NLON, :, :COLS] = values.reshape(NLON, LON, COLS)
    table = table.reshape(MODES, LON, CHUNKS, CUT).astype(ml_dtypes.bfloat16)
    forward = np.ascontiguousarray(table.transpose(2, 0, 1, 3)).reshape(CHUNKS, MODES, WIDE)
    inverse = np.ascontiguousarray(table.transpose(2, 1, 3, 0)).reshape(CHUNKS, WIDE, MODES)
    return forward, inverse


def expansion():
    fwd = np.zeros((32, TAPS, ROWS, 32), np.float32)
    bwd = np.zeros((64, TAPS, ROWS, 32), np.float32)
    for w in range(TAPS):
        for i in range(ROWS):
            fwd[8 * i + w, w, i] = 1.0
            bwd[8 * (i + w) + 4 - w, w, i] = 1.0
    fwd = fwd.reshape(32, TAPS * 128)
    bwd = bwd.reshape(64, TAPS * 128)
    return fwd.astype(ml_dtypes.bfloat16), bwd.astype(ml_dtypes.bfloat16)


def dot(a, b):
    return jnp.dot(a, b, preferred_element_type=F32)


def dot_rows(a, b):
    return lax.dot_general(a, b, (((0,), (0,)), ((), ())), preferred_element_type=F32)


def dot_transpose(a, b):
    return lax.dot_general(a, b, (((1,), (1,)), ((), ())), preferred_element_type=F32)


def lanes_of(shape):
    return lax.broadcasted_iota(jnp.int32, shape, 1)


def turn_groups(parts):
    lane = lanes_of(parts[0].shape)
    low = lane < 64
    a, b, c, d = parts
    a, c = jnp.where(low, a, pltpu.roll(c, 64, 1)), jnp.where(low, pltpu.roll(a, 64, 1), c)
    b, d = jnp.where(low, b, pltpu.roll(d, 64, 1)), jnp.where(low, pltpu.roll(b, 64, 1), d)
    even = (lane % 64) < 32
    a, b = jnp.where(even, a, pltpu.roll(b, 32, 1)), jnp.where(even, pltpu.roll(a, 96, 1), b)
    c, d = jnp.where(even, c, pltpu.roll(d, 32, 1)), jnp.where(even, pltpu.roll(c, 96, 1), d)
    return a, b, c, d


def kernel(
    gin_hbm, cot_hbm, filt_hbm, band_hbm, wmix_hbm, gain_hbm, wup_hbm, wdown_hbm, efwd_hbm, ebwd_hbm, fwd_hbm, inv_hbm,
    out, grad, sums,
    fwd, inv, gf, cflat, send, recv, hsend, hrecv, halo, fstage, fown, fhalo, coef, dcoef,
    spec, banded, cf, conv, field, stream, scaled, before, dhid, hidden, dbef, ds, ds16, res, gres,
    gsum, part, csend, crecv, ps, pr, zf, zs, zr, zall, fin,
    gin, cot, filt, band, wmix, gain, wup, wdown, efwd, ebwd,
    isem, osem, ssem, rsem, hssem, hrsem, fssem, frsem, cssem, crsem, pssem, prsem, zssem, zrsem,
):
    lat = lax.axis_index("lat")
    me = lax.axis_index("lon")
    pair = me // 2
    after = lax.rem(lat + 1, LAT)
    ahead = lax.rem(lat + LAT - 1, LAT)
    core = me - 2 * pair
    x = lat // 8
    z_lo = lat // 4 - 2 * x
    y = lat - 8 * x - 4 * z_lo
    z = 2 * pair + z_lo
    mine = pl.multiple_of(core * HALF, HALF)

    plane = 4 * x + y

    def plane_peer(to):
        return {"lat": to // 4 * 8 + z_lo * 4 + (to - to // 4 * 4)}

    def z_peer(to):
        return {"lat": x * 8 + (to - to // 2 * 2) * 4 + y, "lon": to // 2 * 2 + core}

    inputs = (
        (gin_hbm, gin), (filt_hbm, filt), (efwd_hbm, efwd), (cot_hbm, cot), (wdown_hbm, wdown), (fwd_hbm, fwd),
        (inv_hbm, inv), (ebwd_hbm, ebwd), (wmix_hbm, wmix), (gain_hbm, gain), (wup_hbm, wup), (band_hbm, band),
    )
    gets = [pltpu.make_async_copy(src, dst, isem.at[k]) for k, (src, dst) in enumerate(inputs)]
    gets[0].start()

    barrier = pltpu.get_barrier_semaphore()
    for s in range(1, LON):
        pl.semaphore_signal(barrier, inc=1, device_id={"lon": lax.rem(me + s, LON)}, device_id_type=MESH)
    for there in (after, ahead):
        pl.semaphore_signal(barrier, inc=1, device_id={"lat": there}, device_id_type=MESH)
    for s in range(1, PLANE):
        there = plane_peer(lax.rem(plane + s, PLANE))
        pl.semaphore_signal(barrier, inc=1, device_id=there, device_id_type=MESH)
    for s in range(1, 8):
        pl.semaphore_signal(barrier, inc=1, device_id=z_peer(lax.rem(z + s, 8)), device_id_type=MESH)

    for get in gets[1:]:
        get.start()

    def exchange(ph, c, to, own):
        return pltpu.make_async_remote_copy(
            src_ref=send.at[ph, c, to], dst_ref=recv.at[ph, c, own],
            send_sem=ssem.at[ph], recv_sem=rsem.at[ph, c],
            device_id={"lon": to}, device_id_type=MESH,
        )

    def start_exchange(ph, c):
        for s in (4, 3, 5, 2, 6, 7, 1):
            exchange(ph, c, lax.rem(me + s, LON), me).start()
        recv[ph, c, me] = send[ph, c, me]

    def all_of(ref, sem):
        return pltpu.make_async_remote_copy(
            src_ref=ref, dst_ref=ref, send_sem=sem, recv_sem=sem,
            device_id={"lon": lax.rem(me + 1, LON)}, device_id_type=MESH,
        )

    def arrived(ph, c):
        all_of(recv.at[ph, c, pl.ds(0, LON - 1)], rsem.at[ph, c]).wait_recv()

    def halo_copy(hp, side, c):
        return pltpu.make_async_remote_copy(
            src_ref=hsend.at[hp, c, side], dst_ref=hrecv.at[hp, c, side],
            send_sem=hssem.at[hp], recv_sem=hrsem.at[hp, c],
            device_id={"lat": after if side == 0 else ahead}, device_id_type=MESH,
        )

    def filter_copy(side):
        return pltpu.make_async_remote_copy(
            src_ref=fown.at[pl.ds(16 if side == 0 else 0, 16)], dst_ref=fhalo.at[side],
            send_sem=fssem, recv_sem=frsem,
            device_id={"lat": after if side == 0 else ahead}, device_id_type=MESH,
        )

    def pack(src, ph, c):
        for half in range(2):
            parts = [src[half, pl.ds(c * PART + i, CUT, stride=ROWS), :] for i in range(ROWS)]
            for g, block in enumerate(turn_groups(parts)):
                send[ph, c, half * 4 + g] = block.astype(BF16)

    def unpack(ph, c, put):
        for half in range(2):
            parts = [recv[ph, c, half * 4 + g].astype(F32) for g in range(4)]
            for i, block in enumerate(turn_groups(parts)):
                put(half, pl.ds(c * PART + i, CUT, stride=ROWS), block)

    def pass_halo(ph, hp, c):
        arrived(ph, c)
        for g in range(PAIRS):
            one = recv[ph, c, 2 * g].astype(F32)
            two = recv[ph, c, 2 * g + 1].astype(F32)
            low = lanes_of(one.shape) < 64
            hsend[hp, c, 0, g] = jnp.where(low, pltpu.roll(one, 64, 1), two).astype(BF16)
            hsend[hp, c, 1, g] = jnp.where(low, one, pltpu.roll(two, 64, 1)).astype(BF16)
        halo_copy(hp, 0, c).start()
        halo_copy(hp, 1, c).start()

    def to_modes(ph, hp, c):
        all_of(hrecv.at[hp, c], hrsem.at[hp, c]).wait_recv()
        for g in range(PAIRS):
            one = hrecv[hp, c, 0, g].astype(F32)
            two = hrecv[hp, c, 1, g].astype(F32)
            low = lanes_of(one.shape) < 64
            halo[c, 2 * g] = jnp.where(low, one, pltpu.roll(two, 64, 1)).astype(BF16)
            halo[c, 2 * g + 1] = jnp.where(low, pltpu.roll(one, 64, 1), two).astype(BF16)

        @pl.loop(0, MODES // 512)
        def _(step):
            at = pl.ds(pl.multiple_of(step * 512, 512), 512)
            both = jnp.concatenate(
                [recv[ph, c].reshape(WIDE, 128), halo[c].reshape(WIDE, 128)], axis=1
            )
            term = dot(fwd[c, at, :], both)
            spec[at, :] = term if c == 0 else spec[at, :] + term

    def band_sum(weights):
        @pl.loop(0, MODES // BAND_STEP)
        def _(step):
            at = pl.ds(pl.multiple_of(step * BAND_STEP, BAND_STEP), BAND_STEP)
            own = spec[at, 0:128]
            edge = spec[at, 128:256]
            lane = lanes_of(own.shape)
            half = pltpu.roll(own, 64, 1)
            windows = (
                jnp.where(lane < 64, edge, half),
                jnp.where(lane < 32, pltpu.roll(edge, 96, 1), pltpu.roll(own, 32, 1)),
                own,
                jnp.where(lane >= 96, pltpu.roll(edge, 32, 1), pltpu.roll(own, 96, 1)),
                jnp.where(lane >= 64, edge, half),
            )
            total = windows[0] * weights[at, 0:128]
            for w in range(1, TAPS):
                total = total + windows[w] * weights[at, w * 128 : w * 128 + 128]
            banded[at, :] = total.astype(BF16)

    def to_grid(ph, c):
        block = dot(inv[c], banded[...]).astype(BF16)
        for q in range(LON):
            send[ph, c, q] = block[q * CUT : q * CUT + CUT]

    theirs = pl.multiple_of((1 - core) * HALF, HALF)
    other_core = {"lon": me + 1 - 2 * core}
    gain_rows = pl.ds(GAIN_AT, TILE)

    def core_copy(kind):
        rows = pl.ds(0, TILE + DOWN_AT) if kind == 0 else pl.ds(TILE + DOWN_AT, HALF - DOWN_AT)
        return pltpu.make_async_remote_copy(
            src_ref=csend.at[rows], dst_ref=crecv.at[rows], send_sem=cssem.at[kind], recv_sem=crsem.at[kind],
            device_id=other_core, device_id_type=MESH,
        )

    def core_gather(k):
        rows = pl.ds(mine + k * SHARE, SHARE)
        return pltpu.make_async_remote_copy(
            src_ref=fin.at[rows], dst_ref=fin.at[rows], send_sem=cssem.at[2], recv_sem=crsem.at[2],
            device_id=other_core, device_id_type=MESH,
        )

    def plane_scatter(to):
        return pltpu.make_async_remote_copy(
            src_ref=ps.at[to], dst_ref=pr.at[plane], send_sem=pssem.at[0], recv_sem=prsem.at[0],
            device_id=plane_peer(to), device_id_type=MESH,
        )

    def plane_gather(s):
        return pltpu.make_async_remote_copy(
            src_ref=zall.at[pl.ds(0, SHARE)], dst_ref=fin.at[pl.ds(mine + plane * SHARE, SHARE)],
            send_sem=pssem.at[1], recv_sem=prsem.at[1 + (PLANE - s - 1) // GROUP],
            device_id=plane_peer(lax.rem(plane + s, PLANE)), device_id_type=MESH,
        )

    def z_copy(kind, to):
        src, dst = (
            (zs.at[pl.ds(to * Z_ROWS, Z_ROWS)], zr.at[z]),
            (zall.at[pl.ds(z * Z_ROWS, Z_ROWS)], zall.at[pl.ds(z * Z_ROWS, Z_ROWS)]),
        )[kind]
        return pltpu.make_async_remote_copy(
            src_ref=src, dst_ref=dst, send_sem=zssem.at[kind], recv_sem=zrsem.at[kind],
            device_id=z_peer(to), device_id_type=MESH,
        )

    def z_start(kind):
        for s in range(1, 8):
            z_copy(kind, lax.rem(z + s, 8)).start()

    def others(ref, here, count, rows):
        total = ref[lax.rem(here + 1, count), rows, :].astype(F32)
        for s in range(2, count):
            total = total + ref[lax.rem(here + s, count), rows, :].astype(F32)
        return total

    def send_half(first, last):
        @pl.loop(first // 256, last // 256)
        def _(step):
            csend[pl.ds(TILE + step * 256, 256), :] = part[pl.ds(theirs + step * 256, 256), :].astype(BF16)

    def scatter_plane(half):
        core_copy(half).wait_recv()
        if half == 0:
            part[gain_rows, :] += crecv[0:TILE, :].astype(F32)
        g16 = part[gain_rows, :].astype(BF16)

        @pl.loop(half * 8, half * 8 + 8)
        def _(to):
            rows = pl.ds(mine + to * SHARE, SHARE)
            v = part[rows, :] + crecv[pl.ds(TILE + to * SHARE, SHARE), :].astype(F32)
            part[rows, :] = v
            ps[to, 0:SHARE, :] = v.astype(BF16)
            ps[to, SHARE:, :] = g16

        for s in range(8):
            to = half * 8 + lax.rem(plane + s, 8)

            @pl.when(to != plane)
            def _():
                plane_scatter(to).start()

    def scatter_z():
        all_of(pr.at[pl.ds(0, PLANE - 1)], prsem.at[0]).wait_recv()
        zf[SHARE + TILE :, :] = jnp.zeros((8 * Z_ROWS - SHARE - TILE, 128), F32)
        zf[0:SHARE, :] = part[pl.ds(mine + plane * SHARE, SHARE), :] + others(pr, plane, PLANE, pl.ds(0, SHARE))
        zf[SHARE : SHARE + TILE, :] = part[gain_rows, :] + others(pr, plane, PLANE, pl.ds(SHARE, TILE))
        zs[...] = zf[...].astype(BF16)
        z_start(0)

    def gather_z():
        all_of(zr.at[pl.ds(0, 7)], zrsem.at[0]).wait_recv()
        rows = pl.ds(pl.multiple_of(z * Z_ROWS, Z_ROWS), Z_ROWS)
        zall[rows, :] = (zf[rows, :] + others(zr, z, 8, pl.ds(0, Z_ROWS))).astype(BF16)
        z_start(1)

    def gather_plane():
        all_of(zall.at[pl.ds(0, 7 * Z_ROWS)], zrsem.at[1]).wait_recv()
        for s in range(1, PLANE):
            plane_gather(s).start()
        fin[pl.ds(mine + plane * SHARE, SHARE), :] = zall[0:SHARE, :]
        core_gather(plane).start()

    def gather_core():
        for group in range((PLANE - 1) // GROUP):
            all_of(fin.at[pl.ds(0, GROUP * SHARE)], prsem.at[1 + group]).wait_recv()
            for s in range(1 + group * GROUP, 1 + (group + 1) * GROUP):
                core_gather(lax.rem(plane + s, PLANE)).start()

    gets[0].wait()
    for half in range(2):
        gf[half, ROWS * COLS :, :] = jnp.zeros((FLAT - ROWS * COLS, 128), F32)
    for c in range(CHUNKS):
        count = min(CUT, COLS - c * CUT)
        rows = gin[c * CUT : c * CUT + count].astype(F32).reshape(ROWS * count, CH)
        for half in range(2):
            gf[half, c * PART : c * PART + ROWS * count, :] = rows[:, half * 128 : half * 128 + 128]
    pack(gf, 0, 0)
    pl.semaphore_wait(barrier, LON - 1 + 2 + PLANE - 1 + 7)
    start_exchange(0, 0)
    for c in range(1, CHUNKS):
        pack(gf, 0, c)
        start_exchange(0, c)

    gets[1].wait()
    gets[2].wait()
    gets[11].wait()
    fstage[...] = jnp.zeros_like(fstage)
    row = lax.broadcasted_iota(jnp.int32, (ROWS, NLON), 0)
    mode = lax.broadcasted_iota(jnp.int32, (ROWS, NLON), 1)
    scale = jnp.where(mode == 0, 1.0 / NLON, 2.0 / NLON)
    reach = jnp.where(row == 0, band[0], jnp.where(row == 1, band[1], jnp.where(row == 2, band[2], band[3])))
    for t in range(TAPS):
        at = lat * ROWS + row + (t - 2)
        keep = (reach >= abs(t - 2)) & (at >= 0) & (at < LAT * ROWS)
        kept = jnp.where(keep, filt[t] * scale, 0.0)
        for i in range(ROWS):
            fstage[8 * i + t : 8 * i + t + 1, 0:NLON] = kept[i : i + 1, :]
    fown[...] = fstage[...].astype(BF16)
    filter_copy(0).start()
    filter_copy(1).start()

    @pl.loop(0, MODES // 256)
    def _(step):
        at = pl.ds(pl.multiple_of(step * 256, 256), 256)
        coef[at, :] = dot_rows(fown[:, at], efwd[...])

    gets[3].wait()
    gets[4].wait()
    cflat[ROWS * COLS :, :] = jnp.zeros((FLAT - ROWS * COLS, CH), BF16)
    cflat[0 : ROWS * COLS, :] = cot[...].reshape(ROWS * COLS, CH)
    dhid[...] = dot_transpose(cflat[...], wdown[...])
    gsum[...] = jnp.zeros_like(gsum)

    for c in range(CHUNKS):
        pass_halo(0, 0, c)
    gets[5].wait()
    for c in range(CHUNKS):
        to_modes(0, 0, c)
    band_sum(coef)
    gets[6].wait()
    for c in range(CHUNKS):
        to_grid(1, c)
        start_exchange(1, c)

    for get in gets[7:11]:
        get.wait()
    all_of(fhalo, fssem).wait_send()
    all_of(fhalo, frsem).wait_recv()

    @pl.loop(0, MODES // 256)
    def _(step):
        at = pl.ds(pl.multiple_of(step * 256, 256), 256)
        rows = jnp.concatenate([fhalo[0, :, at], fown[:, at], fhalo[1, :, at]], axis=0)
        dcoef[at, :] = dot_rows(rows, ebwd[...])

    def put_conv(half, rows, block):
        cf[half, rows, :] = block

    def tail(c):
        arrived(1, c)
        unpack(1, c, put_conv)
        all_rows = pl.ds(c * PART, PART)
        conv[all_rows, :] = jnp.concatenate([cf[0, all_rows, :], cf[1, all_rows, :]], axis=1).astype(BF16)
        field[all_rows, :] = dot(conv[all_rows, :], wmix[...])

        @pl.loop(0, PART // NORM_STEP)
        def _(step):
            at = pl.ds(c * PART + step * NORM_STEP, NORM_STEP)
            mixed = field[at, :] + jnp.concatenate([gf[0, at, :], gf[1, at, :]], axis=1)
            s16 = mixed.astype(BF16)
            stream[at, :] = s16
            sf = s16.astype(F32)
            inverse = lax.rsqrt(jnp.mean(sf * sf, axis=-1, keepdims=True) + 1e-06)
            scaled[at, :] = (sf * inverse * gain[...]).astype(BF16)

        before[all_rows, :] = dot(scaled[all_rows, :], wup[...])

        @pl.loop(0, PART // GELU_STEP)
        def _(step):
            at = pl.ds(c * PART + step * GELU_STEP, GELU_STEP)
            u = before[at, :]
            u2 = u * u
            tangent = jnp.tanh(u * (SQRT_TWO_PI + (SQRT_TWO_PI * CUBIC) * u2))
            e = 0.5 * tangent + 0.5
            value = u * e
            hidden[at, :] = value.astype(BF16)
            slope = e + value * (1.0 - e) * (2.0 * SQRT_TWO_PI + (6.0 * SQRT_TWO_PI * CUBIC) * u2)
            dbef[at, :] = (dhid[at, :] * slope).astype(BF16)

        field[all_rows, :] = dot_transpose(dbef[all_rows, :], wup[...])

        @pl.loop(0, PART // NORM_STEP)
        def _(step):
            at = pl.ds(c * PART + step * NORM_STEP, NORM_STEP)
            sf = stream[at, :].astype(F32)
            inverse = lax.rsqrt(jnp.mean(sf * sf, axis=-1, keepdims=True) + 1e-06)
            normed = sf * inverse
            d_scaled = field[at, :]
            gsum[...] += jnp.sum((d_scaled * normed).reshape(NORM_STEP // 8, 8, CH), axis=0)
            gained = d_scaled * gain[...]
            value = cflat[at, :].astype(F32) + inverse * (
                gained - normed * jnp.mean(gained * normed, axis=-1, keepdims=True)
            )
            for half in range(2):
                ds[half, at, :] = value[:, half * 128 : half * 128 + 128]
            ds16[at, :] = value.astype(BF16)

        d_conv = dot_transpose(ds16[all_rows, :], wmix[...])
        for half in range(2):
            cf[half, all_rows, :] = d_conv[:, half * 128 : half * 128 + 128]
        pack(cf, 2, c)
        start_exchange(2, c)

    for c in range(CHUNKS):
        tail(c)

    term = dot_rows(conv[...], ds16[...])
    for h in range(2):
        part[h * HALF : h * HALF + UP_AT, :] = term[:, h * 128 : h * 128 + 128]
    term = dot_rows(scaled[...], dbef[...])
    for h in range(8):
        at = h // 4 * HALF + UP_AT + h % 4 * 256
        part[at : at + 256, :] = term[:, h * 128 : h * 128 + 128]
    part[gain_rows, :] = jnp.zeros((TILE, 128), F32)
    total = jnp.sum(gsum[...], axis=0, keepdims=True)
    for h in range(2):
        part[GAIN_AT + h : GAIN_AT + h + 1, :] = total[:, h * 128 : h * 128 + 128]
    csend[0:TILE, :] = part[gain_rows, :].astype(BF16)
    send_half(0, DOWN_AT)
    core_copy(0).start()
    term = dot_rows(hidden[...], cflat[...])
    for h in range(2):
        part[h * HALF + DOWN_AT : (h + 1) * HALF, :] = term[:, h * 128 : h * 128 + 128]
    send_half(DOWN_AT, HALF)
    core_copy(1).start()
    scatter_plane(0)
    scatter_plane(1)
    result = stream[...].astype(F32) + dot(hidden[...], wdown[...])
    res[...] = result[0 : ROWS * COLS].reshape(COLS, ROWS, CH).astype(BF16)
    put_out = pltpu.make_async_copy(res, out, osem.at[0])
    put_out.start()

    for c in range(CHUNKS):
        pass_halo(2, 1, c)
    scatter_z()
    for c in range(CHUNKS):
        to_modes(2, 1, c)
    gather_z()
    band_sum(dcoef)
    for c in range(CHUNKS):
        to_grid(3, c)
        start_exchange(3, c)

    def put_grad(half, rows, block):
        ds[half, rows, :] = block + ds[half, rows, :]

    gather_plane()
    for c in range(CHUNKS):
        arrived(3, c)
        unpack(3, c, put_grad)
        count = min(CUT, COLS - c * CUT)
        rows = pl.ds(c * PART, ROWS * count)
        both = jnp.concatenate([ds[0, rows, :], ds[1, rows, :]], axis=1)
        gres[c * CUT : c * CUT + count] = both.reshape(count, ROWS, CH).astype(BF16)
    put_grad_out = pltpu.make_async_copy(gres, grad, osem.at[1])
    put_grad_out.start()
    gather_core()
    put_gain = pltpu.make_async_copy(zall.at[pl.ds(SHARE, TILE)], sums.at[pl.ds(GAIN_AT, TILE)], osem.at[2])
    put_own = pltpu.make_async_copy(fin.at[pl.ds(mine, HALF)], sums.at[pl.ds(mine, HALF)], osem.at[3])
    put_other = pltpu.make_async_copy(fin.at[pl.ds(theirs, HALF)], sums.at[pl.ds(theirs, HALF)], osem.at[4])
    put_gain.start()
    put_own.start()
    all_of(fin.at[pl.ds(0, HALF)], crsem.at[2]).wait_recv()
    put_other.start()

    core_copy(0).wait_send()
    core_copy(1).wait_send()
    all_of(fin.at[pl.ds(0, HALF)], cssem.at[2]).wait_send()
    all_of(ps.at[pl.ds(0, PLANE - 1)], pssem.at[0]).wait_send()
    all_of(fin.at[pl.ds(0, (PLANE - 1) * SHARE)], pssem.at[1]).wait_send()
    for kind in range(2):
        all_of(zs.at[pl.ds(0, 7 * Z_ROWS)], zssem.at[kind]).wait_send()
    for ph in range(4):
        all_of(send.at[ph, :, pl.ds(0, LON - 1)], ssem.at[ph]).wait_send()
    for hp in range(2):
        all_of(hsend.at[hp], hssem.at[hp]).wait_send()
    put_out.wait()
    put_grad_out.wait()
    put_gain.wait()
    put_own.wait()
    put_other.wait()


def finish(res, gres, sums, out, grad, mix_o, gain_o, up_o, down_o, first, second, half, mix, gain, up, down, sem):
    fields = [pltpu.make_async_copy(res, first, sem.at[0]), pltpu.make_async_copy(gres, second, sem.at[1])]
    puts = [pltpu.make_async_copy(first, out, sem.at[4]), pltpu.make_async_copy(second, grad, sem.at[5])]
    gets = [
        pltpu.make_async_copy(
            sums.at[pl.ds(h * HALF, HALF + h * TILE)], half.at[pl.ds(h * HALF, HALF + h * TILE)], sem.at[2 + h]
        )
        for h in range(2)
    ]
    for copy in gets + fields:
        copy.start()
    for h in range(2):
        gets[h].wait()
        lanes = slice(h * 128, h * 128 + 128)
        at = h * HALF
        mix[:, lanes] = half[at : at + UP_AT, :].astype(F32) * NORM_SCALE
        for b in range(4):
            start = at + UP_AT + b * 256
            up[:, h * 512 + b * 128 : h * 512 + b * 128 + 128] = half[start : start + 256, :].astype(F32) * NORM_SCALE
        down[:, lanes] = half[at + DOWN_AT : at + HALF, :].astype(F32) * NORM_SCALE
        fields[h].wait()
        puts[h].start()
    for h in range(2):
        gain[:, h * 128 : h * 128 + 128] = half[GAIN_AT : GAIN_AT + TILE, :].astype(F32)[h : h + 1, :] * NORM_SCALE
    for k, (src, dst) in enumerate(((up, up_o), (down, down_o), (mix, mix_o), (gain, gain_o))):
        puts.append(pltpu.make_async_copy(src, dst, sem.at[6 + k]))
        puts[-1].start()
    for copy in puts:
        copy.wait()


def local(grid_in, grid_cotangent, support_filter, band_half, w_mix, norm_gain, w_up, w_down):
    forward, inverse = fourier_tables()
    efwd, ebwd = expansion()
    anywhere = pl.BlockSpec(memory_space=pl.ANY)
    field = jax.ShapeDtypeStruct((COLS, ROWS, CH), BF16)
    res, gres, sums = pl.pallas_call(
        kernel,
        out_shape=(field, field, jax.ShapeDtypeStruct((2 * HALF + TILE, 128), BF16)),
        in_specs=[anywhere] * 12,
        out_specs=[anywhere] * 3,
        scratch_shapes=[
            pltpu.VMEM((CHUNKS, MODES, WIDE), BF16),
            pltpu.VMEM((CHUNKS, WIDE, MODES), BF16),
            pltpu.VMEM((2, FLAT, 128), F32),
            pltpu.VMEM((FLAT, CH), BF16),
            pltpu.VMEM((4, CHUNKS, LON, CUT, 128), BF16),
            pltpu.VMEM((4, CHUNKS, LON, CUT, 128), BF16),
            pltpu.VMEM((2, CHUNKS, 2, PAIRS, CUT, 128), BF16),
            pltpu.VMEM((2, CHUNKS, 2, PAIRS, CUT, 128), BF16),
            pltpu.VMEM((CHUNKS, LON, CUT, 128), BF16),
            pltpu.VMEM((32, MODES), F32),
            pltpu.VMEM((32, MODES), BF16),
            pltpu.VMEM((2, 16, MODES), BF16),
            pltpu.VMEM((MODES, TAPS * 128), F32),
            pltpu.VMEM((MODES, TAPS * 128), F32),
            pltpu.VMEM((MODES, 256), F32),
            pltpu.VMEM((MODES, 128), BF16),
            pltpu.VMEM((2, FLAT, 128), F32),
            pltpu.VMEM((FLAT, CH), BF16),
            pltpu.VMEM((FLAT, CH), F32),
            pltpu.VMEM((FLAT, CH), BF16),
            pltpu.VMEM((FLAT, CH), BF16),
            pltpu.VMEM((FLAT, HID), F32),
            pltpu.VMEM((FLAT, HID), F32),
            pltpu.VMEM((FLAT, HID), BF16),
            pltpu.VMEM((FLAT, HID), BF16),
            pltpu.VMEM((2, FLAT, 128), F32),
            pltpu.VMEM((FLAT, CH), BF16),
            pltpu.VMEM((COLS, ROWS, CH), BF16),
            pltpu.VMEM((COLS, ROWS, CH), BF16),
            pltpu.VMEM((8, CH), F32),
            pltpu.VMEM((2 * HALF + TILE, 128), F32),
            pltpu.VMEM((HALF + TILE, 128), BF16),
            pltpu.VMEM((HALF + TILE, 128), BF16),
            pltpu.VMEM((PLANE, SHARE + TILE, 128), BF16),
            pltpu.VMEM((PLANE, SHARE + TILE, 128), BF16),
            pltpu.VMEM((8 * Z_ROWS, 128), F32),
            pltpu.VMEM((8 * Z_ROWS, 128), BF16),
            pltpu.VMEM((8, Z_ROWS, 128), BF16),
            pltpu.VMEM((8 * Z_ROWS, 128), BF16),
            pltpu.VMEM((2 * HALF, 128), BF16),
            pltpu.VMEM((COLS, ROWS, CH), BF16),
            pltpu.VMEM((COLS, ROWS, CH), BF16),
            pltpu.VMEM((TAPS, ROWS, NLON), F32),
            pltpu.SMEM((ROWS,), jnp.int32),
            pltpu.VMEM((CH, CH), BF16),
            pltpu.VMEM((1, CH), F32),
            pltpu.VMEM((CH, HID), BF16),
            pltpu.VMEM((HID, CH), BF16),
            pltpu.VMEM((32, TAPS * 128), BF16),
            pltpu.VMEM((64, TAPS * 128), BF16),
            pltpu.SemaphoreType.DMA((12,)),
            pltpu.SemaphoreType.DMA((5,)),
            pltpu.SemaphoreType.DMA((4,)),
            pltpu.SemaphoreType.DMA((4, CHUNKS)),
            pltpu.SemaphoreType.DMA((2,)),
            pltpu.SemaphoreType.DMA((2, CHUNKS)),
            pltpu.SemaphoreType.DMA,
            pltpu.SemaphoreType.DMA,
            pltpu.SemaphoreType.DMA((3,)),
            pltpu.SemaphoreType.DMA((3,)),
            pltpu.SemaphoreType.DMA((2,)),
            pltpu.SemaphoreType.DMA((1 + (PLANE - 1) // GROUP,)),
            pltpu.SemaphoreType.DMA((2,)),
            pltpu.SemaphoreType.DMA((2,)),
        ],
        compiler_params=pltpu.CompilerParams(
            collective_id=0, has_side_effects=True, vmem_limit_bytes=60 * 1024 * 1024
        ),
        cost_estimate=pl.CostEstimate(flops=4_700_000_000, bytes_accessed=14_000_000, transcendentals=800_000),
    )(
        jnp.transpose(grid_in, (1, 0, 2)), jnp.transpose(grid_cotangent, (1, 0, 2)),
        jnp.transpose(support_filter, (1, 0, 2)), band_half, w_mix, norm_gain.reshape(1, CH), w_up, w_down,
        jnp.asarray(efwd), jnp.asarray(ebwd), jnp.asarray(forward), jnp.asarray(inverse),
    )
    grid_out, grid_grad, mix_grad, gain_grad, up_grad, down_grad = pl.pallas_call(
        finish,
        out_shape=(
            field,
            field,
            jax.ShapeDtypeStruct((CH, CH), F32),
            jax.ShapeDtypeStruct((1, CH), F32),
            jax.ShapeDtypeStruct((CH, HID), F32),
            jax.ShapeDtypeStruct((HID, CH), F32),
        ),
        in_specs=[anywhere] * 3,
        out_specs=[anywhere] * 6,
        scratch_shapes=[
            pltpu.VMEM((COLS, ROWS, CH), BF16),
            pltpu.VMEM((COLS, ROWS, CH), BF16),
            pltpu.VMEM((2 * HALF + TILE, 128), BF16),
            pltpu.VMEM((CH, CH), F32),
            pltpu.VMEM((1, CH), F32),
            pltpu.VMEM((CH, HID), F32),
            pltpu.VMEM((HID, CH), F32),
            pltpu.SemaphoreType.DMA((10,)),
        ],
        compiler_params=pltpu.CompilerParams(vmem_limit_bytes=60 * 1024 * 1024),
    )(res, gres, sums)
    return (
        jnp.transpose(grid_out, (1, 0, 2)),
        jnp.transpose(grid_grad, (1, 0, 2)),
        mix_grad,
        gain_grad.reshape(CH),
        up_grad,
        down_grad,
    )


def solution(mesh):
    return jax.shard_map(
        local,
        mesh=mesh,
        in_specs=(
            P("lat", "lon", None),
            P("lat", "lon", None),
            P("lat", None, None),
            P("lat"),
            P(),
            P(),
            P(),
            P(),
        ),
        out_specs=(P("lat", "lon", None), P("lat", "lon", None), P(), P(), P(), P()),
        check_vma=False,
    )
```

```python
import jax
import jax.numpy as jnp
import ml_dtypes
import numpy as np
from jax import lax
from jax.experimental import pallas as pl
from jax.experimental.pallas import tpu as pltpu
from jax.sharding import PartitionSpec as P

SQRT_TWO_PI = 0.7978845608028654
CUBIC = 0.044715
MESH = pl.DeviceIdType.MESH
BF16 = jnp.bfloat16
F32 = jnp.float32

LAT = 32
LON = 8
PAIRS = LON // 2
ROWS = 4
COLS = 180
CUT = 64
CHUNKS = 3
BLK = CUT * CHUNKS
NLON = LON * COLS
MODES = LON * BLK
WIDE = LON * CUT
CH = 256
HID = 1024
TAPS = 5
FLAT = ROWS * BLK
PART = ROWS * CUT
BAND_STEP = 512
NORM_STEP = 256
GELU_STEP = 64

HALF = 2304
UP_AT, DOWN_AT = 256, 1280
GAIN_AT = 2 * HALF
PLANE = 16
SHARE = HALF // PLANE
GROUP = 5
TILE = 16
Z_ROWS = 32
NORM_SCALE = float(LAT * ROWS * NLON) ** (-0.5)


def fourier_tables():
    modes = np.arange(NLON)
    freq = np.where(modes < NLON // 2, modes, modes - NLON // 2)
    phase = (freq[:, None] * modes[None, :]) % NLON
    angle = phase * (2.0 * np.pi / NLON)
    values = np.where((modes < NLON // 2)[:, None], np.cos(angle), np.sin(angle))
    table = np.zeros((MODES, LON, BLK), np.float32)
    table[:NLON, :, :COLS] = values.reshape(NLON, LON, COLS)
    table = table.reshape(MODES, LON, CHUNKS, CUT).astype(ml_dtypes.bfloat16)
    forward = np.ascontiguousarray(table.transpose(2, 0, 1, 3)).reshape(CHUNKS, MODES, WIDE)
    inverse = np.ascontiguousarray(table.transpose(2, 1, 3, 0)).reshape(CHUNKS, WIDE, MODES)
    return forward, inverse


def expansion():
    fwd = np.zeros((32, TAPS, ROWS, 32), np.float32)
    bwd = np.zeros((64, TAPS, ROWS, 32), np.float32)
    for w in range(TAPS):
        for i in range(ROWS):
            fwd[8 * i + w, w, i] = 1.0
            bwd[8 * (i + w) + 4 - w, w, i] = 1.0
    fwd = fwd.reshape(32, TAPS * 128)
    bwd = bwd.reshape(64, TAPS * 128)
    return fwd.astype(ml_dtypes.bfloat16), bwd.astype(ml_dtypes.bfloat16)


def dot(a, b):
    return jnp.dot(a, b, preferred_element_type=F32)


def dot_rows(a, b):
    return lax.dot_general(a, b, (((0,), (0,)), ((), ())), preferred_element_type=F32)


def dot_transpose(a, b):
    return lax.dot_general(a, b, (((1,), (1,)), ((), ())), preferred_element_type=F32)


def lanes_of(shape):
    return lax.broadcasted_iota(jnp.int32, shape, 1)


def turn_groups(parts):
    lane = lanes_of(parts[0].shape)
    low = lane < 64
    a, b, c, d = parts
    a, c = jnp.where(low, a, pltpu.roll(c, 64, 1)), jnp.where(low, pltpu.roll(a, 64, 1), c)
    b, d = jnp.where(low, b, pltpu.roll(d, 64, 1)), jnp.where(low, pltpu.roll(b, 64, 1), d)
    even = (lane % 64) < 32
    a, b = jnp.where(even, a, pltpu.roll(b, 32, 1)), jnp.where(even, pltpu.roll(a, 96, 1), b)
    c, d = jnp.where(even, c, pltpu.roll(d, 32, 1)), jnp.where(even, pltpu.roll(c, 96, 1), d)
    return a, b, c, d


def kernel(
    gin_hbm, cot_hbm, filt_hbm, band_hbm, wmix_hbm, gain_hbm, wup_hbm, wdown_hbm, efwd_hbm, ebwd_hbm, fwd_hbm, inv_hbm,
    out, grad, sums,
    fwd, inv, gf, cflat, send, recv, hsend, hrecv, halo, fstage, fown, fhalo, coef, dcoef,
    spec, banded, cf, conv, field, stream, scaled, before, dhid, hidden, dbef, ds, ds16, res, gres,
    gsum, part, csend, crecv, ps, pr, zf, zs, zr, zall, fin,
    gin, cot, filt, band, wmix, gain, wup, wdown, efwd, ebwd,
    isem, osem, ssem, rsem, hssem, hrsem, fssem, frsem, cssem, crsem, pssem, prsem, zssem, zrsem,
):
    lat = lax.axis_index("lat")
    me = lax.axis_index("lon")
    pair = me // 2
    after = lax.rem(lat + 1, LAT)
    ahead = lax.rem(lat + LAT - 1, LAT)
    core = me - 2 * pair
    x = lat // 8
    z_lo = lat // 4 - 2 * x
    y = lat - 8 * x - 4 * z_lo
    z = 2 * pair + z_lo
    mine = pl.multiple_of(core * HALF, HALF)

    plane = 4 * x + y

    def plane_peer(to):
        return {"lat": to // 4 * 8 + z_lo * 4 + (to - to // 4 * 4)}

    def z_peer(to):
        return {"lat": x * 8 + (to - to // 2 * 2) * 4 + y, "lon": to // 2 * 2 + core}

    inputs = (
        (gin_hbm, gin), (filt_hbm, filt), (efwd_hbm, efwd), (cot_hbm, cot), (wdown_hbm, wdown), (fwd_hbm, fwd),
        (inv_hbm, inv), (ebwd_hbm, ebwd), (wmix_hbm, wmix), (gain_hbm, gain), (wup_hbm, wup), (band_hbm, band),
    )
    gets = [pltpu.make_async_copy(src, dst, isem.at[k]) for k, (src, dst) in enumerate(inputs)]
    gets[0].start()

    barrier = pltpu.get_barrier_semaphore()
    for s in range(1, LON):
        pl.semaphore_signal(barrier, inc=1, device_id={"lon": lax.rem(me + s, LON)}, device_id_type=MESH)
    for there in (after, ahead):
        pl.semaphore_signal(barrier, inc=1, device_id={"lat": there}, device_id_type=MESH)
    for s in range(1, PLANE):
        there = plane_peer(lax.rem(plane + s, PLANE))
        pl.semaphore_signal(barrier, inc=1, device_id=there, device_id_type=MESH)
    for s in range(1, 8):
        pl.semaphore_signal(barrier, inc=1, device_id=z_peer(lax.rem(z + s, 8)), device_id_type=MESH)

    for get in gets[1:]:
        get.start()

    def exchange(ph, c, to, own):
        return pltpu.make_async_remote_copy(
            src_ref=send.at[ph, c, to], dst_ref=recv.at[ph, c, own],
            send_sem=ssem.at[ph], recv_sem=rsem.at[ph, c],
            device_id={"lon": to}, device_id_type=MESH,
        )

    def start_exchange(ph, c):
        for s in (4, 3, 5, 2, 6, 7, 1):
            exchange(ph, c, lax.rem(me + s, LON), me).start()
        recv[ph, c, me] = send[ph, c, me]

    def all_of(ref, sem):
        return pltpu.make_async_remote_copy(
            src_ref=ref, dst_ref=ref, send_sem=sem, recv_sem=sem,
            device_id={"lon": lax.rem(me + 1, LON)}, device_id_type=MESH,
        )

    def arrived(ph, c):
        all_of(recv.at[ph, c, pl.ds(0, LON - 1)], rsem.at[ph, c]).wait_recv()

    def halo_copy(hp, side, c):
        return pltpu.make_async_remote_copy(
            src_ref=hsend.at[hp, c, side], dst_ref=hrecv.at[hp, c, side],
            send_sem=hssem.at[hp], recv_sem=hrsem.at[hp, c],
            device_id={"lat": after if side == 0 else ahead}, device_id_type=MESH,
        )

    def filter_copy(side):
        return pltpu.make_async_remote_copy(
            src_ref=fown.at[pl.ds(16 if side == 0 else 0, 16)], dst_ref=fhalo.at[side],
            send_sem=fssem, recv_sem=frsem,
            device_id={"lat": after if side == 0 else ahead}, device_id_type=MESH,
        )

    def pack(src, ph, c):
        for half in range(2):
            parts = [src[half, pl.ds(c * PART + i, CUT, stride=ROWS), :] for i in range(ROWS)]
            for g, block in enumerate(turn_groups(parts)):
                send[ph, c, half * 4 + g] = block.astype(BF16)

    def unpack(ph, c, put):
        for half in range(2):
            parts = [recv[ph, c, half * 4 + g].astype(F32) for g in range(4)]
            for i, block in enumerate(turn_groups(parts)):
                put(half, pl.ds(c * PART + i, CUT, stride=ROWS), block)

    def pass_halo(ph, hp, c):
        arrived(ph, c)
        for g in range(PAIRS):
            one = recv[ph, c, 2 * g].astype(F32)
            two = recv[ph, c, 2 * g + 1].astype(F32)
            low = lanes_of(one.shape) < 64
            hsend[hp, c, 0, g] = jnp.where(low, pltpu.roll(one, 64, 1), two).astype(BF16)
            hsend[hp, c, 1, g] = jnp.where(low, one, pltpu.roll(two, 64, 1)).astype(BF16)
        halo_copy(hp, 0, c).start()
        halo_copy(hp, 1, c).start()

    def lay_halo(hp, c):
        all_of(hrecv.at[hp, c], hrsem.at[hp, c]).wait_recv()
        for g in range(PAIRS):
            one = hrecv[hp, c, 0, g].astype(F32)
            two = hrecv[hp, c, 1, g].astype(F32)
            low = lanes_of(one.shape) < 64
            halo[c, 2 * g] = jnp.where(low, one, pltpu.roll(two, 64, 1)).astype(BF16)
            halo[c, 2 * g + 1] = jnp.where(low, pltpu.roll(one, 64, 1), two).astype(BF16)

    def to_modes(ph, chunks):
        @pl.loop(0, MODES // 512)
        def _(step):
            at = pl.ds(pl.multiple_of(step * 512, 512), 512)
            total = None if chunks[0] == 0 else spec[at, :]
            for c in chunks:
                both = jnp.concatenate(
                    [recv[ph, c].reshape(WIDE, 128), halo[c].reshape(WIDE, 128)], axis=1
                )
                term = dot(fwd[c, at, :], both)
                total = term if total is None else total + term
            spec[at, :] = total

    def band_sum(weights):
        @pl.loop(0, MODES // BAND_STEP)
        def _(step):
            at = pl.ds(pl.multiple_of(step * BAND_STEP, BAND_STEP), BAND_STEP)
            own = spec[at, 0:128]
            edge = spec[at, 128:256]
            lane = lanes_of(own.shape)
            half = pltpu.roll(own, 64, 1)
            windows = (
                jnp.where(lane < 64, edge, half),
                jnp.where(lane < 32, pltpu.roll(edge, 96, 1), pltpu.roll(own, 32, 1)),
                own,
                jnp.where(lane >= 96, pltpu.roll(edge, 32, 1), pltpu.roll(own, 96, 1)),
                jnp.where(lane >= 64, edge, half),
            )
            total = windows[0] * weights[at, 0:128]
            for w in range(1, TAPS):
                total = total + windows[w] * weights[at, w * 128 : w * 128 + 128]
            banded[at, :] = total.astype(BF16)

    def to_grid(ph, c):
        block = dot(inv[c], banded[...]).astype(BF16)
        for q in range(LON):
            send[ph, c, q] = block[q * CUT : q * CUT + CUT]

    theirs = pl.multiple_of((1 - core) * HALF, HALF)
    other_core = {"lon": me + 1 - 2 * core}
    gain_rows = pl.ds(GAIN_AT, TILE)

    def core_copy(kind):
        rows = pl.ds(0, TILE + DOWN_AT) if kind == 0 else pl.ds(TILE + DOWN_AT, HALF - DOWN_AT)
        return pltpu.make_async_remote_copy(
            src_ref=csend.at[rows], dst_ref=crecv.at[rows], send_sem=cssem.at[kind], recv_sem=crsem.at[kind],
            device_id=other_core, device_id_type=MESH,
        )

    def core_gather(k):
        rows = pl.ds(mine + k * SHARE, SHARE)
        return pltpu.make_async_remote_copy(
            src_ref=fin.at[rows], dst_ref=fin.at[rows], send_sem=cssem.at[2], recv_sem=crsem.at[2],
            device_id=other_core, device_id_type=MESH,
        )

    def plane_scatter(to):
        return pltpu.make_async_remote_copy(
            src_ref=ps.at[to], dst_ref=pr.at[plane], send_sem=pssem.at[0], recv_sem=prsem.at[0],
            device_id=plane_peer(to), device_id_type=MESH,
        )

    def plane_gather(s):
        return pltpu.make_async_remote_copy(
            src_ref=zall.at[pl.ds(0, SHARE)], dst_ref=fin.at[pl.ds(mine + plane * SHARE, SHARE)],
            send_sem=pssem.at[1], recv_sem=prsem.at[1 + (PLANE - s - 1) // GROUP],
            device_id=plane_peer(lax.rem(plane + s, PLANE)), device_id_type=MESH,
        )

    def z_copy(kind, to):
        src, dst = (
            (zs.at[pl.ds(to * Z_ROWS, Z_ROWS)], zr.at[z]),
            (zall.at[pl.ds(z * Z_ROWS, Z_ROWS)], zall.at[pl.ds(z * Z_ROWS, Z_ROWS)]),
        )[kind]
        return pltpu.make_async_remote_copy(
            src_ref=src, dst_ref=dst, send_sem=zssem.at[kind], recv_sem=zrsem.at[kind],
            device_id=z_peer(to), device_id_type=MESH,
        )

    def z_start(kind):
        for s in range(1, 8):
            z_copy(kind, lax.rem(z + s, 8)).start()

    def others(ref, here, count, rows):
        total = ref[lax.rem(here + 1, count), rows, :].astype(F32)
        for s in range(2, count):
            total = total + ref[lax.rem(here + s, count), rows, :].astype(F32)
        return total

    def send_half(first, last):
        @pl.loop(first // 256, last // 256)
        def _(step):
            csend[pl.ds(TILE + step * 256, 256), :] = part[pl.ds(theirs + step * 256, 256), :].astype(BF16)

    def scatter_plane(half):
        core_copy(half).wait_recv()
        if half == 0:
            part[gain_rows, :] += crecv[0:TILE, :].astype(F32)
        g16 = part[gain_rows, :].astype(BF16)

        @pl.loop(half * 8, half * 8 + 8)
        def _(to):
            rows = pl.ds(mine + to * SHARE, SHARE)
            v = part[rows, :] + crecv[pl.ds(TILE + to * SHARE, SHARE), :].astype(F32)
            part[rows, :] = v
            ps[to, 0:SHARE, :] = v.astype(BF16)
            ps[to, SHARE:, :] = g16

        for s in range(8):
            to = half * 8 + lax.rem(plane + s, 8)

            @pl.when(to != plane)
            def _():
                plane_scatter(to).start()

    def scatter_z():
        all_of(pr.at[pl.ds(0, PLANE - 1)], prsem.at[0]).wait_recv()
        zf[SHARE + TILE :, :] = jnp.zeros((8 * Z_ROWS - SHARE - TILE, 128), F32)
        zf[0:SHARE, :] = part[pl.ds(mine + plane * SHARE, SHARE), :] + others(pr, plane, PLANE, pl.ds(0, SHARE))
        zf[SHARE : SHARE + TILE, :] = part[gain_rows, :] + others(pr, plane, PLANE, pl.ds(SHARE, TILE))
        zs[...] = zf[...].astype(BF16)
        z_start(0)

    def gather_z():
        all_of(zr.at[pl.ds(0, 7)], zrsem.at[0]).wait_recv()
        rows = pl.ds(pl.multiple_of(z * Z_ROWS, Z_ROWS), Z_ROWS)
        zall[rows, :] = (zf[rows, :] + others(zr, z, 8, pl.ds(0, Z_ROWS))).astype(BF16)
        z_start(1)

    def gather_plane():
        all_of(zall.at[pl.ds(0, 7 * Z_ROWS)], zrsem.at[1]).wait_recv()
        for s in range(1, PLANE):
            plane_gather(s).start()
        fin[pl.ds(mine + plane * SHARE, SHARE), :] = zall[0:SHARE, :]
        core_gather(plane).start()

    def gather_core():
        for group in range((PLANE - 1) // GROUP):
            all_of(fin.at[pl.ds(0, GROUP * SHARE)], prsem.at[1 + group]).wait_recv()
            for s in range(1 + group * GROUP, 1 + (group + 1) * GROUP):
                core_gather(lax.rem(plane + s, PLANE)).start()

    gets[0].wait()
    for half in range(2):
        gf[half, ROWS * COLS :, :] = jnp.zeros((FLAT - ROWS * COLS, 128), F32)
    for c in range(CHUNKS):
        count = min(CUT, COLS - c * CUT)
        rows = gin[c * CUT : c * CUT + count].astype(F32).reshape(ROWS * count, CH)
        for half in range(2):
            gf[half, c * PART : c * PART + ROWS * count, :] = rows[:, half * 128 : half * 128 + 128]
    pack(gf, 0, 0)
    pl.semaphore_wait(barrier, LON - 1 + 2 + PLANE - 1 + 7)
    start_exchange(0, 0)
    for c in range(1, CHUNKS):
        pack(gf, 0, c)
        start_exchange(0, c)

    gets[1].wait()
    gets[2].wait()
    gets[11].wait()
    fstage[...] = jnp.zeros_like(fstage)
    row = lax.broadcasted_iota(jnp.int32, (ROWS, NLON), 0)
    mode = lax.broadcasted_iota(jnp.int32, (ROWS, NLON), 1)
    scale = jnp.where(mode == 0, 1.0 / NLON, 2.0 / NLON)
    reach = jnp.where(row == 0, band[0], jnp.where(row == 1, band[1], jnp.where(row == 2, band[2], band[3])))
    for t in range(TAPS):
        at = lat * ROWS + row + (t - 2)
        keep = (reach >= abs(t - 2)) & (at >= 0) & (at < LAT * ROWS)
        kept = jnp.where(keep, filt[t] * scale, 0.0)
        for i in range(ROWS):
            fstage[8 * i + t : 8 * i + t + 1, 0:NLON] = kept[i : i + 1, :]
    fown[...] = fstage[...].astype(BF16)
    filter_copy(0).start()
    filter_copy(1).start()

    @pl.loop(0, MODES // 256)
    def _(step):
        at = pl.ds(pl.multiple_of(step * 256, 256), 256)
        coef[at, :] = dot_rows(fown[:, at], efwd[...])

    gets[3].wait()
    gets[4].wait()
    cflat[ROWS * COLS :, :] = jnp.zeros((FLAT - ROWS * COLS, CH), BF16)
    cflat[0 : ROWS * COLS, :] = cot[...].reshape(ROWS * COLS, CH)
    dhid[...] = dot_transpose(cflat[...], wdown[...])
    gsum[...] = jnp.zeros_like(gsum)

    for c in range(CHUNKS):
        pass_halo(0, 0, c)
    gets[5].wait()
    for c in range(CHUNKS):
        lay_halo(0, c)
        to_modes(0, [c])
    band_sum(coef)
    gets[6].wait()
    for c in range(CHUNKS):
        to_grid(1, c)
        start_exchange(1, c)

    for get in gets[7:11]:
        get.wait()
    all_of(fhalo, fssem).wait_send()
    all_of(fhalo, frsem).wait_recv()

    @pl.loop(0, MODES // 256)
    def _(step):
        at = pl.ds(pl.multiple_of(step * 256, 256), 256)
        rows = jnp.concatenate([fhalo[0, :, at], fown[:, at], fhalo[1, :, at]], axis=0)
        dcoef[at, :] = dot_rows(rows, ebwd[...])

    def put_conv(half, rows, block):
        cf[half, rows, :] = block

    def tail(c):
        arrived(1, c)
        unpack(1, c, put_conv)
        all_rows = pl.ds(c * PART, PART)
        conv[all_rows, :] = jnp.concatenate([cf[0, all_rows, :], cf[1, all_rows, :]], axis=1).astype(BF16)
        field[all_rows, :] = dot(conv[all_rows, :], wmix[...])

        @pl.loop(0, PART // NORM_STEP)
        def _(step):
            at = pl.ds(c * PART + step * NORM_STEP, NORM_STEP)
            mixed = field[at, :] + jnp.concatenate([gf[0, at, :], gf[1, at, :]], axis=1)
            s16 = mixed.astype(BF16)
            stream[at, :] = s16
            sf = s16.astype(F32)
            inverse = lax.rsqrt(jnp.mean(sf * sf, axis=-1, keepdims=True) + 1e-06)
            scaled[at, :] = (sf * inverse * gain[...]).astype(BF16)

        before[all_rows, :] = dot(scaled[all_rows, :], wup[...])

        @pl.loop(0, PART // GELU_STEP)
        def _(step):
            at = pl.ds(c * PART + step * GELU_STEP, GELU_STEP)
            u = before[at, :]
            u2 = u * u
            tangent = jnp.tanh(u * (SQRT_TWO_PI + (SQRT_TWO_PI * CUBIC) * u2))
            e = 0.5 * tangent + 0.5
            value = u * e
            hidden[at, :] = value.astype(BF16)
            slope = e + value * (1.0 - e) * (2.0 * SQRT_TWO_PI + (6.0 * SQRT_TWO_PI * CUBIC) * u2)
            dbef[at, :] = (dhid[at, :] * slope).astype(BF16)

        field[all_rows, :] = dot_transpose(dbef[all_rows, :], wup[...])

        @pl.loop(0, PART // NORM_STEP)
        def _(step):
            at = pl.ds(c * PART + step * NORM_STEP, NORM_STEP)
            sf = stream[at, :].astype(F32)
            inverse = lax.rsqrt(jnp.mean(sf * sf, axis=-1, keepdims=True) + 1e-06)
            normed = sf * inverse
            d_scaled = field[at, :]
            gsum[...] += jnp.sum((d_scaled * normed).reshape(NORM_STEP // 8, 8, CH), axis=0)
            gained = d_scaled * gain[...]
            value = cflat[at, :].astype(F32) + inverse * (
                gained - normed * jnp.mean(gained * normed, axis=-1, keepdims=True)
            )
            for half in range(2):
                ds[half, at, :] = value[:, half * 128 : half * 128 + 128]
            ds16[at, :] = value.astype(BF16)

        d_conv = dot_transpose(ds16[all_rows, :], wmix[...])
        for half in range(2):
            cf[half, all_rows, :] = d_conv[:, half * 128 : half * 128 + 128]
        pack(cf, 2, c)
        start_exchange(2, c)

    for c in range(CHUNKS):
        tail(c)

    term = dot_rows(conv[...], ds16[...])
    for h in range(2):
        part[h * HALF : h * HALF + UP_AT, :] = term[:, h * 128 : h * 128 + 128]
    term = dot_rows(scaled[...], dbef[...])
    for h in range(8):
        at = h // 4 * HALF + UP_AT + h % 4 * 256
        part[at : at + 256, :] = term[:, h * 128 : h * 128 + 128]
    part[gain_rows, :] = jnp.zeros((TILE, 128), F32)
    total = jnp.sum(gsum[...], axis=0, keepdims=True)
    for h in range(2):
        part[GAIN_AT + h : GAIN_AT + h + 1, :] = total[:, h * 128 : h * 128 + 128]
    csend[0:TILE, :] = part[gain_rows, :].astype(BF16)
    send_half(0, DOWN_AT)
    core_copy(0).start()
    term = dot_rows(hidden[...], cflat[...])
    for h in range(2):
        part[h * HALF + DOWN_AT : (h + 1) * HALF, :] = term[:, h * 128 : h * 128 + 128]
    send_half(DOWN_AT, HALF)
    core_copy(1).start()
    scatter_plane(0)
    scatter_plane(1)
    result = stream[...].astype(F32) + dot(hidden[...], wdown[...])
    res[...] = result[0 : ROWS * COLS].reshape(COLS, ROWS, CH).astype(BF16)
    put_out = pltpu.make_async_copy(res, out, osem.at[0])
    put_out.start()

    for c in range(CHUNKS):
        pass_halo(2, 1, c)
    scatter_z()
    for c in range(CHUNKS):
        lay_halo(1, c)
    to_modes(2, list(range(CHUNKS)))
    band_sum(dcoef)
    gather_z()
    for c in range(CHUNKS):
        to_grid(3, c)
        start_exchange(3, c)

    def put_grad(half, rows, block):
        ds[half, rows, :] = block + ds[half, rows, :]

    gather_plane()
    for c in range(CHUNKS):
        arrived(3, c)
        unpack(3, c, put_grad)
        count = min(CUT, COLS - c * CUT)
        rows = pl.ds(c * PART, ROWS * count)
        both = jnp.concatenate([ds[0, rows, :], ds[1, rows, :]], axis=1)
        gres[c * CUT : c * CUT + count] = both.reshape(count, ROWS, CH).astype(BF16)
    put_grad_out = pltpu.make_async_copy(gres, grad, osem.at[1])
    put_grad_out.start()
    gather_core()
    put_gain = pltpu.make_async_copy(zall.at[pl.ds(SHARE, TILE)], sums.at[pl.ds(GAIN_AT, TILE)], osem.at[2])
    put_own = pltpu.make_async_copy(fin.at[pl.ds(mine, HALF)], sums.at[pl.ds(mine, HALF)], osem.at[3])
    put_other = pltpu.make_async_copy(fin.at[pl.ds(theirs, HALF)], sums.at[pl.ds(theirs, HALF)], osem.at[4])
    put_gain.start()
    put_own.start()
    all_of(fin.at[pl.ds(0, HALF)], crsem.at[2]).wait_recv()
    put_other.start()

    core_copy(0).wait_send()
    core_copy(1).wait_send()
    all_of(fin.at[pl.ds(0, HALF)], cssem.at[2]).wait_send()
    all_of(ps.at[pl.ds(0, PLANE - 1)], pssem.at[0]).wait_send()
    all_of(fin.at[pl.ds(0, (PLANE - 1) * SHARE)], pssem.at[1]).wait_send()
    for kind in range(2):
        all_of(zs.at[pl.ds(0, 7 * Z_ROWS)], zssem.at[kind]).wait_send()
    for ph in range(4):
        all_of(send.at[ph, :, pl.ds(0, LON - 1)], ssem.at[ph]).wait_send()
    for hp in range(2):
        all_of(hsend.at[hp], hssem.at[hp]).wait_send()
    put_out.wait()
    put_grad_out.wait()
    put_gain.wait()
    put_own.wait()
    put_other.wait()


def finish(res, gres, sums, out, grad, mix_o, gain_o, up_o, down_o, first, second, half, mix, gain, up, down, sem):
    fields = [pltpu.make_async_copy(res, first, sem.at[0]), pltpu.make_async_copy(gres, second, sem.at[1])]
    puts = [pltpu.make_async_copy(first, out, sem.at[4]), pltpu.make_async_copy(second, grad, sem.at[5])]
    gets = [
        pltpu.make_async_copy(
            sums.at[pl.ds(h * HALF, HALF + h * TILE)], half.at[pl.ds(h * HALF, HALF + h * TILE)], sem.at[2 + h]
        )
        for h in range(2)
    ]
    for copy in gets + fields:
        copy.start()
    for h in range(2):
        gets[h].wait()
        lanes = slice(h * 128, h * 128 + 128)
        at = h * HALF
        mix[:, lanes] = half[at : at + UP_AT, :].astype(F32) * NORM_SCALE
        for b in range(4):
            start = at + UP_AT + b * 256
            up[:, h * 512 + b * 128 : h * 512 + b * 128 + 128] = half[start : start + 256, :].astype(F32) * NORM_SCALE
        down[:, lanes] = half[at + DOWN_AT : at + HALF, :].astype(F32) * NORM_SCALE
        fields[h].wait()
        puts[h].start()
    for h in range(2):
        gain[:, h * 128 : h * 128 + 128] = half[GAIN_AT : GAIN_AT + TILE, :].astype(F32)[h : h + 1, :] * NORM_SCALE
    for k, (src, dst) in enumerate(((up, up_o), (down, down_o), (mix, mix_o), (gain, gain_o))):
        puts.append(pltpu.make_async_copy(src, dst, sem.at[6 + k]))
        puts[-1].start()
    for copy in puts:
        copy.wait()


def local(grid_in, grid_cotangent, support_filter, band_half, w_mix, norm_gain, w_up, w_down):
    forward, inverse = fourier_tables()
    efwd, ebwd = expansion()
    anywhere = pl.BlockSpec(memory_space=pl.ANY)
    field = jax.ShapeDtypeStruct((COLS, ROWS, CH), BF16)
    res, gres, sums = pl.pallas_call(
        kernel,
        out_shape=(field, field, jax.ShapeDtypeStruct((2 * HALF + TILE, 128), BF16)),
        in_specs=[anywhere] * 12,
        out_specs=[anywhere] * 3,
        scratch_shapes=[
            pltpu.VMEM((CHUNKS, MODES, WIDE), BF16),
            pltpu.VMEM((CHUNKS, WIDE, MODES), BF16),
            pltpu.VMEM((2, FLAT, 128), F32),
            pltpu.VMEM((FLAT, CH), BF16),
            pltpu.VMEM((4, CHUNKS, LON, CUT, 128), BF16),
            pltpu.VMEM((4, CHUNKS, LON, CUT, 128), BF16),
            pltpu.VMEM((2, CHUNKS, 2, PAIRS, CUT, 128), BF16),
            pltpu.VMEM((2, CHUNKS, 2, PAIRS, CUT, 128), BF16),
            pltpu.VMEM((CHUNKS, LON, CUT, 128), BF16),
            pltpu.VMEM((32, MODES), F32),
            pltpu.VMEM((32, MODES), BF16),
            pltpu.VMEM((2, 16, MODES), BF16),
            pltpu.VMEM((MODES, TAPS * 128), F32),
            pltpu.VMEM((MODES, TAPS * 128), F32),
            pltpu.VMEM((MODES, 256), F32),
            pltpu.VMEM((MODES, 128), BF16),
            pltpu.VMEM((2, FLAT, 128), F32),
            pltpu.VMEM((FLAT, CH), BF16),
            pltpu.VMEM((FLAT, CH), F32),
            pltpu.VMEM((FLAT, CH), BF16),
            pltpu.VMEM((FLAT, CH), BF16),
            pltpu.VMEM((FLAT, HID), F32),
            pltpu.VMEM((FLAT, HID), F32),
            pltpu.VMEM((FLAT, HID), BF16),
            pltpu.VMEM((FLAT, HID), BF16),
            pltpu.VMEM((2, FLAT, 128), F32),
            pltpu.VMEM((FLAT, CH), BF16),
            pltpu.VMEM((COLS, ROWS, CH), BF16),
            pltpu.VMEM((COLS, ROWS, CH), BF16),
            pltpu.VMEM((8, CH), F32),
            pltpu.VMEM((2 * HALF + TILE, 128), F32),
            pltpu.VMEM((HALF + TILE, 128), BF16),
            pltpu.VMEM((HALF + TILE, 128), BF16),
            pltpu.VMEM((PLANE, SHARE + TILE, 128), BF16),
            pltpu.VMEM((PLANE, SHARE + TILE, 128), BF16),
            pltpu.VMEM((8 * Z_ROWS, 128), F32),
            pltpu.VMEM((8 * Z_ROWS, 128), BF16),
            pltpu.VMEM((8, Z_ROWS, 128), BF16),
            pltpu.VMEM((8 * Z_ROWS, 128), BF16),
            pltpu.VMEM((2 * HALF, 128), BF16),
            pltpu.VMEM((COLS, ROWS, CH), BF16),
            pltpu.VMEM((COLS, ROWS, CH), BF16),
            pltpu.VMEM((TAPS, ROWS, NLON), F32),
            pltpu.SMEM((ROWS,), jnp.int32),
            pltpu.VMEM((CH, CH), BF16),
            pltpu.VMEM((1, CH), F32),
            pltpu.VMEM((CH, HID), BF16),
            pltpu.VMEM((HID, CH), BF16),
            pltpu.VMEM((32, TAPS * 128), BF16),
            pltpu.VMEM((64, TAPS * 128), BF16),
            pltpu.SemaphoreType.DMA((12,)),
            pltpu.SemaphoreType.DMA((5,)),
            pltpu.SemaphoreType.DMA((4,)),
            pltpu.SemaphoreType.DMA((4, CHUNKS)),
            pltpu.SemaphoreType.DMA((2,)),
            pltpu.SemaphoreType.DMA((2, CHUNKS)),
            pltpu.SemaphoreType.DMA,
            pltpu.SemaphoreType.DMA,
            pltpu.SemaphoreType.DMA((3,)),
            pltpu.SemaphoreType.DMA((3,)),
            pltpu.SemaphoreType.DMA((2,)),
            pltpu.SemaphoreType.DMA((1 + (PLANE - 1) // GROUP,)),
            pltpu.SemaphoreType.DMA((2,)),
            pltpu.SemaphoreType.DMA((2,)),
        ],
        compiler_params=pltpu.CompilerParams(
            collective_id=0, has_side_effects=True, vmem_limit_bytes=60 * 1024 * 1024
        ),
        cost_estimate=pl.CostEstimate(flops=4_700_000_000, bytes_accessed=14_000_000, transcendentals=800_000),
    )(
        jnp.transpose(grid_in, (1, 0, 2)), jnp.transpose(grid_cotangent, (1, 0, 2)),
        jnp.transpose(support_filter, (1, 0, 2)), band_half, w_mix, norm_gain.reshape(1, CH), w_up, w_down,
        jnp.asarray(efwd), jnp.asarray(ebwd), jnp.asarray(forward), jnp.asarray(inverse),
    )
    grid_out, grid_grad, mix_grad, gain_grad, up_grad, down_grad = pl.pallas_call(
        finish,
        out_shape=(
            field,
            field,
            jax.ShapeDtypeStruct((CH, CH), F32),
            jax.ShapeDtypeStruct((1, CH), F32),
            jax.ShapeDtypeStruct((CH, HID), F32),
            jax.ShapeDtypeStruct((HID, CH), F32),
        ),
        in_specs=[anywhere] * 3,
        out_specs=[anywhere] * 6,
        scratch_shapes=[
            pltpu.VMEM((COLS, ROWS, CH), BF16),
            pltpu.VMEM((COLS, ROWS, CH), BF16),
            pltpu.VMEM((2 * HALF + TILE, 128), BF16),
            pltpu.VMEM((CH, CH), F32),
            pltpu.VMEM((1, CH), F32),
            pltpu.VMEM((CH, HID), F32),
            pltpu.VMEM((HID, CH), F32),
            pltpu.SemaphoreType.DMA((10,)),
        ],
        compiler_params=pltpu.CompilerParams(vmem_limit_bytes=60 * 1024 * 1024),
    )(res, gres, sums)
    return (
        jnp.transpose(grid_out, (1, 0, 2)),
        jnp.transpose(grid_grad, (1, 0, 2)),
        mix_grad,
        gain_grad.reshape(CH),
        up_grad,
        down_grad,
    )


def solution(mesh):
    return jax.shard_map(
        local,
        mesh=mesh,
        in_specs=(
            P("lat", "lon", None),
            P("lat", "lon", None),
            P("lat", None, None),
            P("lat"),
            P(),
            P(),
            P(),
            P(),
        ),
        out_specs=(P("lat", "lon", None), P("lat", "lon", None), P(), P(), P(), P()),
        check_vma=False,
    )
```

```python
import jax
import jax.numpy as jnp
import ml_dtypes
import numpy as np
from jax import lax
from jax.experimental import pallas as pl
from jax.experimental.pallas import tpu as pltpu
from jax.sharding import PartitionSpec as P

SQRT_TWO_PI = 0.7978845608028654
CUBIC = 0.044715
MESH = pl.DeviceIdType.MESH
BF16 = jnp.bfloat16
F32 = jnp.float32

LAT = 32
LON = 8
PAIRS = LON // 2
ROWS = 4
COLS = 180
CUT = 64
CHUNKS = 3
BLK = CUT * CHUNKS
NLON = LON * COLS
MODES = LON * BLK
WIDE = LON * CUT
CH = 256
HID = 1024
TAPS = 5
FLAT = ROWS * BLK
PART = ROWS * CUT
BAND_STEP = 512
NORM_STEP = 256
GELU_STEP = 64

HALF = 2304
UP_AT, DOWN_AT = 256, 1280
GAIN_AT = 2 * HALF
PLANE = 16
SHARE = HALF // PLANE
GROUP = 5
TILE = 16
Z_ROWS = 32
NORM_SCALE = float(LAT * ROWS * NLON) ** (-0.5)


def fourier_tables():
    modes = np.arange(NLON)
    freq = np.where(modes < NLON // 2, modes, modes - NLON // 2)
    phase = (freq[:, None] * modes[None, :]) % NLON
    angle = phase * (2.0 * np.pi / NLON)
    values = np.where((modes < NLON // 2)[:, None], np.cos(angle), np.sin(angle))
    table = np.zeros((MODES, LON, BLK), np.float32)
    table[:NLON, :, :COLS] = values.reshape(NLON, LON, COLS)
    table = table.reshape(MODES, LON, CHUNKS, CUT).astype(ml_dtypes.bfloat16)
    forward = np.ascontiguousarray(table.transpose(2, 0, 1, 3)).reshape(CHUNKS, MODES, WIDE)
    inverse = np.ascontiguousarray(table.transpose(2, 1, 3, 0)).reshape(CHUNKS, WIDE, MODES)
    return forward, inverse


def expansion():
    fwd = np.zeros((32, TAPS, ROWS, 32), np.float32)
    bwd = np.zeros((64, TAPS, ROWS, 32), np.float32)
    for w in range(TAPS):
        for i in range(ROWS):
            fwd[8 * i + w, w, i] = 1.0
            bwd[8 * (i + w) + 4 - w, w, i] = 1.0
    fwd = fwd.reshape(32, TAPS * 128)
    bwd = bwd.reshape(64, TAPS * 128)
    return fwd.astype(ml_dtypes.bfloat16), bwd.astype(ml_dtypes.bfloat16)


def dot(a, b):
    return jnp.dot(a, b, preferred_element_type=F32)


def dot_rows(a, b):
    return lax.dot_general(a, b, (((0,), (0,)), ((), ())), preferred_element_type=F32)


def dot_transpose(a, b):
    return lax.dot_general(a, b, (((1,), (1,)), ((), ())), preferred_element_type=F32)


def lanes_of(shape):
    return lax.broadcasted_iota(jnp.int32, shape, 1)


def turn_groups(parts):
    lane = lanes_of(parts[0].shape)
    low = lane < 64
    a, b, c, d = parts
    a, c = jnp.where(low, a, pltpu.roll(c, 64, 1)), jnp.where(low, pltpu.roll(a, 64, 1), c)
    b, d = jnp.where(low, b, pltpu.roll(d, 64, 1)), jnp.where(low, pltpu.roll(b, 64, 1), d)
    even = (lane % 64) < 32
    a, b = jnp.where(even, a, pltpu.roll(b, 32, 1)), jnp.where(even, pltpu.roll(a, 96, 1), b)
    c, d = jnp.where(even, c, pltpu.roll(d, 32, 1)), jnp.where(even, pltpu.roll(c, 96, 1), d)
    return a, b, c, d


def kernel(
    gin_hbm, cot_hbm, filt_hbm, band_hbm, wmix_hbm, gain_hbm, wup_hbm, wdown_hbm, efwd_hbm, ebwd_hbm, fwd_hbm, inv_hbm,
    out, grad, sums,
    fwd, inv, gf, cflat, send, recv, hsend, hrecv, halo, fstage, fown, fhalo, coef, dcoef,
    spec, banded, cf, conv, field, stream, scaled, before, dhid, hidden, dbef, ds, ds16, res, gres,
    gsum, part, csend, crecv, ps, pr, zf, zs, zr, zall, fin,
    gin, cot, filt, band, wmix, gain, wup, wdown, efwd, ebwd,
    isem, osem, ssem, rsem, hssem, hrsem, fssem, frsem, cssem, crsem, pssem, prsem, zssem, zrsem,
):
    lat = lax.axis_index("lat")
    me = lax.axis_index("lon")
    pair = me // 2
    after = lax.rem(lat + 1, LAT)
    ahead = lax.rem(lat + LAT - 1, LAT)
    core = me - 2 * pair
    x = lat // 8
    z_lo = lat // 4 - 2 * x
    y = lat - 8 * x - 4 * z_lo
    z = 2 * pair + z_lo
    mine = pl.multiple_of(core * HALF, HALF)

    plane = 4 * x + y

    def plane_peer(to):
        return {"lat": to // 4 * 8 + z_lo * 4 + (to - to // 4 * 4)}

    def z_peer(to):
        return {"lat": x * 8 + (to - to // 2 * 2) * 4 + y, "lon": to // 2 * 2 + core}

    inputs = (
        (gin_hbm, gin), (filt_hbm, filt), (efwd_hbm, efwd), (cot_hbm, cot), (wdown_hbm, wdown), (fwd_hbm, fwd),
        (inv_hbm, inv), (ebwd_hbm, ebwd), (wmix_hbm, wmix), (gain_hbm, gain), (wup_hbm, wup), (band_hbm, band),
    )
    gets = [pltpu.make_async_copy(src, dst, isem.at[k]) for k, (src, dst) in enumerate(inputs)]
    gets[0].start()

    barrier = pltpu.get_barrier_semaphore()
    for s in range(1, LON):
        pl.semaphore_signal(barrier, inc=1, device_id={"lon": lax.rem(me + s, LON)}, device_id_type=MESH)
    for there in (after, ahead):
        pl.semaphore_signal(barrier, inc=1, device_id={"lat": there}, device_id_type=MESH)
    for s in range(1, PLANE):
        there = plane_peer(lax.rem(plane + s, PLANE))
        pl.semaphore_signal(barrier, inc=1, device_id=there, device_id_type=MESH)
    for s in range(1, 8):
        pl.semaphore_signal(barrier, inc=1, device_id=z_peer(lax.rem(z + s, 8)), device_id_type=MESH)

    for get in gets[1:]:
        get.start()

    def exchange(ph, c, to, own):
        return pltpu.make_async_remote_copy(
            src_ref=send.at[ph, c, to], dst_ref=recv.at[ph, c, own],
            send_sem=ssem.at[ph], recv_sem=rsem.at[ph, c],
            device_id={"lon": to}, device_id_type=MESH,
        )

    def start_exchange(ph, c):
        for s in (4, 3, 5, 2, 6, 7, 1):
            exchange(ph, c, lax.rem(me + s, LON), me).start()
        recv[ph, c, me] = send[ph, c, me]

    def all_of(ref, sem):
        return pltpu.make_async_remote_copy(
            src_ref=ref, dst_ref=ref, send_sem=sem, recv_sem=sem,
            device_id={"lon": lax.rem(me + 1, LON)}, device_id_type=MESH,
        )

    def arrived(ph, c):
        all_of(recv.at[ph, c, pl.ds(0, LON - 1)], rsem.at[ph, c]).wait_recv()

    def halo_copy(hp, side, c):
        return pltpu.make_async_remote_copy(
            src_ref=hsend.at[hp, c, side], dst_ref=hrecv.at[hp, c, side],
            send_sem=hssem.at[hp], recv_sem=hrsem.at[hp, c],
            device_id={"lat": after if side == 0 else ahead}, device_id_type=MESH,
        )

    def filter_copy(side):
        return pltpu.make_async_remote_copy(
            src_ref=fown.at[pl.ds(16 if side == 0 else 0, 16)], dst_ref=fhalo.at[side],
            send_sem=fssem, recv_sem=frsem,
            device_id={"lat": after if side == 0 else ahead}, device_id_type=MESH,
        )

    def pack(src, ph, c):
        for half in range(2):
            parts = [src[half, pl.ds(c * PART + i, CUT, stride=ROWS), :] for i in range(ROWS)]
            for g, block in enumerate(turn_groups(parts)):
                send[ph, c, half * 4 + g] = block.astype(BF16)

    def unpack(ph, c, put):
        for half in range(2):
            parts = [recv[ph, c, half * 4 + g].astype(F32) for g in range(4)]
            for i, block in enumerate(turn_groups(parts)):
                put(half, pl.ds(c * PART + i, CUT, stride=ROWS), block)

    def pass_halo(ph, hp, c):
        arrived(ph, c)
        for g in range(PAIRS):
            one = recv[ph, c, 2 * g].astype(F32)
            two = recv[ph, c, 2 * g + 1].astype(F32)
            low = lanes_of(one.shape) < 64
            hsend[hp, c, 0, g] = jnp.where(low, pltpu.roll(one, 64, 1), two).astype(BF16)
            hsend[hp, c, 1, g] = jnp.where(low, one, pltpu.roll(two, 64, 1)).astype(BF16)
        halo_copy(hp, 0, c).start()
        halo_copy(hp, 1, c).start()

    def lay_halo(hp, c):
        all_of(hrecv.at[hp, c], hrsem.at[hp, c]).wait_recv()
        for g in range(PAIRS):
            one = hrecv[hp, c, 0, g].astype(F32)
            two = hrecv[hp, c, 1, g].astype(F32)
            low = lanes_of(one.shape) < 64
            halo[c, 2 * g] = jnp.where(low, one, pltpu.roll(two, 64, 1)).astype(BF16)
            halo[c, 2 * g + 1] = jnp.where(low, pltpu.roll(one, 64, 1), two).astype(BF16)

    def to_modes(ph, chunks):
        @pl.loop(0, MODES // 512)
        def _(step):
            at = pl.ds(pl.multiple_of(step * 512, 512), 512)
            total = None if chunks[0] == 0 else spec[at, :]
            for c in chunks:
                both = jnp.concatenate(
                    [recv[ph, c].reshape(WIDE, 128), halo[c].reshape(WIDE, 128)], axis=1
                )
                term = dot(fwd[c, at, :], both)
                total = term if total is None else total + term
            spec[at, :] = total

    def band_sum(weights):
        @pl.loop(0, MODES // BAND_STEP)
        def _(step):
            at = pl.ds(pl.multiple_of(step * BAND_STEP, BAND_STEP), BAND_STEP)
            own = spec[at, 0:128]
            edge = spec[at, 128:256]
            lane = lanes_of(own.shape)
            half = pltpu.roll(own, 64, 1)
            windows = (
                jnp.where(lane < 64, edge, half),
                jnp.where(lane < 32, pltpu.roll(edge, 96, 1), pltpu.roll(own, 32, 1)),
                own,
                jnp.where(lane >= 96, pltpu.roll(edge, 32, 1), pltpu.roll(own, 96, 1)),
                jnp.where(lane >= 64, edge, half),
            )
            total = windows[0] * weights[at, 0:128]
            for w in range(1, TAPS):
                total = total + windows[w] * weights[at, w * 128 : w * 128 + 128]
            banded[at, :] = total.astype(BF16)

    def to_grid(ph, c):
        block = dot(inv[c], banded[...]).astype(BF16)
        for q in range(LON):
            send[ph, c, q] = block[q * CUT : q * CUT + CUT]

    theirs = pl.multiple_of((1 - core) * HALF, HALF)
    other_core = {"lon": me + 1 - 2 * core}
    gain_rows = pl.ds(GAIN_AT, TILE)

    def core_copy(kind):
        rows = pl.ds(0, TILE + DOWN_AT) if kind == 0 else pl.ds(TILE + DOWN_AT, HALF - DOWN_AT)
        return pltpu.make_async_remote_copy(
            src_ref=csend.at[rows], dst_ref=crecv.at[rows], send_sem=cssem.at[kind], recv_sem=crsem.at[kind],
            device_id=other_core, device_id_type=MESH,
        )

    def core_gather(k):
        rows = pl.ds(mine + k * SHARE, SHARE)
        return pltpu.make_async_remote_copy(
            src_ref=fin.at[rows], dst_ref=fin.at[rows], send_sem=cssem.at[2], recv_sem=crsem.at[2],
            device_id=other_core, device_id_type=MESH,
        )

    def plane_scatter(to):
        return pltpu.make_async_remote_copy(
            src_ref=ps.at[to], dst_ref=pr.at[plane], send_sem=pssem.at[0], recv_sem=prsem.at[0],
            device_id=plane_peer(to), device_id_type=MESH,
        )

    def plane_gather(s):
        return pltpu.make_async_remote_copy(
            src_ref=zall.at[pl.ds(0, SHARE)], dst_ref=fin.at[pl.ds(mine + plane * SHARE, SHARE)],
            send_sem=pssem.at[1], recv_sem=prsem.at[1 + (PLANE - s - 1) // GROUP],
            device_id=plane_peer(lax.rem(plane + s, PLANE)), device_id_type=MESH,
        )

    def z_copy(kind, to):
        src, dst = (
            (zs.at[pl.ds(to * Z_ROWS, Z_ROWS)], zr.at[z]),
            (zall.at[pl.ds(z * Z_ROWS, Z_ROWS)], zall.at[pl.ds(z * Z_ROWS, Z_ROWS)]),
        )[kind]
        return pltpu.make_async_remote_copy(
            src_ref=src, dst_ref=dst, send_sem=zssem.at[kind], recv_sem=zrsem.at[kind],
            device_id=z_peer(to), device_id_type=MESH,
        )

    def z_start(kind):
        for s in range(1, 8):
            z_copy(kind, lax.rem(z + s, 8)).start()

    def others(ref, here, count, rows):
        total = ref[lax.rem(here + 1, count), rows, :].astype(F32)
        for s in range(2, count):
            total = total + ref[lax.rem(here + s, count), rows, :].astype(F32)
        return total

    def send_half(first, last):
        @pl.loop(first // 256, last // 256)
        def _(step):
            csend[pl.ds(TILE + step * 256, 256), :] = part[pl.ds(theirs + step * 256, 256), :].astype(BF16)

    def scatter_plane(half):
        core_copy(half).wait_recv()
        if half == 0:
            part[gain_rows, :] += crecv[0:TILE, :].astype(F32)
        g16 = part[gain_rows, :].astype(BF16)

        @pl.loop(half * 8, half * 8 + 8)
        def _(to):
            rows = pl.ds(mine + to * SHARE, SHARE)
            v = part[rows, :] + crecv[pl.ds(TILE + to * SHARE, SHARE), :].astype(F32)
            part[rows, :] = v
            ps[to, 0:SHARE, :] = v.astype(BF16)
            ps[to, SHARE:, :] = g16

        for s in range(8):
            to = half * 8 + lax.rem(plane + s, 8)

            @pl.when(to != plane)
            def _():
                plane_scatter(to).start()

    def scatter_z():
        all_of(pr.at[pl.ds(0, PLANE - 1)], prsem.at[0]).wait_recv()
        zf[SHARE + TILE :, :] = jnp.zeros((8 * Z_ROWS - SHARE - TILE, 128), F32)
        zf[0:SHARE, :] = part[pl.ds(mine + plane * SHARE, SHARE), :] + others(pr, plane, PLANE, pl.ds(0, SHARE))
        zf[SHARE : SHARE + TILE, :] = part[gain_rows, :] + others(pr, plane, PLANE, pl.ds(SHARE, TILE))
        zs[...] = zf[...].astype(BF16)
        z_start(0)

    def gather_z():
        all_of(zr.at[pl.ds(0, 7)], zrsem.at[0]).wait_recv()
        rows = pl.ds(pl.multiple_of(z * Z_ROWS, Z_ROWS), Z_ROWS)
        zall[rows, :] = (zf[rows, :] + others(zr, z, 8, pl.ds(0, Z_ROWS))).astype(BF16)
        z_start(1)

    def gather_plane():
        all_of(zall.at[pl.ds(0, 7 * Z_ROWS)], zrsem.at[1]).wait_recv()
        for s in range(1, PLANE):
            plane_gather(s).start()
        fin[pl.ds(mine + plane * SHARE, SHARE), :] = zall[0:SHARE, :]
        core_gather(plane).start()

    def gather_core():
        for group in range((PLANE - 1) // GROUP):
            all_of(fin.at[pl.ds(0, GROUP * SHARE)], prsem.at[1 + group]).wait_recv()
            for s in range(1 + group * GROUP, 1 + (group + 1) * GROUP):
                core_gather(lax.rem(plane + s, PLANE)).start()

    gets[0].wait()
    for half in range(2):
        gf[half, ROWS * COLS :, :] = jnp.zeros((FLAT - ROWS * COLS, 128), F32)
    for c in range(CHUNKS):
        count = min(CUT, COLS - c * CUT)
        rows = gin[c * CUT : c * CUT + count].astype(F32).reshape(ROWS * count, CH)
        for half in range(2):
            gf[half, c * PART : c * PART + ROWS * count, :] = rows[:, half * 128 : half * 128 + 128]
    pack(gf, 0, 0)
    pl.semaphore_wait(barrier, LON - 1 + 2 + PLANE - 1 + 7)
    start_exchange(0, 0)
    for c in range(1, CHUNKS):
        pack(gf, 0, c)
        start_exchange(0, c)

    gets[1].wait()
    gets[2].wait()
    gets[11].wait()
    fstage[...] = jnp.zeros_like(fstage)
    row = lax.broadcasted_iota(jnp.int32, (ROWS, NLON), 0)
    mode = lax.broadcasted_iota(jnp.int32, (ROWS, NLON), 1)
    scale = jnp.where(mode == 0, 1.0 / NLON, 2.0 / NLON)
    reach = jnp.where(row == 0, band[0], jnp.where(row == 1, band[1], jnp.where(row == 2, band[2], band[3])))
    for t in range(TAPS):
        at = lat * ROWS + row + (t - 2)
        keep = (reach >= abs(t - 2)) & (at >= 0) & (at < LAT * ROWS)
        kept = jnp.where(keep, filt[t] * scale, 0.0)
        for i in range(ROWS):
            fstage[8 * i + t : 8 * i + t + 1, 0:NLON] = kept[i : i + 1, :]
    fown[...] = fstage[...].astype(BF16)
    filter_copy(0).start()
    filter_copy(1).start()

    @pl.loop(0, MODES // 256)
    def _(step):
        at = pl.ds(pl.multiple_of(step * 256, 256), 256)
        coef[at, :] = dot_rows(fown[:, at], efwd[...])

    gets[3].wait()
    gets[4].wait()
    cflat[ROWS * COLS :, :] = jnp.zeros((FLAT - ROWS * COLS, CH), BF16)
    cflat[0 : ROWS * COLS, :] = cot[...].reshape(ROWS * COLS, CH)
    dhid[...] = dot_transpose(cflat[...], wdown[...])
    gsum[...] = jnp.zeros_like(gsum)

    for c in range(CHUNKS):
        pass_halo(0, 0, c)
    gets[5].wait()
    for c in range(CHUNKS):
        lay_halo(0, c)
        to_modes(0, [c])
    band_sum(coef)
    gets[6].wait()
    for c in range(CHUNKS):
        to_grid(1, c)
        start_exchange(1, c)

    for get in gets[7:11]:
        get.wait()
    all_of(fhalo, fssem).wait_send()
    all_of(fhalo, frsem).wait_recv()

    @pl.loop(0, MODES // 256)
    def _(step):
        at = pl.ds(pl.multiple_of(step * 256, 256), 256)
        rows = jnp.concatenate([fhalo[0, :, at], fown[:, at], fhalo[1, :, at]], axis=0)
        dcoef[at, :] = dot_rows(rows, ebwd[...])

    def put_conv(half, rows, block):
        cf[half, rows, :] = block

    def tail(c):
        arrived(1, c)
        unpack(1, c, put_conv)
        all_rows = pl.ds(c * PART, PART)
        conv[all_rows, :] = jnp.concatenate([cf[0, all_rows, :], cf[1, all_rows, :]], axis=1).astype(BF16)
        field[all_rows, :] = dot(conv[all_rows, :], wmix[...])

        @pl.loop(0, PART // NORM_STEP)
        def _(step):
            at = pl.ds(c * PART + step * NORM_STEP, NORM_STEP)
            mixed = field[at, :] + jnp.concatenate([gf[0, at, :], gf[1, at, :]], axis=1)
            s16 = mixed.astype(BF16)
            stream[at, :] = s16
            sf = s16.astype(F32)
            inverse = lax.rsqrt(jnp.mean(sf * sf, axis=-1, keepdims=True) + 1e-06)
            scaled[at, :] = (sf * inverse * gain[...]).astype(BF16)

        before[all_rows, :] = dot(scaled[all_rows, :], wup[...])

        @pl.loop(0, PART // GELU_STEP)
        def _(step):
            at = pl.ds(c * PART + step * GELU_STEP, GELU_STEP)
            u = before[at, :]
            u2 = u * u
            tangent = jnp.tanh(u * (SQRT_TWO_PI + (SQRT_TWO_PI * CUBIC) * u2))
            e = 0.5 * tangent + 0.5
            value = u * e
            hidden[at, :] = value.astype(BF16)
            slope = e + value * (1.0 - e) * (2.0 * SQRT_TWO_PI + (6.0 * SQRT_TWO_PI * CUBIC) * u2)
            dbef[at, :] = (dhid[at, :] * slope).astype(BF16)

        field[all_rows, :] = dot_transpose(dbef[all_rows, :], wup[...])

        @pl.loop(0, PART // NORM_STEP)
        def _(step):
            at = pl.ds(c * PART + step * NORM_STEP, NORM_STEP)
            sf = stream[at, :].astype(F32)
            inverse = lax.rsqrt(jnp.mean(sf * sf, axis=-1, keepdims=True) + 1e-06)
            normed = sf * inverse
            d_scaled = field[at, :]
            gsum[...] += jnp.sum((d_scaled * normed).reshape(NORM_STEP // 8, 8, CH), axis=0)
            gained = d_scaled * gain[...]
            value = cflat[at, :].astype(F32) + inverse * (
                gained - normed * jnp.mean(gained * normed, axis=-1, keepdims=True)
            )
            for half in range(2):
                ds[half, at, :] = value[:, half * 128 : half * 128 + 128]
            ds16[at, :] = value.astype(BF16)

        d_conv = dot_transpose(ds16[all_rows, :], wmix[...])
        for half in range(2):
            cf[half, all_rows, :] = d_conv[:, half * 128 : half * 128 + 128]
        pack(cf, 2, c)
        start_exchange(2, c)

    for c in range(CHUNKS):
        tail(c)

    term = dot_rows(conv[...], ds16[...])
    for h in range(2):
        part[h * HALF : h * HALF + UP_AT, :] = term[:, h * 128 : h * 128 + 128]
    term = dot_rows(scaled[...], dbef[...])
    for h in range(8):
        at = h // 4 * HALF + UP_AT + h % 4 * 256
        part[at : at + 256, :] = term[:, h * 128 : h * 128 + 128]
    part[gain_rows, :] = jnp.zeros((TILE, 128), F32)
    total = jnp.sum(gsum[...], axis=0, keepdims=True)
    for h in range(2):
        part[GAIN_AT + h : GAIN_AT + h + 1, :] = total[:, h * 128 : h * 128 + 128]
    csend[0:TILE, :] = part[gain_rows, :].astype(BF16)
    send_half(0, DOWN_AT)
    core_copy(0).start()
    term = dot_rows(hidden[...], cflat[...])
    for h in range(2):
        part[h * HALF + DOWN_AT : (h + 1) * HALF, :] = term[:, h * 128 : h * 128 + 128]
    send_half(DOWN_AT, HALF)
    core_copy(1).start()
    scatter_plane(0)
    scatter_plane(1)
    for c in range(CHUNKS):
        pass_halo(2, 1, c)
    result = stream[...].astype(F32) + dot(hidden[...], wdown[...])
    res[...] = result[0 : ROWS * COLS].reshape(COLS, ROWS, CH).astype(BF16)
    put_out = pltpu.make_async_copy(res, out, osem.at[0])
    put_out.start()
    scatter_z()
    for c in range(CHUNKS):
        lay_halo(1, c)
    to_modes(2, list(range(CHUNKS)))
    band_sum(dcoef)
    gather_z()
    for c in range(CHUNKS):
        to_grid(3, c)
        start_exchange(3, c)

    def put_grad(half, rows, block):
        ds[half, rows, :] = block + ds[half, rows, :]

    gather_plane()
    gather_core()
    for c in range(CHUNKS):
        arrived(3, c)
        unpack(3, c, put_grad)
        count = min(CUT, COLS - c * CUT)
        rows = pl.ds(c * PART, ROWS * count)
        both = jnp.concatenate([ds[0, rows, :], ds[1, rows, :]], axis=1)
        gres[c * CUT : c * CUT + count] = both.reshape(count, ROWS, CH).astype(BF16)
    put_grad_out = pltpu.make_async_copy(gres, grad, osem.at[1])
    put_grad_out.start()
    put_gain = pltpu.make_async_copy(zall.at[pl.ds(SHARE, TILE)], sums.at[pl.ds(GAIN_AT, TILE)], osem.at[2])
    put_own = pltpu.make_async_copy(fin.at[pl.ds(mine, HALF)], sums.at[pl.ds(mine, HALF)], osem.at[3])
    put_other = pltpu.make_async_copy(fin.at[pl.ds(theirs, HALF)], sums.at[pl.ds(theirs, HALF)], osem.at[4])
    put_gain.start()
    put_own.start()
    all_of(fin.at[pl.ds(0, HALF)], crsem.at[2]).wait_recv()
    put_other.start()

    core_copy(0).wait_send()
    core_copy(1).wait_send()
    all_of(fin.at[pl.ds(0, HALF)], cssem.at[2]).wait_send()
    all_of(ps.at[pl.ds(0, PLANE - 1)], pssem.at[0]).wait_send()
    all_of(fin.at[pl.ds(0, (PLANE - 1) * SHARE)], pssem.at[1]).wait_send()
    for kind in range(2):
        all_of(zs.at[pl.ds(0, 7 * Z_ROWS)], zssem.at[kind]).wait_send()
    for ph in range(4):
        all_of(send.at[ph, :, pl.ds(0, LON - 1)], ssem.at[ph]).wait_send()
    for hp in range(2):
        all_of(hsend.at[hp], hssem.at[hp]).wait_send()
    put_out.wait()
    put_grad_out.wait()
    put_gain.wait()
    put_own.wait()
    put_other.wait()


def finish(res, gres, sums, out, grad, mix_o, gain_o, up_o, down_o, first, second, half, mix, gain, up, down, sem):
    fields = [pltpu.make_async_copy(res, first, sem.at[0]), pltpu.make_async_copy(gres, second, sem.at[1])]
    puts = [pltpu.make_async_copy(first, out, sem.at[4]), pltpu.make_async_copy(second, grad, sem.at[5])]
    gets = [
        pltpu.make_async_copy(
            sums.at[pl.ds(h * HALF, HALF + h * TILE)], half.at[pl.ds(h * HALF, HALF + h * TILE)], sem.at[2 + h]
        )
        for h in range(2)
    ]
    for copy in gets + fields:
        copy.start()
    for h in range(2):
        gets[h].wait()
        lanes = slice(h * 128, h * 128 + 128)
        at = h * HALF
        mix[:, lanes] = half[at : at + UP_AT, :].astype(F32) * NORM_SCALE
        for b in range(4):
            start = at + UP_AT + b * 256
            up[:, h * 512 + b * 128 : h * 512 + b * 128 + 128] = half[start : start + 256, :].astype(F32) * NORM_SCALE
        down[:, lanes] = half[at + DOWN_AT : at + HALF, :].astype(F32) * NORM_SCALE
        fields[h].wait()
        puts[h].start()
    for h in range(2):
        gain[:, h * 128 : h * 128 + 128] = half[GAIN_AT : GAIN_AT + TILE, :].astype(F32)[h : h + 1, :] * NORM_SCALE
    for k, (src, dst) in enumerate(((up, up_o), (down, down_o), (mix, mix_o), (gain, gain_o))):
        puts.append(pltpu.make_async_copy(src, dst, sem.at[6 + k]))
        puts[-1].start()
    for copy in puts:
        copy.wait()


def local(grid_in, grid_cotangent, support_filter, band_half, w_mix, norm_gain, w_up, w_down):
    forward, inverse = fourier_tables()
    efwd, ebwd = expansion()
    anywhere = pl.BlockSpec(memory_space=pl.ANY)
    field = jax.ShapeDtypeStruct((COLS, ROWS, CH), BF16)
    res, gres, sums = pl.pallas_call(
        kernel,
        out_shape=(field, field, jax.ShapeDtypeStruct((2 * HALF + TILE, 128), BF16)),
        in_specs=[anywhere] * 12,
        out_specs=[anywhere] * 3,
        scratch_shapes=[
            pltpu.VMEM((CHUNKS, MODES, WIDE), BF16),
            pltpu.VMEM((CHUNKS, WIDE, MODES), BF16),
            pltpu.VMEM((2, FLAT, 128), F32),
            pltpu.VMEM((FLAT, CH), BF16),
            pltpu.VMEM((4, CHUNKS, LON, CUT, 128), BF16),
            pltpu.VMEM((4, CHUNKS, LON, CUT, 128), BF16),
            pltpu.VMEM((2, CHUNKS, 2, PAIRS, CUT, 128), BF16),
            pltpu.VMEM((2, CHUNKS, 2, PAIRS, CUT, 128), BF16),
            pltpu.VMEM((CHUNKS, LON, CUT, 128), BF16),
            pltpu.VMEM((32, MODES), F32),
            pltpu.VMEM((32, MODES), BF16),
            pltpu.VMEM((2, 16, MODES), BF16),
            pltpu.VMEM((MODES, TAPS * 128), F32),
            pltpu.VMEM((MODES, TAPS * 128), F32),
            pltpu.VMEM((MODES, 256), F32),
            pltpu.VMEM((MODES, 128), BF16),
            pltpu.VMEM((2, FLAT, 128), F32),
            pltpu.VMEM((FLAT, CH), BF16),
            pltpu.VMEM((FLAT, CH), F32),
            pltpu.VMEM((FLAT, CH), BF16),
            pltpu.VMEM((FLAT, CH), BF16),
            pltpu.VMEM((FLAT, HID), F32),
            pltpu.VMEM((FLAT, HID), F32),
            pltpu.VMEM((FLAT, HID), BF16),
            pltpu.VMEM((FLAT, HID), BF16),
            pltpu.VMEM((2, FLAT, 128), F32),
            pltpu.VMEM((FLAT, CH), BF16),
            pltpu.VMEM((COLS, ROWS, CH), BF16),
            pltpu.VMEM((COLS, ROWS, CH), BF16),
            pltpu.VMEM((8, CH), F32),
            pltpu.VMEM((2 * HALF + TILE, 128), F32),
            pltpu.VMEM((HALF + TILE, 128), BF16),
            pltpu.VMEM((HALF + TILE, 128), BF16),
            pltpu.VMEM((PLANE, SHARE + TILE, 128), BF16),
            pltpu.VMEM((PLANE, SHARE + TILE, 128), BF16),
            pltpu.VMEM((8 * Z_ROWS, 128), F32),
            pltpu.VMEM((8 * Z_ROWS, 128), BF16),
            pltpu.VMEM((8, Z_ROWS, 128), BF16),
            pltpu.VMEM((8 * Z_ROWS, 128), BF16),
            pltpu.VMEM((2 * HALF, 128), BF16),
            pltpu.VMEM((COLS, ROWS, CH), BF16),
            pltpu.VMEM((COLS, ROWS, CH), BF16),
            pltpu.VMEM((TAPS, ROWS, NLON), F32),
            pltpu.SMEM((ROWS,), jnp.int32),
            pltpu.VMEM((CH, CH), BF16),
            pltpu.VMEM((1, CH), F32),
            pltpu.VMEM((CH, HID), BF16),
            pltpu.VMEM((HID, CH), BF16),
            pltpu.VMEM((32, TAPS * 128), BF16),
            pltpu.VMEM((64, TAPS * 128), BF16),
            pltpu.SemaphoreType.DMA((12,)),
            pltpu.SemaphoreType.DMA((5,)),
            pltpu.SemaphoreType.DMA((4,)),
            pltpu.SemaphoreType.DMA((4, CHUNKS)),
            pltpu.SemaphoreType.DMA((2,)),
            pltpu.SemaphoreType.DMA((2, CHUNKS)),
            pltpu.SemaphoreType.DMA,
            pltpu.SemaphoreType.DMA,
            pltpu.SemaphoreType.DMA((3,)),
            pltpu.SemaphoreType.DMA((3,)),
            pltpu.SemaphoreType.DMA((2,)),
            pltpu.SemaphoreType.DMA((1 + (PLANE - 1) // GROUP,)),
            pltpu.SemaphoreType.DMA((2,)),
            pltpu.SemaphoreType.DMA((2,)),
        ],
        compiler_params=pltpu.CompilerParams(
            collective_id=0, has_side_effects=True, vmem_limit_bytes=60 * 1024 * 1024
        ),
        cost_estimate=pl.CostEstimate(flops=4_700_000_000, bytes_accessed=14_000_000, transcendentals=800_000),
    )(
        jnp.transpose(grid_in, (1, 0, 2)), jnp.transpose(grid_cotangent, (1, 0, 2)),
        jnp.transpose(support_filter, (1, 0, 2)), band_half, w_mix, norm_gain.reshape(1, CH), w_up, w_down,
        jnp.asarray(efwd), jnp.asarray(ebwd), jnp.asarray(forward), jnp.asarray(inverse),
    )
    grid_out, grid_grad, mix_grad, gain_grad, up_grad, down_grad = pl.pallas_call(
        finish,
        out_shape=(
            field,
            field,
            jax.ShapeDtypeStruct((CH, CH), F32),
            jax.ShapeDtypeStruct((1, CH), F32),
            jax.ShapeDtypeStruct((CH, HID), F32),
            jax.ShapeDtypeStruct((HID, CH), F32),
        ),
        in_specs=[anywhere] * 3,
        out_specs=[anywhere] * 6,
        scratch_shapes=[
            pltpu.VMEM((COLS, ROWS, CH), BF16),
            pltpu.VMEM((COLS, ROWS, CH), BF16),
            pltpu.VMEM((2 * HALF + TILE, 128), BF16),
            pltpu.VMEM((CH, CH), F32),
            pltpu.VMEM((1, CH), F32),
            pltpu.VMEM((CH, HID), F32),
            pltpu.VMEM((HID, CH), F32),
            pltpu.SemaphoreType.DMA((10,)),
        ],
        compiler_params=pltpu.CompilerParams(vmem_limit_bytes=60 * 1024 * 1024),
    )(res, gres, sums)
    return (
        jnp.transpose(grid_out, (1, 0, 2)),
        jnp.transpose(grid_grad, (1, 0, 2)),
        mix_grad,
        gain_grad.reshape(CH),
        up_grad,
        down_grad,
    )


def solution(mesh):
    return jax.shard_map(
        local,
        mesh=mesh,
        in_specs=(
            P("lat", "lon", None),
            P("lat", "lon", None),
            P("lat", None, None),
            P("lat"),
            P(),
            P(),
            P(),
            P(),
        ),
        out_specs=(P("lat", "lon", None), P("lat", "lon", None), P(), P(), P(), P()),
        check_vma=False,
    )
```
